32 devices in a mesh: grp: 2 (over y), chol: 8 (over z, core), walk: 2 (over x), orb: 1.
Axes of the slice: x: 2, y: 2, z: 4, core: 2. Of those that a mesh axis runs over, the one named last changes fastest.
Arguments:
- green_blocks: bfloat16 [16, 1024, 256], P(('grp', 'walk'), 'chol', 'orb'), parts along dimension 0, may hold values from -6 to 6
- half_chol: bfloat16 [32, 1024, 256], P(('grp', 'chol'), None, 'orb'), parts along dimension 0, may hold values from -0.125 to 0.125
- full_chol: bfloat16 [32, 1024, 1024], P(('grp', 'chol'), 'orb'), parts along dimension 0, may hold values from -0.125 to 0.125
- meanfield: float32 [32], P(('grp', 'chol')), parts along dimension 0, may hold values from -60 to 60
- noise_draws: float32 [16, 16], P(('grp', 'walk'), 'chol'), parts along dimension 0, may hold values from -6 to 6
- orbitals: float32 [1, 1024, 16, 256], P('orb', 'chol', ('grp', 'walk')), parts along dimension 2, may hold values from -6 to 6
Outputs:
- walkers_next: float32 [1, 1024, 16, 256], P('orb', 'chol', ('grp', 'walk')), parts along dimension 2
- bias_shift: float32 [16, 16], P(('grp', 'walk'), 'chol'), parts along dimension 0
The draws below stay inside these ranges and needn't reach their ends.
There are 2 independent parts, one for each index of `grp`. The reference program is written for one: setup_inputs(seed, part) draws one part's arguments, and reference() takes and returns one part's arrays. A program takes and returns all parts, laid end to end along the dimension named above; each array names one. Nothing has to cross between parts.
All inputs are finite; a program needn't handle non-finite values.
Results may differ from the reference program's by a relative error of at most 0.0015.
Values may be sent and summed in bfloat16 or wider, within the bound.
No kernel may reach another device: no remote copies, remote signals or barrier semaphores. Data moves between devices by JAX's collectives and lax.ppermute only.
A program may use at most 64 MiB of HBM per device.

```python
import jax
import jax.numpy as jnp
from jax import lax

NORB = 1024
NOCC = 256
CHOL_DEV = 2
NCHOL = 16
WALKERS = 8
ROW_HALF = 1024
N_CHOL = 8
N_ORB = 1


def shard_levels(rng, shape, cuts, least, high):
    level, own = 1.0, jax.random.fold_in(rng, 6)
    for dim, parts in cuts:
        draws = jnp.exp(jax.random.uniform(jax.random.fold_in(own, dim), (parts,), jnp.float32, least / len(cuts), high / len(cuts)))
        level = level * jnp.repeat(draws, shape[dim] // parts).reshape([-1 if axis == dim else 1 for axis in range(len(shape))])
    return level


def scatter_about(stream_key, dims, width, bound, shards=(), held_as=jnp.bfloat16):
    values = width * jax.random.normal(stream_key, dims, jnp.float32)
    if shards:
        values = values * shard_levels(stream_key, dims, shards, -0.22, 0.18)
    return jnp.clip(values, -bound, bound).astype(held_as)


def setup_inputs(seed: int = 0, part: int = 0) -> dict:
    keys = jax.random.split(jax.random.key(seed), 7)
    own_keys = jax.random.split(jax.random.fold_in(keys[6], part), 7)
    return {
        "green_blocks": scatter_about(own_keys[0], (WALKERS, NORB, NOCC), 1.0, 6.0, ((0, 2), (1, 8))),
        "half_chol": scatter_about(own_keys[1], (NCHOL, NORB, NOCC), (NORB * NOCC // 100) ** -0.5, 0.125, ((0, 8),)),
        "full_chol": scatter_about(own_keys[2], (NCHOL, NORB, NORB), (NORB * NCHOL // 9) ** -0.5, 0.125, ((0, 8),)),
        "meanfield": scatter_about(own_keys[3], (NCHOL,), 10.0, 60.0, ((0, 8),), jnp.float32),
        "noise_draws": scatter_about(own_keys[4], (WALKERS, NCHOL), 1.0, 6.0, ((0, 2), (1, 8)), jnp.float32),
        "orbitals": scatter_about(own_keys[5], (N_ORB, ROW_HALF, WALKERS, NOCC), 1.0, 6.0, ((1, 8), (2, 2)), jnp.float32),
    }


time_root = 0.1


def reference(green_blocks, half_chol, full_chol, meanfield, noise_draws, orbitals):
    force_bias = jnp.einsum('wki,cki->wc', green_blocks.astype(jnp.float32), half_chol.astype(jnp.float32))
    bias_shift = jnp.clip(time_root * (force_bias - meanfield[None, :]), -1.0, 1.0)
    shifted_field = noise_draws - bias_shift
    block_fields = jnp.transpose(shifted_field.reshape(WALKERS, N_CHOL, CHOL_DEV), (1, 0, 2))
    block_chols = full_chol.reshape(N_CHOL, CHOL_DEV, NORB, NORB)

    def propagate(vector):
        wide_vector = lax.optimization_barrier(vector).astype(jnp.float32)

        def add_block(running, inputs):
            block_field, block_chol = inputs
            operator_block = (time_root * jnp.einsum('wc,crk->wrk', block_field, block_chol.astype(jnp.float32))).astype(jnp.bfloat16)
            operator_wide = lax.optimization_barrier(operator_block).astype(jnp.float32)
            return running + jnp.einsum('wrk,kwn->rwn', operator_wide, wide_vector), None

        start_sum = jnp.zeros((NORB, WALKERS, NOCC), jnp.float32)
        summed, _ = lax.scan(add_block, start_sum, (block_fields, block_chols))
        return summed

    flat_orbitals = orbitals.reshape(NORB, WALKERS, NOCC)
    first_term = propagate(flat_orbitals.astype(jnp.bfloat16))
    second_term = propagate(first_term.astype(jnp.bfloat16))
    advanced = flat_orbitals + first_term + 0.5 * second_term
    return advanced.reshape(N_ORB, ROW_HALF, WALKERS, NOCC), bias_shift
```

```python
import jax
import jax.numpy as jnp
from jax import lax
from jax.sharding import PartitionSpec as P

time_root = 0.1


def general_device(green_blocks, half_chol, full_chol, meanfield, noise_draws, orbitals):
    walkers_here = green_blocks.shape[0]
    chol_here = half_chol.shape[0]
    half_rows = full_chol.shape[1]
    orbital_count = full_chol.shape[2]
    occupied = orbitals.shape[3]
    rows_here = orbitals.shape[1]
    partial_bias = jnp.einsum(
        "wki,cki->wc",
        lax.all_gather(green_blocks, "chol", axis=1, tiled=True),
        half_chol,
        preferred_element_type=jnp.float32,
    )
    force_bias = lax.psum(partial_bias, "orb")
    bias_shift = jnp.clip(time_root * (force_bias - meanfield[None, :]), -1.0, 1.0)
    shifted_field = noise_draws - bias_shift
    combined = jnp.zeros((walkers_here, half_rows, orbital_count), jnp.float32)
    for chol_index in range(chol_here):
        combined = combined + shifted_field[:, chol_index, None, None] * full_chol[chol_index][
            None
        ].astype(jnp.float32)
    operator_rows = (time_root * combined).astype(jnp.bfloat16)

    def apply_operator(vector):
        both_halves = lax.all_gather(vector, "orb", axis=0, tiled=True)
        running = jnp.zeros((walkers_here, half_rows, occupied), jnp.float32)
        shard_piece = lax.all_gather(both_halves, "chol", axis=1, tiled=True)
        row_count = shard_piece.shape[1]
        for half_index in range(shard_piece.shape[0]):
            col_block = lax.dynamic_slice_in_dim(
                operator_rows, half_index * half_rows, row_count, 2
            )
            running = running + lax.dot_general(
                col_block,
                shard_piece[half_index],
                (((2,), (0,)), ((0,), (1,))),
                preferred_element_type=jnp.float32,
            )
        summed = lax.psum(running, "chol")
        chol_slot = lax.axis_index("chol")
        owned_rows = lax.dynamic_slice_in_dim(summed, chol_slot * rows_here, rows_here, 1)
        return jnp.transpose(owned_rows, (1, 0, 2))[None]

    first_term = apply_operator(orbitals.astype(jnp.bfloat16))
    second_term = apply_operator(first_term.astype(jnp.bfloat16))
    walkers_next = orbitals + first_term + 0.5 * second_term
    return (walkers_next, bias_shift)


def row_device(chips):
    devices = 2 * chips

    def ring(value, step):
        pairs = [(i, (i + 2 * step) % devices) for i in range(devices)]
        return lax.ppermute(value, "chol", pairs)

    def core(value):
        return lax.ppermute(value, "chol", [(i, i ^ 1) for i in range(devices)])

    def across(value):
        return lax.ppermute(value, "walk", [(0, 1), (1, 0)])

    def gather_ring(value):
        half = value.shape[0] // 2
        below = ring(value, 1)
        above = ring(value, -1)
        far = jnp.concatenate([ring(below[:half], 1), ring(above[half:], -1)])
        return [value, above, far, below]

    def device(green_blocks, half_chol, full_chol, meanfield, noise_draws, orbitals):
        slot = lax.axis_index("chol")
        z, k = slot // 2, slot % 2
        x = lax.axis_index("walk")
        walkers, rows_here, occupied = green_blocks.shape
        order = full_chol.shape[2]
        half_rows = full_chol.shape[1]
        chip_rows = 2 * rows_here

        def gather_rows(value):
            mine = gather_ring(value)
            theirs = [core(block) for block in mine]
            blocks = []
            for a, b in zip(mine, theirs, strict=True):
                blocks.append(jnp.where(k == 0, a, b))
                blocks.append(jnp.where(k == 0, b, a))
            relative = jnp.stack(blocks, 1)
            relative = jnp.roll(relative, 2 * z, axis=1)
            return relative.reshape(walkers, half_rows, occupied)

        mine_here = lax.dynamic_index_in_dim(full_chol, x, 0, False)
        by_chip = mine_here.reshape(chips, 2, rows_here, order)

        def for_chip(step):
            return lax.dynamic_index_in_dim(by_chip, (z + step) % chips, 0, False)

        far = for_chip(2)
        far_low, far_high = ring(far[0], 1), ring(far[1], -1)
        below, above = ring(for_chip(1), 1), ring(for_chip(-1), -1)
        far_here = jnp.stack([ring(far_low, 1), ring(far_high, -1)])

        half_by = half_chol.reshape(-1, chips, 2, rows_here, occupied)
        half_mine = lax.dynamic_index_in_dim(half_by, k, 2, False)
        half_theirs = core(lax.dynamic_index_in_dim(half_by, 1 - k, 2, False))
        green_ring = gather_ring(green_blocks)
        green_here = jnp.roll(jnp.stack(green_ring, 1), z, axis=1)
        dims = "wzki,czki->wc"
        bias_mine = jnp.einsum(dims, green_here, half_mine, preferred_element_type=jnp.float32)
        bias_theirs = jnp.einsum(dims, green_here, half_theirs, preferred_element_type=jnp.float32)
        force_bias = bias_mine + core(bias_theirs)
        bias_shift = jnp.clip(time_root * (force_bias - meanfield[None, :]), -1.0, 1.0)
        shifted_field = noise_draws - bias_shift
        field_here = jnp.where(x == 0, shifted_field, shifted_field[:, ::-1])
        field_chip = jnp.stack([field_here, core(field_here)], 1)
        fields = [field_chip, ring(field_chip, -1), ring(field_chip, 2), ring(field_chip, 1)]

        def pick(pair):
            return jnp.where(k == 0, pair[0], pair[1]), jnp.where(k == 0, pair[1], pair[0])

        def spread(pair):
            mine, send = pick(pair)
            both = jnp.stack([mine, core(send)])
            return jnp.stack([both, across(both)], 1)

        full_by = full_chol.reshape(2, chips, 2, rows_here, order)
        own = lax.dynamic_index_in_dim(full_by, z, 1, False)
        own = jnp.where(x == 0, own, own[::-1])
        own_mine = jnp.where(k == 0, own[:, 0], own[:, 1])
        own_send = jnp.where(k == 0, own[:, 1], own[:, 0])
        own_rows = jnp.stack([own_mine, core(own_send)])
        chol_rows = [own_rows, spread(above), spread(far_here), spread(below)]

        summed = jnp.zeros((walkers, rows_here, order), jnp.float32)
        for field, chols in zip(fields, chol_rows, strict=True):
            for source in range(2):
                wide = chols[source].astype(jnp.float32)
                block = (
                    field[:, source, 0, None, None] * wide[0]
                    + field[:, source, 1, None, None] * wide[1]
                )
                summed = summed + (time_root * block).astype(jnp.bfloat16).astype(jnp.float32)
        high = summed.astype(jnp.bfloat16)
        low = (summed - high.astype(jnp.float32)).astype(jnp.bfloat16)

        def apply_operator(vector):
            dims = (((2,), (1,)), ((0,), (0,)))
            return lax.dot_general(
                high, vector, dims, preferred_element_type=jnp.float32
            ) + lax.dot_general(low, vector, dims, preferred_element_type=jnp.float32)

        start = jnp.transpose(orbitals[0], (1, 0, 2))
        first_term = apply_operator(gather_rows(start.astype(jnp.bfloat16)))
        second_term = apply_operator(gather_rows(first_term.astype(jnp.bfloat16)))
        walkers_next = start + first_term + 0.5 * second_term
        return (jnp.transpose(walkers_next, (1, 0, 2))[None], bias_shift)

    return device


def solution(mesh):
    placed = (
        P(("grp", "walk"), "chol", "orb"),
        P(("grp", "chol"), None, "orb"),
        P(("grp", "chol"), "orb", None),
        P(("grp", "chol")),
        P(("grp", "walk"), "chol"),
        P("orb", "chol", ("grp", "walk"), None),
    )
    sizes = mesh.shape
    if sizes["orb"] == 1 and sizes["walk"] == 2 and sizes["chol"] == 8:
        per_device = row_device(sizes["chol"] // 2)
    else:
        per_device = general_device
    return jax.shard_map(
        per_device,
        mesh=mesh,
        in_specs=placed,
        out_specs=(P("orb", "chol", ("grp", "walk"), None), P(("grp", "walk"), "chol")),
        check_vma=False,
    )
```

```python
import functools

import jax
import jax.numpy as jnp
from jax import lax
from jax.experimental import pallas as pl
from jax.experimental.pallas import tpu as pltpu
from jax.sharding import PartitionSpec as P

time_root = 0.1


def general_device(green_blocks, half_chol, full_chol, meanfield, noise_draws, orbitals):
    walkers_here = green_blocks.shape[0]
    chol_here = half_chol.shape[0]
    half_rows = full_chol.shape[1]
    orbital_count = full_chol.shape[2]
    occupied = orbitals.shape[3]
    rows_here = orbitals.shape[1]
    partial_bias = jnp.einsum(
        "wki,cki->wc",
        lax.all_gather(green_blocks, "chol", axis=1, tiled=True),
        half_chol,
        preferred_element_type=jnp.float32,
    )
    force_bias = lax.psum(partial_bias, "orb")
    bias_shift = jnp.clip(time_root * (force_bias - meanfield[None, :]), -1.0, 1.0)
    shifted_field = noise_draws - bias_shift
    combined = jnp.zeros((walkers_here, half_rows, orbital_count), jnp.float32)
    for chol_index in range(chol_here):
        combined = combined + shifted_field[:, chol_index, None, None] * full_chol[chol_index][
            None
        ].astype(jnp.float32)
    operator_rows = (time_root * combined).astype(jnp.bfloat16)

    def apply_operator(vector):
        both_halves = lax.all_gather(vector, "orb", axis=0, tiled=True)
        running = jnp.zeros((walkers_here, half_rows, occupied), jnp.float32)
        shard_piece = lax.all_gather(both_halves, "chol", axis=1, tiled=True)
        row_count = shard_piece.shape[1]
        for half_index in range(shard_piece.shape[0]):
            col_block = lax.dynamic_slice_in_dim(
                operator_rows, half_index * half_rows, row_count, 2
            )
            running = running + lax.dot_general(
                col_block,
                shard_piece[half_index],
                (((2,), (0,)), ((0,), (1,))),
                preferred_element_type=jnp.float32,
            )
        summed = lax.psum(running, "chol")
        chol_slot = lax.axis_index("chol")
        owned_rows = lax.dynamic_slice_in_dim(summed, chol_slot * rows_here, rows_here, 1)
        return jnp.transpose(owned_rows, (1, 0, 2))[None]

    first_term = apply_operator(orbitals.astype(jnp.bfloat16))
    second_term = apply_operator(first_term.astype(jnp.bfloat16))
    walkers_next = orbitals + first_term + 0.5 * second_term
    return (walkers_next, bias_shift)


vmem_spec = pl.BlockSpec(memory_space=pltpu.VMEM)
any_spec = pl.BlockSpec(memory_space=pl.ANY)
wide = jnp.float32
narrow = jnp.bfloat16


def after(value, *others):
    return lax.optimization_barrier((value, *others))[0]


def place(chips):
    slot = lax.axis_index("chol")
    return slot // 2, slot % 2, lax.axis_index("walk")


def cut_kernel(chips, rows, wanted, full_ref, *refs):
    z, k, x = place(chips)
    outs, sem = refs[:-1], refs[-1]
    copies = []
    for index, (step, crossed, both) in enumerate(wanted):
        core = 1 - k if crossed else k
        start = pl.multiple_of((2 * lax.rem(z + step + chips, chips) + core) * rows, rows)
        picked = pl.ds(start, rows)
        source = full_ref.at[:, picked, :] if both else full_ref.at[x, picked, :]
        copies.append(pltpu.make_async_copy(source, outs[index], sem.at[index]))
        copies[-1].start()
    for copy in copies:
        copy.wait()


def cut(chips, rows, full_chol, wanted):
    order = full_chol.shape[2]
    shapes = [
        jax.ShapeDtypeStruct((2, rows, order) if both else (rows, order), narrow)
        for _, _, both in wanted
    ]
    return pl.pallas_call(
        functools.partial(cut_kernel, chips, rows, wanted),
        out_shape=shapes,
        in_specs=[any_spec],
        out_specs=[vmem_spec] * len(wanted),
        scratch_shapes=[pltpu.SemaphoreType.DMA((len(wanted),))],
        name="cut_rows",
    )(full_chol)


def start_kernel(orbitals_ref, out_ref):
    for walker in range(out_ref.shape[0]):
        out_ref[walker] = orbitals_ref[0, :, walker, :].astype(narrow)


def walker_major(orbitals):
    _, rows, walkers, occupied = orbitals.shape
    return pl.pallas_call(
        start_kernel,
        out_shape=jax.ShapeDtypeStruct((walkers, rows, occupied), narrow),
        in_specs=[vmem_spec],
        out_specs=vmem_spec,
        name="walker_major",
    )(orbitals)


def bias_kernel(chips, here_ref, above_ref, low_ref, high_ref, below_ref, mine_ref, theirs_ref, out_ref):
    z, k, _ = place(chips)
    walkers, rows, occupied = here_ref.shape
    vectors = mine_ref.shape[0]
    half = walkers // 2
    step_rows = 16
    totals = [jnp.zeros((8, 128), wide) for _ in range(2 * vectors * walkers)]
    for step, green in ((0, here_ref), (1, above_ref), (2, None), (-1, below_ref)):
        base = (2 * lax.rem(z + step + chips, chips) + k) * rows

        def add(index, totals, base=base, green=green):
            here = pl.multiple_of(index * step_rows, step_rows)
            there = pl.multiple_of(base + index * step_rows, step_rows)
            picked = pl.ds(here, step_rows)
            if green is None:
                greens = [low_ref[w, picked, :] for w in range(half)]
                greens += [high_ref[w, picked, :] for w in range(half)]
            else:
                greens = [green[w, picked, :] for w in range(walkers)]
            greens = [g.astype(wide) for g in greens]
            totals = list(totals)
            for c in range(2 * vectors):
                chol_ref = mine_ref if c < vectors else theirs_ref
                chol = chol_ref[c % vectors, pl.ds(there, step_rows), :].astype(wide)
                for w in range(walkers):
                    product = greens[w] * chol
                    tiles = [
                        product[r : r + 8, n : n + 128]
                        for r in range(0, step_rows, 8)
                        for n in range(0, occupied, 128)
                    ]
                    totals[c * walkers + w] = totals[c * walkers + w] + sum(tiles[1:], tiles[0])
            return tuple(totals)

        totals = lax.fori_loop(0, rows // step_rows, add, tuple(totals))
    for index, total in enumerate(totals):
        value = jnp.sum(jnp.sum(total, axis=0, keepdims=True), axis=1, keepdims=True)
        out_ref[pl.ds(index, 1), :] = jnp.broadcast_to(value, (1, 128))


def chip_bias(chips, here, above, low, high, below, mine, theirs):
    entries = 2 * mine.shape[0] * here.shape[0]
    return pl.pallas_call(
        functools.partial(bias_kernel, chips),
        out_shape=jax.ShapeDtypeStruct((entries, 128), wide),
        in_specs=[vmem_spec] * 7,
        out_specs=vmem_spec,
        name="chip_bias",
    )(here, above, low, high, below, mine, theirs)


def field_kernel(mine_ref, theirs_ref, noise_ref, noise_there_ref, shift_ref, field_ref):
    half = mine_ref.shape[0] // 2
    low, high = pl.ds(0, half), pl.ds(half, half)
    for rows, other, consts in ((low, high, noise_ref), (high, low, noise_there_ref)):
        force = mine_ref[rows, :] + theirs_ref[other, :]
        shift = jnp.clip(time_root * (force - consts[high, :]), -1.0, 1.0)
        field_ref[rows, :] = consts[low, :] - shift
        if rows is low:
            shift_ref[...] = shift


def chip_field(mine, theirs, noise, noise_there):
    entries = mine.shape[0]
    return pl.pallas_call(
        field_kernel,
        out_shape=[
            jax.ShapeDtypeStruct((entries // 2, 128), wide),
            jax.ShapeDtypeStruct((entries, 128), wide),
        ],
        in_specs=[vmem_spec] * 4,
        out_specs=[vmem_spec] * 2,
        name="chip_field",
    )(mine, theirs, noise, noise_there)


def build_operator(x, walkers, sources, summed_ref, summed_in_ref, emit):
    rows, order = summed_ref.shape[1:]
    high, across = 16, 256
    columns = order // across

    def tile(index, carry):
        row = pl.multiple_of((index // columns) * high, high)
        column = pl.multiple_of((index % columns) * across, across)
        picked = (pl.ds(row, high), pl.ds(column, across))
        sums = [None if summed_in_ref is None else summed_in_ref[(w, *picked)] for w in range(walkers)]
        for field_ref, first, near, other in sources:
            one = near(picked).astype(wide)
            two = other(picked).astype(wide)
            for w in range(walkers):
                scale_one = field_ref[pl.ds(first + x * walkers + w, 1), :]
                scale_two = field_ref[pl.ds(first + (1 - x) * walkers + w, 1), :]
                scale_one = jnp.concatenate([scale_one] * (across // 128), 1)
                scale_two = jnp.concatenate([scale_two] * (across // 128), 1)
                block = time_root * (scale_one * one + scale_two * two)
                block = block.astype(narrow).astype(wide)
                sums[w] = block if sums[w] is None else sums[w] + block
        for w in range(walkers):
            emit(w, picked, sums[w])
        return carry

    lax.fori_loop(0, (rows // high) * columns, tile, 0)


def plain(ref):
    return lambda picked: ref[picked]


def pair_sources(x, field_ref, walkers, near_own, other_own, near_theirs, other_theirs):
    vectors = 2
    return [
        (field_ref, 0, plain(near_own), plain(other_own)),
        (field_ref, vectors * walkers, plain(near_theirs), plain(other_theirs)),
    ]


def early_kernel(chips, walkers, field_here, field_above, field_below, own_ref, own_theirs, *refs):
    _, _, x = place(chips)
    blocks, summed_ref = refs[:-1], refs[-1]
    sources = []
    for ref, first in ((own_ref, 0), (own_theirs, 2 * walkers)):
        sources.append(
            (
                field_here,
                first,
                lambda picked, ref=ref: ref[(x, *picked)],
                lambda picked, ref=ref: ref[(1 - x, *picked)],
            )
        )
    sources += pair_sources(x, field_above, walkers, *blocks[:4])
    sources += pair_sources(x, field_below, walkers, *blocks[4:])

    def emit(w, picked, value):
        summed_ref[(w, *picked)] = value

    build_operator(x, walkers, sources, summed_ref, None, emit)


def early_operator(chips, walkers, fields, own, own_theirs, blocks):
    rows, order = blocks[0].shape
    return pl.pallas_call(
        functools.partial(early_kernel, chips, walkers),
        out_shape=jax.ShapeDtypeStruct((walkers, rows, order), wide),
        in_specs=[vmem_spec] * (5 + len(blocks)),
        out_specs=vmem_spec,
        compiler_params=pltpu.CompilerParams(vmem_limit_bytes=24 << 20),
        name="early_operator",
    )(*fields, own, own_theirs, *blocks)


def collect(chips, vector_ref, pieces):
    z, k, _ = place(chips)
    for step, crossed, first, ref in pieces:
        count, rows, _ = ref.shape
        core = 1 - k if crossed else k
        start = pl.multiple_of((2 * lax.rem(z + step + chips, chips) + core) * rows, rows)
        for w in range(count):
            vector_ref[first + w, pl.ds(start, rows), :] = ref[w]


def vector_pieces(refs):
    here, above, low, high, below, here_t, above_t, low_t, high_t, below_t = refs
    half = low.shape[0]
    return [
        (0, False, 0, here),
        (1, False, 0, above),
        (2, False, 0, low),
        (2, False, half, high),
        (-1, False, 0, below),
        (0, True, 0, here_t),
        (1, True, 0, above_t),
        (2, True, 0, low_t),
        (2, True, half, high_t),
        (-1, True, 0, below_t),
    ]


def first_kernel(chips, walkers, summed_in, field_far, *refs):
    blocks, refs = refs[:4], refs[4:]
    pieces, refs = refs[:10], refs[10:]
    operator_ref, first_ref, narrow_ref, vector_ref = refs
    rows = summed_in.shape[1]
    _, _, x = place(chips)
    collect(chips, vector_ref, vector_pieces(pieces))

    def emit(w, picked, value):
        row, column = picked
        top = value.astype(narrow)
        operator_ref[w, row, column] = top
        rest = (value - top.astype(wide)).astype(narrow)
        operator_ref[w, pl.ds(rows + row.start, row.size), column] = rest

    build_operator(
        x, walkers, pair_sources(x, field_far, walkers, *blocks), summed_in, summed_in, emit
    )
    for w in range(walkers):
        both = jnp.dot(operator_ref[w], vector_ref[w], preferred_element_type=wide)
        term = both[:rows] + both[rows:]
        first_ref[w] = term
        narrow_ref[w] = term.astype(narrow)


def first_application(chips, summed, field_far, blocks, pieces):
    walkers, rows, order = summed.shape
    occupied = pieces[0].shape[2]
    return pl.pallas_call(
        functools.partial(first_kernel, chips, walkers),
        out_shape=[
            jax.ShapeDtypeStruct((walkers, 2 * rows, order), narrow),
            jax.ShapeDtypeStruct((walkers, rows, occupied), wide),
            jax.ShapeDtypeStruct((walkers, rows, occupied), narrow),
        ],
        in_specs=[vmem_spec] * 16,
        out_specs=[vmem_spec] * 3,
        scratch_shapes=[pltpu.VMEM((walkers, order, occupied), narrow)],
        compiler_params=pltpu.CompilerParams(vmem_limit_bytes=24 << 20),
        name="first_application",
    )(summed, field_far, *blocks, *pieces)


def second_kernel(chips, operator_ref, first_ref, orbitals_ref, *refs):
    pieces, (out_ref, vector_ref) = refs[:10], refs[10:]
    walkers, rows, _ = first_ref.shape
    collect(chips, vector_ref, vector_pieces(pieces))
    for w in range(walkers):
        both = jnp.dot(operator_ref[w], vector_ref[w], preferred_element_type=wide)
        second = both[:rows] + both[rows:]
        out_ref[0, :, w, :] = orbitals_ref[0, :, w, :] + first_ref[w] + 0.5 * second


def second_application(chips, operator, first_term, orbitals, pieces):
    walkers, _, order = operator.shape
    occupied = orbitals.shape[3]
    return pl.pallas_call(
        functools.partial(second_kernel, chips),
        out_shape=jax.ShapeDtypeStruct(orbitals.shape, wide),
        in_specs=[vmem_spec] * 13,
        out_specs=vmem_spec,
        scratch_shapes=[pltpu.VMEM((walkers, order, occupied), narrow)],
        compiler_params=pltpu.CompilerParams(vmem_limit_bytes=24 << 20),
        name="second_application",
    )(operator, first_term, orbitals, *pieces)


def row_device(chips):
    devices = 2 * chips

    def ring(value, step):
        pairs = [(i, (i + 2 * step) % devices) for i in range(devices)]
        return lax.ppermute(value, "chol", pairs)

    def core(value):
        return lax.ppermute(value, "chol", [(i, i ^ 1) for i in range(devices)])

    def across(value):
        return lax.ppermute(value, "walk", [(0, 1), (1, 0)])

    def gather_ring(value):
        half = value.shape[0] // 2
        below, above = ring(value, 1), ring(value, -1)
        low, high = ring(below[:half], 1), ring(above[half:], -1)
        return [value, above, low, high, below]

    def device(green_blocks, half_chol, full_chol, meanfield, noise_draws, orbitals):
        walkers, rows, _ = green_blocks.shape
        vectors = half_chol.shape[0]
        slot = lax.axis_index("chol")

        half_theirs = core(half_chol)
        cross_up, cross_down = cut(chips, rows, full_chol, ((1, True, False), (-1, True, False)))
        straight_up, straight_down, far_up, far_down, own_cross = cut(
            chips,
            rows,
            after(full_chol, cross_up),
            (
                (1, False, False),
                (-1, False, False),
                (2, False, False),
                (2, True, False),
                (0, True, True),
            ),
        )
        start = walker_major(orbitals)
        constants = jnp.concatenate(
            [noise_draws.T.reshape(-1), jnp.repeat(meanfield, walkers)]
        )
        constants = jnp.broadcast_to(constants[:, None], (2 * vectors * walkers, 128))
        constants_there = core(constants)
        cross_below, cross_above = ring(cross_up, 1), ring(cross_down, -1)
        own_theirs = core(own_cross)
        below, above = ring(straight_up, 1), ring(straight_down, -1)
        green = after(green_blocks, cross_below, cross_above)
        green_pieces = gather_ring(green)
        far_up, far_down = after((far_up, far_down), below, above)
        far_half, far_half_cross = ring(far_up, 1), ring(far_down, -1)
        start = after(start, far_half, far_half_cross)
        start_pieces = gather_ring(start)
        far, far_cross = ring(far_half, 1), ring(far_half_cross, -1)

        above_theirs, below_theirs = core(cross_above), core(cross_below)
        above_theirs_x, below_theirs_x = across(above_theirs), across(below_theirs)
        above_x, below_x = across(above), across(below)
        far_theirs = core(far_cross)
        far_x, far_theirs_x = across(far), across(far_theirs)

        bias = chip_bias(chips, *green_pieces, half_chol, half_theirs)
        shift_rows, field = chip_field(bias, core(bias), constants, constants_there)
        field_above, field_below, field_far = ring(field, -1), ring(field, 1), ring(field, 2)
        bias_shift = shift_rows[:, 0].reshape(vectors, walkers).T

        own = lax.dynamic_slice_in_dim(full_chol, slot * rows, rows, 1)
        summed = early_operator(
            chips,
            walkers,
            (field, field_above, field_below),
            own,
            own_theirs,
            (
                *(above, above_x, above_theirs, above_theirs_x),
                *(below, below_x, below_theirs, below_theirs_x),
            ),
        )
        operator, first_term, first_narrow = first_application(
            chips,
            summed,
            field_far,
            (far, far_x, far_theirs, far_theirs_x),
            [*start_pieces, *[core(piece) for piece in start_pieces]],
        )
        first_pieces = gather_ring(first_narrow)
        walkers_next = second_application(
            chips,
            operator,
            first_term,
            orbitals,
            [*first_pieces, *[core(piece) for piece in first_pieces]],
        )
        return (walkers_next, bias_shift)

    return device


def solution(mesh):
    placed = (
        P(("grp", "walk"), "chol", "orb"),
        P(("grp", "chol"), None, "orb"),
        P(("grp", "chol"), "orb", None),
        P(("grp", "chol")),
        P(("grp", "walk"), "chol"),
        P("orb", "chol", ("grp", "walk"), None),
    )
    sizes = mesh.shape
    if sizes["orb"] == 1 and sizes["walk"] == 2 and sizes["chol"] == 8:
        per_device = row_device(sizes["chol"] // 2)
    else:
        per_device = general_device
    return jax.shard_map(
        per_device,
        mesh=mesh,
        in_specs=placed,
        out_specs=(P("orb", "chol", ("grp", "walk"), None), P(("grp", "walk"), "chol")),
        check_vma=False,
    )
```

```python
import functools

import jax
import jax.numpy as jnp
from jax import lax
from jax.experimental import pallas as pl
from jax.experimental.pallas import tpu as pltpu
from jax.sharding import PartitionSpec as P

time_root = 0.1


def general_device(green_blocks, half_chol, full_chol, meanfield, noise_draws, orbitals):
    walkers_here = green_blocks.shape[0]
    chol_here = half_chol.shape[0]
    half_rows = full_chol.shape[1]
    orbital_count = full_chol.shape[2]
    occupied = orbitals.shape[3]
    rows_here = orbitals.shape[1]
    partial_bias = jnp.einsum(
        "wki,cki->wc",
        lax.all_gather(green_blocks, "chol", axis=1, tiled=True),
        half_chol,
        preferred_element_type=jnp.float32,
    )
    force_bias = lax.psum(partial_bias, "orb")
    bias_shift = jnp.clip(time_root * (force_bias - meanfield[None, :]), -1.0, 1.0)
    shifted_field = noise_draws - bias_shift
    combined = jnp.zeros((walkers_here, half_rows, orbital_count), jnp.float32)
    for chol_index in range(chol_here):
        combined = combined + shifted_field[:, chol_index, None, None] * full_chol[chol_index][
            None
        ].astype(jnp.float32)
    operator_rows = (time_root * combined).astype(jnp.bfloat16)

    def apply_operator(vector):
        both_halves = lax.all_gather(vector, "orb", axis=0, tiled=True)
        running = jnp.zeros((walkers_here, half_rows, occupied), jnp.float32)
        shard_piece = lax.all_gather(both_halves, "chol", axis=1, tiled=True)
        row_count = shard_piece.shape[1]
        for half_index in range(shard_piece.shape[0]):
            col_block = lax.dynamic_slice_in_dim(
                operator_rows, half_index * half_rows, row_count, 2
            )
            running = running + lax.dot_general(
                col_block,
                shard_piece[half_index],
                (((2,), (0,)), ((0,), (1,))),
                preferred_element_type=jnp.float32,
            )
        summed = lax.psum(running, "chol")
        chol_slot = lax.axis_index("chol")
        owned_rows = lax.dynamic_slice_in_dim(summed, chol_slot * rows_here, rows_here, 1)
        return jnp.transpose(owned_rows, (1, 0, 2))[None]

    first_term = apply_operator(orbitals.astype(jnp.bfloat16))
    second_term = apply_operator(first_term.astype(jnp.bfloat16))
    walkers_next = orbitals + first_term + 0.5 * second_term
    return (walkers_next, bias_shift)


vmem_spec = pl.BlockSpec(memory_space=pltpu.VMEM)
any_spec = pl.BlockSpec(memory_space=pl.ANY)
wide = jnp.float32
narrow = jnp.bfloat16
small = pltpu.CompilerParams(vmem_limit_bytes=16 << 20)


def after(value, *others):
    return lax.optimization_barrier((value, *others))[0]


def place(chips):
    slot = lax.axis_index("chol")
    return slot // 2, slot % 2, lax.axis_index("walk")


def cut_kernel(chips, rows, wanted, full_ref, *refs):
    z, k, x = place(chips)
    outs, sem = refs[:-1], refs[-1]
    copies = []
    for index, (step, crossed, both) in enumerate(wanted):
        core = 1 - k if crossed else k
        start = pl.multiple_of((2 * lax.rem(z + step + chips, chips) + core) * rows, rows)
        picked = pl.ds(start, rows)
        source = full_ref.at[:, picked, :] if both else full_ref.at[x, picked, :]
        copies.append(pltpu.make_async_copy(source, outs[index], sem.at[index]))
        copies[-1].start()
    for copy in copies:
        copy.wait()


def cut(chips, rows, full_chol, wanted):
    order = full_chol.shape[2]
    shapes = [
        jax.ShapeDtypeStruct((2, rows, order) if both else (rows, order), narrow)
        for _, _, both in wanted
    ]
    return pl.pallas_call(
        functools.partial(cut_kernel, chips, rows, wanted),
        out_shape=shapes,
        in_specs=[any_spec],
        out_specs=[vmem_spec] * len(wanted),
        scratch_shapes=[pltpu.SemaphoreType.DMA((len(wanted),))],
        compiler_params=small,
        name="cut_rows",
    )(full_chol)


def start_kernel(orbitals_ref, out_ref):
    for walker in range(out_ref.shape[0]):
        out_ref[walker] = orbitals_ref[0, :, walker, :].astype(narrow)


def walker_major(orbitals):
    _, rows, walkers, occupied = orbitals.shape
    return pl.pallas_call(
        start_kernel,
        out_shape=jax.ShapeDtypeStruct((walkers, rows, occupied), narrow),
        in_specs=[vmem_spec],
        out_specs=vmem_spec,
        compiler_params=small,
        name="walker_major",
    )(orbitals)


def bias_kernel(chips, here_ref, above_ref, low_ref, high_ref, below_ref, mine_ref, theirs_ref, out_ref):
    z, k, _ = place(chips)
    walkers, rows, occupied = here_ref.shape
    vectors = mine_ref.shape[0]
    half = walkers // 2
    step_rows = 16
    totals = [jnp.zeros((8, 128), wide) for _ in range(2 * vectors * walkers)]
    for step, green in ((0, here_ref), (1, above_ref), (2, None), (-1, below_ref)):
        base = (2 * lax.rem(z + step + chips, chips) + k) * rows

        def add(index, totals, base=base, green=green):
            here = pl.multiple_of(index * step_rows, step_rows)
            there = pl.multiple_of(base + index * step_rows, step_rows)
            picked = pl.ds(here, step_rows)
            if green is None:
                greens = [low_ref[w, picked, :] for w in range(half)]
                greens += [high_ref[w, picked, :] for w in range(half)]
            else:
                greens = [green[w, picked, :] for w in range(walkers)]
            greens = [g.astype(wide) for g in greens]
            totals = list(totals)
            for c in range(2 * vectors):
                chol_ref = mine_ref if c < vectors else theirs_ref
                chol = chol_ref[c % vectors, pl.ds(there, step_rows), :].astype(wide)
                for w in range(walkers):
                    product = greens[w] * chol
                    tiles = [
                        product[r : r + 8, n : n + 128]
                        for r in range(0, step_rows, 8)
                        for n in range(0, occupied, 128)
                    ]
                    totals[c * walkers + w] = totals[c * walkers + w] + sum(tiles[1:], tiles[0])
            return tuple(totals)

        totals = lax.fori_loop(0, rows // step_rows, add, tuple(totals))
    for index, total in enumerate(totals):
        value = jnp.sum(jnp.sum(total, axis=0, keepdims=True), axis=1, keepdims=True)
        out_ref[pl.ds(index, 1), :] = jnp.broadcast_to(value, (1, 128))


def chip_bias(chips, here, above, low, high, below, mine, theirs):
    entries = 2 * mine.shape[0] * here.shape[0]
    return pl.pallas_call(
        functools.partial(bias_kernel, chips),
        out_shape=jax.ShapeDtypeStruct((entries, 128), wide),
        in_specs=[vmem_spec] * 7,
        out_specs=vmem_spec,
        compiler_params=small,
        name="chip_bias",
    )(here, above, low, high, below, mine, theirs)


def field_kernel(gathered_ref, shift_ref, field_ref):
    devices, entries, _ = gathered_ref.shape
    part = entries // 4
    here = lax.axis_index("chol")
    for device in range(devices):
        mine, other = gathered_ref.at[device], gathered_ref.at[device ^ 1]
        force = mine[:part, :] + other[part : 2 * part, :]
        noise, mean = mine[2 * part : 3 * part, :], mine[3 * part :, :]
        shift = jnp.clip(time_root * (force - mean), -1.0, 1.0)
        field_ref[device * part : (device + 1) * part, :] = noise - shift

        @pl.when(here == device)
        def _(shift=shift):
            shift_ref[...] = shift


def all_fields(gathered):
    devices, entries, lanes = gathered.shape
    part = entries // 4
    return pl.pallas_call(
        field_kernel,
        out_shape=[
            jax.ShapeDtypeStruct((part, lanes), wide),
            jax.ShapeDtypeStruct((devices * part, lanes), wide),
        ],
        in_specs=[vmem_spec],
        out_specs=[vmem_spec] * 2,
        compiler_params=small,
        name="all_fields",
    )(gathered)


def block_operators(z, x, chips, walkers, field_ref, sources, picked):
    tiles = []
    for step, core, near, other in sources:
        chip = lax.rem(z + step + chips, chips)
        first = (2 * chip + core) * 2 * walkers
        one, two = near(picked).astype(wide), other(picked).astype(wide)
        copies = one.shape[1] // 128
        tiles.append([])
        for w in range(walkers):
            scale_one = field_ref[pl.ds(first + x * walkers + w, 1), :]
            scale_two = field_ref[pl.ds(first + (1 - x) * walkers + w, 1), :]
            scale_one = jnp.concatenate([scale_one] * copies, 1)
            scale_two = jnp.concatenate([scale_two] * copies, 1)
            block = time_root * (scale_one * one + scale_two * two)
            tiles[-1].append(block.astype(narrow))
    return tiles


def over_tiles(rows, order, body):
    high, across = 16, 256
    columns = order // across

    def tile(index, carry):
        row = pl.multiple_of((index // columns) * high, high)
        column = pl.multiple_of((index % columns) * across, across)
        body((pl.ds(row, high), pl.ds(column, across)))
        return carry

    lax.fori_loop(0, (rows // high) * columns, tile, 0)


def of_pair(ref, index):
    return lambda picked: ref[(index, *picked)]


def of_one(ref):
    return lambda picked: ref[picked]


def early_kernel(chips, walkers, field_ref, own, own_theirs, far, far_x, far_theirs, far_theirs_x, summed_ref):
    z, k, x = place(chips)
    sources = [
        (0, k, of_pair(own, x), of_pair(own, 1 - x)),
        (0, 1 - k, of_pair(own_theirs, x), of_pair(own_theirs, 1 - x)),
        (2, k, of_one(far), of_one(far_x)),
        (2, 1 - k, of_one(far_theirs), of_one(far_theirs_x)),
    ]

    def body(picked):
        tiles = block_operators(z, x, chips, walkers, field_ref, sources, picked)
        for w in range(walkers):
            parts = [block[w].astype(wide) for block in tiles]
            summed_ref[(w, *picked)] = sum(parts[1:], parts[0])

    over_tiles(*summed_ref.shape[1:], body)


def early_operator(chips, walkers, field, own, own_theirs, blocks):
    rows, order = blocks[0].shape
    return pl.pallas_call(
        functools.partial(early_kernel, chips, walkers),
        out_shape=jax.ShapeDtypeStruct((walkers, rows, order), wide),
        in_specs=[vmem_spec] * (3 + len(blocks)),
        out_specs=vmem_spec,
        compiler_params=small,
        name="early_operator",
    )(field, own, own_theirs, *blocks)


def collect(chips, vector_ref, pieces, absolute=True):
    z, k, _ = place(chips)
    for step, crossed, first, ref in pieces:
        count, rows, _ = ref.shape
        core = 1 - k if crossed else k
        chip = 2 * lax.rem(z + step + chips, chips) if absolute else 0
        start = pl.multiple_of((chip + core) * rows, rows)
        for w in range(count):
            vector_ref[first + w, pl.ds(start, rows), :] = ref[w]


def vector_pieces(refs):
    here, above, low, high, below, here_t, above_t, low_t, high_t, below_t = refs
    half = low.shape[0]
    return [
        (0, False, 0, here),
        (1, False, 0, above),
        (2, False, 0, low),
        (2, False, half, high),
        (-1, False, 0, below),
        (0, True, 0, here_t),
        (1, True, 0, above_t),
        (2, True, 0, low_t),
        (2, True, half, high_t),
        (-1, True, 0, below_t),
    ]


def middle_kernel(chips, summed_ref, field_ref, above_theirs, below_theirs, *refs):
    pieces, (operator_ref, vector_ref, first_ref) = refs[:10], refs[10:]
    walkers, rows, order = summed_ref.shape
    z, k, x = place(chips)
    collect(chips, vector_ref, vector_pieces(pieces))
    sources = [
        (1, 1 - k, of_pair(above_theirs, x), of_pair(above_theirs, 1 - x)),
        (-1, 1 - k, of_pair(below_theirs, x), of_pair(below_theirs, 1 - x)),
    ]

    def body(picked):
        tiles = block_operators(z, x, chips, walkers, field_ref, sources, picked)
        row, column = picked
        for w in range(walkers):
            value = summed_ref[(w, *picked)]
            for block in tiles:
                value = value + block[w].astype(wide)
            top = value.astype(narrow)
            operator_ref[w, row, column] = top
            rest = (value - top.astype(wide)).astype(narrow)
            operator_ref[w, pl.ds(rows + row.start, row.size), column] = rest

    over_tiles(rows, order, body)
    for w in range(walkers):
        both = jnp.dot(operator_ref[w], vector_ref[w], preferred_element_type=wide)
        first_ref[w] = both[:rows] + both[rows:]


def middle_operator(chips, summed, field, above_theirs, below_theirs, pieces):
    walkers, rows, order = summed.shape
    occupied = pieces[0].shape[2]
    return pl.pallas_call(
        functools.partial(middle_kernel, chips),
        out_shape=[
            jax.ShapeDtypeStruct((walkers, 2 * rows, order), narrow),
            jax.ShapeDtypeStruct((walkers, order, occupied), narrow),
            jax.ShapeDtypeStruct((walkers, rows, occupied), wide),
        ],
        in_specs=[vmem_spec] * 14,
        out_specs=[vmem_spec] * 3,
        compiler_params=small,
        name="middle_operator",
    )(summed, field, above_theirs, below_theirs, *pieces)


def first_kernel(chips, field_ref, above, below, vector_ref, partial_ref, operator_ref, first_ref, narrow_ref):
    walkers, rows, _ = partial_ref.shape
    order = vector_ref.shape[1]
    z, k, x = place(chips)
    sources = [
        (1, k, of_pair(above, x), of_pair(above, 1 - x)),
        (-1, k, of_pair(below, x), of_pair(below, 1 - x)),
    ]

    def body(picked):
        tiles = block_operators(z, x, chips, walkers, field_ref, sources, picked)
        row, column = picked
        for w in range(walkers):
            operator_ref[w, row, column] = tiles[0][w]
            operator_ref[w, pl.ds(rows + row.start, row.size), column] = tiles[1][w]

    over_tiles(rows, order, body)
    for w in range(walkers):
        both = jnp.dot(operator_ref[w], vector_ref[w], preferred_element_type=wide)
        term = partial_ref[w] + (both[:rows] + both[rows:])
        first_ref[w] = term
        narrow_ref[w] = term.astype(narrow)


def first_application(chips, field, above, below, vector, partial):
    walkers, rows, occupied = partial.shape
    order = vector.shape[1]
    return pl.pallas_call(
        functools.partial(first_kernel, chips),
        out_shape=[
            jax.ShapeDtypeStruct((walkers, 2 * rows, order), narrow),
            jax.ShapeDtypeStruct((walkers, rows, occupied), wide),
            jax.ShapeDtypeStruct((walkers, rows, occupied), narrow),
        ],
        in_specs=[vmem_spec] * 5,
        out_specs=[vmem_spec] * 3,
        compiler_params=small,
        name="first_application",
    )(field, above, below, vector, partial)


def applied(chips, step, z, operators, vector, rows, w):
    chip_rows = 2 * rows
    start = pl.multiple_of(lax.rem(z + step + chips, chips) * chip_rows, chip_rows)
    total = None
    for operator_ref in operators:
        both = jnp.dot(
            operator_ref[w, :, pl.ds(start, chip_rows)], vector, preferred_element_type=wide
        )
        part = both[:rows] + both[rows:]
        total = part if total is None else total + part
    return total


def near_kernel(chips, early_ref, late_ref, first_ref, orbitals_ref, *refs):
    here, above, below, here_t, above_t, below_t, out_ref, vector_ref = refs
    walkers, rows, _ = first_ref.shape
    z, _, _ = place(chips)
    for index, (mine, theirs) in enumerate(((here, here_t), (above, above_t), (below, below_t))):
        pieces = [(0, False, 0, mine), (0, True, 0, theirs)]
        collect(chips, vector_ref.at[index], pieces, absolute=False)
    for w in range(walkers):
        second = None
        for index, step in enumerate((0, 1, -1)):
            part = applied(chips, step, z, (early_ref, late_ref), vector_ref[index, w], rows, w)
            second = part if second is None else second + part
        out_ref[w] = orbitals_ref[0, :, w, :] + first_ref[w] + 0.5 * second


def near_application(chips, early, late, first_term, orbitals, pieces):
    walkers, rows, occupied = first_term.shape
    return pl.pallas_call(
        functools.partial(near_kernel, chips),
        out_shape=jax.ShapeDtypeStruct(first_term.shape, wide),
        in_specs=[vmem_spec] * 10,
        out_specs=vmem_spec,
        scratch_shapes=[pltpu.VMEM((3, walkers, 2 * rows, occupied), narrow)],
        compiler_params=small,
        name="near_application",
    )(early, late, first_term, orbitals, *pieces)


def far_kernel(chips, early_ref, late_ref, base_ref, low, high, low_t, high_t, out_ref, vector_ref):
    walkers, rows, _ = base_ref.shape
    z, _, _ = place(chips)
    half = low.shape[0]
    pieces = [(0, False, 0, low), (0, False, half, high), (0, True, 0, low_t), (0, True, half, high_t)]
    collect(chips, vector_ref, pieces, absolute=False)
    for w in range(walkers):
        second = applied(chips, 2, z, (early_ref, late_ref), vector_ref[w], rows, w)
        out_ref[0, :, w, :] = base_ref[w] + 0.5 * second


def far_application(chips, early, late, base, pieces):
    walkers, rows, occupied = base.shape
    return pl.pallas_call(
        functools.partial(far_kernel, chips),
        out_shape=jax.ShapeDtypeStruct((1, rows, walkers, occupied), wide),
        in_specs=[vmem_spec] * 7,
        out_specs=vmem_spec,
        scratch_shapes=[pltpu.VMEM((walkers, 2 * rows, occupied), narrow)],
        compiler_params=small,
        name="far_application",
    )(early, late, base, *pieces)


def row_device(chips):
    devices = 2 * chips

    def ring(value, step):
        pairs = [(i, (i + 2 * step) % devices) for i in range(devices)]
        return lax.ppermute(value, "chol", pairs)

    def core(value):
        return lax.ppermute(value, "chol", [(i, i ^ 1) for i in range(devices)])

    def across(value):
        return lax.ppermute(value, "walk", [(0, 1), (1, 0)])

    def gather_ring(value):
        half = value.shape[0] // 2
        below, above = ring(value, 1), ring(value, -1)
        low, high = ring(below[:half], 1), ring(above[half:], -1)
        return [value, above, low, high, below]

    def device(green_blocks, half_chol, full_chol, meanfield, noise_draws, orbitals):
        walkers, rows, _ = green_blocks.shape
        vectors = half_chol.shape[0]
        slot = lax.axis_index("chol")

        half_theirs = core(half_chol)
        green_pieces = gather_ring(green_blocks)
        far_up, far_down = cut(chips, rows, full_chol, ((2, False, False), (2, True, False)))
        far_half, far_half_cross = ring(far_up, 1), ring(far_down, -1)
        cross_up, cross_down, own_cross = cut(
            chips,
            rows,
            after(full_chol, far_up),
            ((1, True, True), (-1, True, True), (0, True, True)),
        )
        cross_below, cross_above = ring(cross_up, 1), ring(cross_down, -1)
        own_theirs = core(own_cross)
        straight_up, straight_down = cut(
            chips, rows, after(full_chol, cross_up), ((1, False, True), (-1, False, True))
        )
        far, far_cross = ring(far_half, 1), ring(far_half_cross, -1)
        straight_up, straight_down = after((straight_up, straight_down), far_half, far_half_cross)
        below, above = ring(straight_up, 1), ring(straight_down, -1)
        start = after(walker_major(orbitals), far, far_cross)
        start_pieces = gather_ring(start)

        far_theirs = core(far_cross)
        far_x, far_theirs_x = across(far), across(far_theirs)

        bias = chip_bias(chips, *green_pieces, half_chol, half_theirs)
        constants = jnp.concatenate([noise_draws.T.reshape(-1), jnp.repeat(meanfield, walkers)])
        constants = jnp.broadcast_to(constants[:, None], bias.shape)
        gathered = lax.all_gather(jnp.concatenate([bias, constants]), "chol")
        shift_rows, field = all_fields(gathered)
        bias_shift = shift_rows[:, 0].reshape(vectors, walkers).T

        own = lax.dynamic_slice_in_dim(full_chol, slot * rows, rows, 1)
        summed = early_operator(
            chips,
            walkers,
            field,
            own,
            own_theirs,
            (far, far_x, far_theirs, far_theirs_x),
        )
        early, vector, partial = middle_operator(
            chips,
            summed,
            field,
            core(cross_above),
            core(cross_below),
            [*start_pieces, *[core(piece) for piece in start_pieces]],
        )
        late, first_term, first_narrow = first_application(
            chips, field, above, below, vector, partial
        )
        here, above, low, high, below = gather_ring(first_narrow)
        base = near_application(
            chips,
            early,
            late,
            first_term,
            orbitals,
            [here, above, below, core(here), core(above), core(below)],
        )
        walkers_next = far_application(
            chips, early, late, base, [low, high, core(low), core(high)]
        )
        return (walkers_next, bias_shift)

    return device


def solution(mesh):
    placed = (
        P(("grp", "walk"), "chol", "orb"),
        P(("grp", "chol"), None, "orb"),
        P(("grp", "chol"), "orb", None),
        P(("grp", "chol")),
        P(("grp", "walk"), "chol"),
        P("orb", "chol", ("grp", "walk"), None),
    )
    sizes = mesh.shape
    if sizes["orb"] == 1 and sizes["walk"] == 2 and sizes["chol"] == 8:
        per_device = row_device(sizes["chol"] // 2)
    else:
        per_device = general_device
    return jax.shard_map(
        per_device,
        mesh=mesh,
        in_specs=placed,
        out_specs=(P("orb", "chol", ("grp", "walk"), None), P(("grp", "walk"), "chol")),
        check_vma=False,
    )
```

```python
import functools

import jax
import jax.numpy as jnp
from jax import lax
from jax.experimental import pallas as pl
from jax.experimental.pallas import tpu as pltpu
from jax.sharding import PartitionSpec as P

time_root = 0.1


def general_device(green_blocks, half_chol, full_chol, meanfield, noise_draws, orbitals):
    walkers_here = green_blocks.shape[0]
    chol_here = half_chol.shape[0]
    half_rows = full_chol.shape[1]
    orbital_count = full_chol.shape[2]
    occupied = orbitals.shape[3]
    rows_here = orbitals.shape[1]
    partial_bias = jnp.einsum(
        "wki,cki->wc",
        lax.all_gather(green_blocks, "chol", axis=1, tiled=True),
        half_chol,
        preferred_element_type=jnp.float32,
    )
    force_bias = lax.psum(partial_bias, "orb")
    bias_shift = jnp.clip(time_root * (force_bias - meanfield[None, :]), -1.0, 1.0)
    shifted_field = noise_draws - bias_shift
    combined = jnp.zeros((walkers_here, half_rows, orbital_count), jnp.float32)
    for chol_index in range(chol_here):
        combined = combined + shifted_field[:, chol_index, None, None] * full_chol[chol_index][
            None
        ].astype(jnp.float32)
    operator_rows = (time_root * combined).astype(jnp.bfloat16)

    def apply_operator(vector):
        both_halves = lax.all_gather(vector, "orb", axis=0, tiled=True)
        running = jnp.zeros((walkers_here, half_rows, occupied), jnp.float32)
        shard_piece = lax.all_gather(both_halves, "chol", axis=1, tiled=True)
        row_count = shard_piece.shape[1]
        for half_index in range(shard_piece.shape[0]):
            col_block = lax.dynamic_slice_in_dim(
                operator_rows, half_index * half_rows, row_count, 2
            )
            running = running + lax.dot_general(
                col_block,
                shard_piece[half_index],
                (((2,), (0,)), ((0,), (1,))),
                preferred_element_type=jnp.float32,
            )
        summed = lax.psum(running, "chol")
        chol_slot = lax.axis_index("chol")
        owned_rows = lax.dynamic_slice_in_dim(summed, chol_slot * rows_here, rows_here, 1)
        return jnp.transpose(owned_rows, (1, 0, 2))[None]

    first_term = apply_operator(orbitals.astype(jnp.bfloat16))
    second_term = apply_operator(first_term.astype(jnp.bfloat16))
    walkers_next = orbitals + first_term + 0.5 * second_term
    return (walkers_next, bias_shift)


vmem_spec = pl.BlockSpec(memory_space=pltpu.VMEM)
any_spec = pl.BlockSpec(memory_space=pl.ANY)
wide = jnp.float32
narrow = jnp.bfloat16
small = pltpu.CompilerParams(vmem_limit_bytes=16 << 20)


def after(value, *others):
    return lax.optimization_barrier((value, *others))[0]


def place():
    slot = lax.axis_index("chol")
    return slot // 2, slot % 2, lax.axis_index("walk")


def flipped(z, step):
    return lax.bitwise_xor(z, jnp.int32(step))


def cut_kernel(rows, wanted, full_ref, *refs):
    z, k, x = place()
    outs, sem = refs[:-1], refs[-1]
    copies = []
    for index, (step, crossed, both) in enumerate(wanted):
        core = 1 - k if crossed else k
        start = pl.multiple_of((2 * flipped(z, step) + core) * rows, rows)
        picked = pl.ds(start, rows)
        source = full_ref.at[:, picked, :] if both else full_ref.at[x, picked, :]
        copies.append(pltpu.make_async_copy(source, outs[index], sem.at[index]))
        copies[-1].start()
    for copy in copies:
        copy.wait()


def cut(rows, full_chol, wanted):
    order = full_chol.shape[2]
    shapes = [
        jax.ShapeDtypeStruct((2, rows, order) if both else (rows, order), narrow)
        for _, _, both in wanted
    ]
    return pl.pallas_call(
        functools.partial(cut_kernel, rows, wanted),
        out_shape=shapes,
        in_specs=[any_spec],
        out_specs=[vmem_spec] * len(wanted),
        scratch_shapes=[pltpu.SemaphoreType.DMA((len(wanted),))],
        compiler_params=small,
        name="cut_rows",
    )(full_chol)


def start_kernel(orbitals_ref, out_ref):
    for walker in range(out_ref.shape[0]):
        out_ref[walker] = orbitals_ref[0, :, walker, :].astype(narrow)


def walker_major(orbitals):
    _, rows, walkers, occupied = orbitals.shape
    return pl.pallas_call(
        start_kernel,
        out_shape=jax.ShapeDtypeStruct((walkers, rows, occupied), narrow),
        in_specs=[vmem_spec],
        out_specs=vmem_spec,
        compiler_params=small,
        name="walker_major",
    )(orbitals)


def bias_kernel(here_ref, one_ref, two_ref, three_ref, mine_ref, theirs_ref, out_ref):
    z, k, _ = place()
    walkers, rows, occupied = here_ref.shape
    vectors = mine_ref.shape[0]
    step_rows = 16
    totals = [jnp.zeros((8, 128), wide) for _ in range(2 * vectors * walkers)]
    for step, green in enumerate((here_ref, one_ref, two_ref, three_ref)):
        base = (2 * flipped(z, step) + k) * rows

        def add(index, totals, base=base, green=green):
            here = pl.multiple_of(index * step_rows, step_rows)
            there = pl.multiple_of(base + index * step_rows, step_rows)
            picked = pl.ds(here, step_rows)
            greens = [green[w, picked, :] for w in range(walkers)]
            greens = [g.astype(wide) for g in greens]
            totals = list(totals)
            for c in range(2 * vectors):
                chol_ref = mine_ref if c < vectors else theirs_ref
                chol = chol_ref[c % vectors, pl.ds(there, step_rows), :].astype(wide)
                for w in range(walkers):
                    product = greens[w] * chol
                    tiles = [
                        product[r : r + 8, n : n + 128]
                        for r in range(0, step_rows, 8)
                        for n in range(0, occupied, 128)
                    ]
                    totals[c * walkers + w] = totals[c * walkers + w] + sum(tiles[1:], tiles[0])
            return tuple(totals)

        totals = lax.fori_loop(0, rows // step_rows, add, tuple(totals))
    for index, total in enumerate(totals):
        value = jnp.sum(jnp.sum(total, axis=0, keepdims=True), axis=1, keepdims=True)
        out_ref[pl.ds(index, 1), :] = jnp.broadcast_to(value, (1, 128))


def chip_bias(green, mine, theirs):
    entries = 2 * mine.shape[0] * green[0].shape[0]
    return pl.pallas_call(
        bias_kernel,
        out_shape=jax.ShapeDtypeStruct((entries, 128), wide),
        in_specs=[vmem_spec] * 6,
        out_specs=vmem_spec,
        compiler_params=small,
        name="chip_bias",
    )(*green, mine, theirs)


def field_kernel(mine_ref, theirs_ref, noise_ref, noise_there_ref, shift_ref, field_ref):
    half = mine_ref.shape[0] // 2
    low, high = pl.ds(0, half), pl.ds(half, half)
    for rows, other, consts in ((low, high, noise_ref), (high, low, noise_there_ref)):
        force = mine_ref[rows, :] + theirs_ref[other, :]
        shift = jnp.clip(time_root * (force - consts[high, :]), -1.0, 1.0)
        field_ref[rows, :] = consts[low, :] - shift
        if rows is low:
            shift_ref[...] = shift


def chip_field(mine, theirs, noise, noise_there):
    entries = mine.shape[0]
    return pl.pallas_call(
        field_kernel,
        out_shape=[
            jax.ShapeDtypeStruct((entries // 2, 128), wide),
            jax.ShapeDtypeStruct((entries, 128), wide),
        ],
        in_specs=[vmem_spec] * 4,
        out_specs=[vmem_spec] * 2,
        compiler_params=small,
        name="chip_field",
    )(mine, theirs, noise, noise_there)


def block_operators(x, walkers, sources, picked):
    tiles = []
    for field_ref, crossed, near, other in sources:
        first = 2 * walkers * crossed
        one, two = near(picked).astype(wide), other(picked).astype(wide)
        copies = one.shape[1] // 128
        tiles.append([])
        for w in range(walkers):
            scale_one = field_ref[pl.ds(first + x * walkers + w, 1), :]
            scale_two = field_ref[pl.ds(first + (1 - x) * walkers + w, 1), :]
            scale_one = jnp.concatenate([scale_one] * copies, 1)
            scale_two = jnp.concatenate([scale_two] * copies, 1)
            block = time_root * (scale_one * one + scale_two * two)
            tiles[-1].append(block.astype(narrow))
    return tiles


def over_tiles(rows, order, body):
    high, across = 16, 256
    columns = order // across

    def tile(index, carry):
        row = pl.multiple_of((index // columns) * high, high)
        column = pl.multiple_of((index % columns) * across, across)
        body((pl.ds(row, high), pl.ds(column, across)))
        return carry

    lax.fori_loop(0, (rows // high) * columns, tile, 0)


def of_pair(ref, index):
    return lambda picked: ref[(index, *picked)]


def of_one(ref):
    return lambda picked: ref[picked]


def both_cores(field_ref, mine, mine_x, theirs, theirs_x):
    return [
        (field_ref, 0, of_one(mine), of_one(mine_x)),
        (field_ref, 1, of_one(theirs), of_one(theirs_x)),
    ]


def early_kernel(walkers, field_here, field_one, field_two, own, own_theirs, *refs):
    blocks, summed_ref = refs[:-1], refs[-1]
    _, _, x = place()
    sources = [
        (field_here, 0, of_pair(own, x), of_pair(own, 1 - x)),
        (field_here, 1, of_pair(own_theirs, x), of_pair(own_theirs, 1 - x)),
    ]
    sources += both_cores(field_one, *blocks[:4]) + both_cores(field_two, *blocks[4:])

    def body(picked):
        tiles = block_operators(x, walkers, sources, picked)
        for w in range(walkers):
            parts = [block[w].astype(wide) for block in tiles]
            summed_ref[(w, *picked)] = sum(parts[1:], parts[0])

    over_tiles(*summed_ref.shape[1:], body)


def early_operator(walkers, fields, own, own_theirs, blocks):
    rows, order = blocks[0].shape
    return pl.pallas_call(
        functools.partial(early_kernel, walkers),
        out_shape=jax.ShapeDtypeStruct((walkers, rows, order), wide),
        in_specs=[vmem_spec] * (5 + len(blocks)),
        out_specs=vmem_spec,
        compiler_params=small,
        name="early_operator",
    )(*fields, own, own_theirs, *blocks)


def late_kernel(summed_ref, field_ref, *refs):
    blocks, operator_ref = refs[:-1], refs[-1]
    walkers, rows, order = summed_ref.shape
    _, _, x = place()
    sources = both_cores(field_ref, *blocks)

    def body(picked):
        tiles = block_operators(x, walkers, sources, picked)
        row, column = picked
        for w in range(walkers):
            value = summed_ref[(w, *picked)]
            for block in tiles:
                value = value + block[w].astype(wide)
            top = value.astype(narrow)
            operator_ref[w, row, column] = top
            rest = (value - top.astype(wide)).astype(narrow)
            operator_ref[w, pl.ds(rows + row.start, row.size), column] = rest

    over_tiles(rows, order, body)


def split_operator(summed, field, blocks):
    walkers, rows, order = summed.shape
    return pl.pallas_call(
        late_kernel,
        out_shape=jax.ShapeDtypeStruct((walkers, 2 * rows, order), narrow),
        in_specs=[vmem_spec] * (2 + len(blocks)),
        out_specs=vmem_spec,
        compiler_params=small,
        name="split_operator",
    )(summed, field, *blocks)


def applied(operator_ref, vector_ref, step, mine, theirs):
    z, k, _ = place()
    _, rows, _ = mine.shape
    vector_ref[:, pl.ds(pl.multiple_of(k * rows, rows), rows), :] = mine[...]
    vector_ref[:, pl.ds(pl.multiple_of((1 - k) * rows, rows), rows), :] = theirs[...]
    start = pl.multiple_of(flipped(z, step) * 2 * rows, 2 * rows)

    def of_walker(w):
        both = jnp.dot(
            operator_ref[w, :, pl.ds(start, 2 * rows)],
            vector_ref[w],
            preferred_element_type=wide,
        )
        return both[:rows] + both[rows:]

    return of_walker


def near_kernel(operator_ref, *refs):
    pieces, (out_ref, vector_ref) = refs[:6], refs[6:]
    parts = [
        applied(operator_ref, vector_ref.at[step], step, pieces[step], pieces[3 + step])
        for step in range(3)
    ]
    for w in range(out_ref.shape[0]):
        out_ref[w] = parts[0](w) + parts[1](w) + parts[2](w)


def near_application(operator, pieces):
    walkers, rows, occupied = pieces[0].shape
    return pl.pallas_call(
        near_kernel,
        out_shape=jax.ShapeDtypeStruct((walkers, rows, occupied), wide),
        in_specs=[vmem_spec] * 7,
        out_specs=vmem_spec,
        scratch_shapes=[pltpu.VMEM((3, walkers, 2 * rows, occupied), narrow)],
        compiler_params=small,
        name="near_application",
    )(operator, *pieces)


def first_kernel(operator_ref, partial_ref, mine, theirs, first_ref, narrow_ref, vector_ref):
    part = applied(operator_ref, vector_ref, 3, mine, theirs)
    for w in range(first_ref.shape[0]):
        term = partial_ref[w] + part(w)
        first_ref[w] = term
        narrow_ref[w] = term.astype(narrow)


def first_application(operator, partial, mine, theirs):
    walkers, rows, occupied = mine.shape
    return pl.pallas_call(
        first_kernel,
        out_shape=[
            jax.ShapeDtypeStruct((walkers, rows, occupied), wide),
            jax.ShapeDtypeStruct((walkers, rows, occupied), narrow),
        ],
        in_specs=[vmem_spec] * 4,
        out_specs=[vmem_spec] * 2,
        scratch_shapes=[pltpu.VMEM((walkers, 2 * rows, occupied), narrow)],
        compiler_params=small,
        name="first_application",
    )(operator, partial, mine, theirs)


def second_kernel(operator_ref, partial_ref, first_ref, orbitals_ref, mine, theirs, out_ref, vector_ref):
    part = applied(operator_ref, vector_ref, 3, mine, theirs)
    for w in range(first_ref.shape[0]):
        second = partial_ref[w] + part(w)
        out_ref[0, :, w, :] = orbitals_ref[0, :, w, :] + first_ref[w] + 0.5 * second


def second_application(operator, partial, first_term, orbitals, mine, theirs):
    walkers, rows, occupied = mine.shape
    return pl.pallas_call(
        second_kernel,
        out_shape=jax.ShapeDtypeStruct(orbitals.shape, wide),
        in_specs=[vmem_spec] * 6,
        out_specs=vmem_spec,
        scratch_shapes=[pltpu.VMEM((walkers, 2 * rows, occupied), narrow)],
        compiler_params=small,
        name="second_application",
    )(operator, partial, first_term, orbitals, mine, theirs)


def to_chip(value, step):
    return lax.ppermute(value, "chol", [(i, i ^ (2 * step)) for i in range(8)])


def to_core(value):
    return lax.ppermute(value, "chol", [(i, i ^ 1) for i in range(8)])


def across(value):
    return lax.ppermute(value, "walk", [(0, 1), (1, 0)])


def row_device(green_blocks, half_chol, full_chol, meanfield, noise_draws, orbitals):
    walkers, rows, _ = green_blocks.shape
    vectors = half_chol.shape[0]

    green_two, green_one = to_chip(green_blocks, 2), to_chip(green_blocks, 1)
    half_theirs = to_core(half_chol)
    constants = jnp.concatenate([noise_draws.T.reshape(-1), jnp.repeat(meanfield, walkers)])
    constants = jnp.broadcast_to(constants[:, None], (2 * vectors * walkers, 128))
    constants_theirs = to_core(constants)

    cross, straight = {}, {}
    cross[2], straight[2] = cut(rows, full_chol, ((2, True, False), (2, False, False)))
    cross[1], straight[1], cross[3], straight[3], own, own_cross = cut(
        rows,
        after(full_chol, cross[2]),
        (
            (1, True, False),
            (1, False, False),
            (3, True, False),
            (3, False, False),
            (0, False, True),
            (0, True, True),
        ),
    )
    own_theirs = to_core(own_cross)
    blocks = {}

    def exchange(step):
        theirs = to_core(to_chip(cross[step], step))
        mine = to_chip(straight[step], step)
        blocks[step] = (mine, across(mine), theirs, across(theirs))
        return mine

    second_mine = exchange(2)
    green_three = to_chip(green_two, 1)
    cross[1], straight[1] = after((cross[1], straight[1]), green_two)
    first_mine = exchange(1)
    cross[3], straight[3] = after((cross[3], straight[3]), green_three)
    exchange(3)

    start = after(walker_major(orbitals), second_mine, first_mine)
    start_two, start_one = to_chip(start, 2), to_chip(start, 1)
    start_three = to_chip(start_two, 1)

    green = (green_blocks, green_one, green_two, green_three)
    bias = chip_bias(green, half_chol, half_theirs)
    shift_rows, field = chip_field(bias, to_core(bias), constants, constants_theirs)
    field_one, field_two, field_three = (to_chip(field, step) for step in (1, 2, 3))
    bias_shift = shift_rows[:, 0].reshape(vectors, walkers).T

    summed = early_operator(
        walkers,
        (field, field_one, field_two),
        own,
        own_theirs,
        (*blocks[1], *blocks[2]),
    )
    operator = split_operator(summed, field_three, blocks[3])

    near = [start, start_one, start_two]
    partial = near_application(operator, [*near, *[to_core(piece) for piece in near]])
    first_term, first_narrow = first_application(
        operator, partial, start_three, to_core(start_three)
    )
    first_two, first_one = to_chip(first_narrow, 2), to_chip(first_narrow, 1)
    first_three = to_chip(first_two, 1)
    near = [first_narrow, first_one, first_two]
    partial = near_application(operator, [*near, *[to_core(piece) for piece in near]])
    walkers_next = second_application(
        operator, partial, first_term, orbitals, first_three, to_core(first_three)
    )
    return (walkers_next, bias_shift)


def solution(mesh):
    placed = (
        P(("grp", "walk"), "chol", "orb"),
        P(("grp", "chol"), None, "orb"),
        P(("grp", "chol"), "orb", None),
        P(("grp", "chol")),
        P(("grp", "walk"), "chol"),
        P("orb", "chol", ("grp", "walk"), None),
    )
    sizes = mesh.shape
    if sizes["orb"] == 1 and sizes["walk"] == 2 and sizes["chol"] == 8:
        per_device = row_device
    else:
        per_device = general_device
    return jax.shard_map(
        per_device,
        mesh=mesh,
        in_specs=placed,
        out_specs=(P("orb", "chol", ("grp", "walk"), None), P(("grp", "walk"), "chol")),
        check_vma=False,
    )
```

```python
import functools

import jax
import jax.numpy as jnp
from jax import lax
from jax.experimental import pallas as pl
from jax.experimental.pallas import tpu as pltpu
from jax.sharding import PartitionSpec as P

time_root = 0.1


def general_device(green_blocks, half_chol, full_chol, meanfield, noise_draws, orbitals):
    walkers_here = green_blocks.shape[0]
    chol_here = half_chol.shape[0]
    half_rows = full_chol.shape[1]
    orbital_count = full_chol.shape[2]
    occupied = orbitals.shape[3]
    rows_here = orbitals.shape[1]
    partial_bias = jnp.einsum(
        "wki,cki->wc",
        lax.all_gather(green_blocks, "chol", axis=1, tiled=True),
        half_chol,
        preferred_element_type=jnp.float32,
    )
    force_bias = lax.psum(partial_bias, "orb")
    bias_shift = jnp.clip(time_root * (force_bias - meanfield[None, :]), -1.0, 1.0)
    shifted_field = noise_draws - bias_shift
    combined = jnp.zeros((walkers_here, half_rows, orbital_count), jnp.float32)
    for chol_index in range(chol_here):
        combined = combined + shifted_field[:, chol_index, None, None] * full_chol[chol_index][
            None
        ].astype(jnp.float32)
    operator_rows = (time_root * combined).astype(jnp.bfloat16)

    def apply_operator(vector):
        both_halves = lax.all_gather(vector, "orb", axis=0, tiled=True)
        running = jnp.zeros((walkers_here, half_rows, occupied), jnp.float32)
        shard_piece = lax.all_gather(both_halves, "chol", axis=1, tiled=True)
        row_count = shard_piece.shape[1]
        for half_index in range(shard_piece.shape[0]):
            col_block = lax.dynamic_slice_in_dim(
                operator_rows, half_index * half_rows, row_count, 2
            )
            running = running + lax.dot_general(
                col_block,
                shard_piece[half_index],
                (((2,), (0,)), ((0,), (1,))),
                preferred_element_type=jnp.float32,
            )
        summed = lax.psum(running, "chol")
        chol_slot = lax.axis_index("chol")
        owned_rows = lax.dynamic_slice_in_dim(summed, chol_slot * rows_here, rows_here, 1)
        return jnp.transpose(owned_rows, (1, 0, 2))[None]

    first_term = apply_operator(orbitals.astype(jnp.bfloat16))
    second_term = apply_operator(first_term.astype(jnp.bfloat16))
    walkers_next = orbitals + first_term + 0.5 * second_term
    return (walkers_next, bias_shift)


vmem_spec = pl.BlockSpec(memory_space=pltpu.VMEM)
hbm_spec = pl.BlockSpec(memory_space=pltpu.HBM)
wide = jnp.float32
narrow = jnp.bfloat16
small = pltpu.CompilerParams(vmem_limit_bytes=8 << 20)
large = pltpu.CompilerParams(vmem_limit_bytes=16 << 20)


def after(value, *others):
    return lax.optimization_barrier((value, *others))[0]


def place():
    slot = lax.axis_index("chol")
    return slot // 2, slot % 2, lax.axis_index("walk")


def flipped(z, step):
    return lax.bitwise_xor(z, jnp.int32(step))


def cut_kernel(rows, wanted, full_ref, *refs):
    z, k, x = place()
    outs, sem = refs[:-1], refs[-1]
    copies = []
    for index, (step, crossed, both) in enumerate(wanted):
        core = 1 - k if crossed else k
        start = pl.multiple_of((2 * flipped(z, step) + core) * rows, rows)
        picked = pl.ds(start, rows)
        source = full_ref.at[:, picked, :] if both else full_ref.at[x, picked, :]
        copies.append(pltpu.make_async_copy(source, outs[index], sem.at[index]))
        copies[-1].start()
    for copy in copies:
        copy.wait()


def cut(rows, full_chol, wanted):
    order = full_chol.shape[2]
    shapes = [
        jax.ShapeDtypeStruct((2, rows, order) if both else (rows, order), narrow)
        for _, _, both in wanted
    ]
    return pl.pallas_call(
        functools.partial(cut_kernel, rows, wanted),
        out_shape=shapes,
        in_specs=[hbm_spec],
        out_specs=[vmem_spec] * len(wanted),
        scratch_shapes=[pltpu.SemaphoreType.DMA((len(wanted),))],
        compiler_params=small,
        name="cut_rows",
    )(full_chol)


def start_kernel(orbitals_ref, out_ref):
    for walker in range(out_ref.shape[0]):
        out_ref[walker] = orbitals_ref[0, :, walker, :].astype(narrow)


def walker_major(orbitals):
    _, rows, walkers, occupied = orbitals.shape
    return pl.pallas_call(
        start_kernel,
        out_shape=jax.ShapeDtypeStruct((walkers, rows, occupied), narrow),
        in_specs=[vmem_spec],
        out_specs=vmem_spec,
        compiler_params=small,
        name="walker_major",
    )(orbitals)


def bias_kernel(here_ref, one_ref, two_ref, three_ref, mine_ref, theirs_ref, out_ref):
    z, k, _ = place()
    walkers, rows, occupied = here_ref.shape
    vectors = mine_ref.shape[0]
    step_rows = 16
    totals = [jnp.zeros((8, 128), wide) for _ in range(2 * vectors * walkers)]
    for step, green in enumerate((here_ref, one_ref, two_ref, three_ref)):
        base = (2 * flipped(z, step) + k) * rows

        def add(index, totals, base=base, green=green):
            here = pl.multiple_of(index * step_rows, step_rows)
            there = pl.multiple_of(base + index * step_rows, step_rows)
            picked = pl.ds(here, step_rows)
            greens = [green[w, picked, :] for w in range(walkers)]
            greens = [g.astype(wide) for g in greens]
            totals = list(totals)
            for c in range(2 * vectors):
                chol_ref = mine_ref if c < vectors else theirs_ref
                chol = chol_ref[c % vectors, pl.ds(there, step_rows), :].astype(wide)
                for w in range(walkers):
                    product = greens[w] * chol
                    tiles = [
                        product[r : r + 8, n : n + 128]
                        for r in range(0, step_rows, 8)
                        for n in range(0, occupied, 128)
                    ]
                    totals[c * walkers + w] = totals[c * walkers + w] + sum(tiles[1:], tiles[0])
            return tuple(totals)

        totals = lax.fori_loop(0, rows // step_rows, add, tuple(totals))
    for index, total in enumerate(totals):
        value = jnp.sum(jnp.sum(total, axis=0, keepdims=True), axis=1, keepdims=True)
        out_ref[pl.ds(index, 1), :] = jnp.broadcast_to(value, (1, 128))


def chip_bias(green, mine, theirs):
    entries = 2 * mine.shape[0] * green[0].shape[0]
    return pl.pallas_call(
        bias_kernel,
        out_shape=jax.ShapeDtypeStruct((entries, 128), wide),
        in_specs=[vmem_spec] * 6,
        out_specs=vmem_spec,
        compiler_params=small,
        name="chip_bias",
    )(*green, mine, theirs)


def field_kernel(mine_ref, theirs_ref, noise_ref, noise_there_ref, shift_ref, field_ref):
    half = mine_ref.shape[0] // 2
    low, high = pl.ds(0, half), pl.ds(half, half)
    for rows, other, consts in ((low, high, noise_ref), (high, low, noise_there_ref)):
        force = mine_ref[rows, :] + theirs_ref[other, :]
        shift = jnp.clip(time_root * (force - consts[high, :]), -1.0, 1.0)
        field_ref[rows, :] = consts[low, :] - shift
        if rows is low:
            walkers, vectors = shift_ref.shape
            for vector in range(vectors):
                part = shift[vector * walkers : (vector + 1) * walkers, :1]
                shift_ref[:, vector : vector + 1] = part


def chip_field(mine, theirs, noise, noise_there, walkers):
    entries = mine.shape[0]
    return pl.pallas_call(
        field_kernel,
        out_shape=[
            jax.ShapeDtypeStruct((walkers, entries // 2 // walkers), wide),
            jax.ShapeDtypeStruct((entries, 128), wide),
        ],
        in_specs=[vmem_spec] * 4,
        out_specs=[vmem_spec] * 2,
        compiler_params=small,
        name="chip_field",
    )(mine, theirs, noise, noise_there)


def block_operators(x, walkers, sources, picked):
    tiles = []
    for field_ref, crossed, near, other in sources:
        first = 2 * walkers * crossed
        one, two = near(picked).astype(wide), other(picked).astype(wide)
        copies = one.shape[1] // 128
        tiles.append([])
        for w in range(walkers):
            scale_one = field_ref[pl.ds(first + x * walkers + w, 1), :]
            scale_two = field_ref[pl.ds(first + (1 - x) * walkers + w, 1), :]
            scale_one = jnp.concatenate([scale_one] * copies, 1)
            scale_two = jnp.concatenate([scale_two] * copies, 1)
            block = time_root * (scale_one * one + scale_two * two)
            tiles[-1].append(block.astype(narrow))
    return tiles


def over_tiles(rows, order, body):
    high, across = 16, 256
    columns = order // across

    def tile(index, carry):
        row = pl.multiple_of((index // columns) * high, high)
        column = pl.multiple_of((index % columns) * across, across)
        body((pl.ds(row, high), pl.ds(column, across)))
        return carry

    lax.fori_loop(0, (rows // high) * columns, tile, 0)


def of_pair(ref, index):
    return lambda picked: ref[(index, *picked)]


def of_one(ref):
    return lambda picked: ref[picked]


def both_cores(field_ref, mine, mine_x, theirs, theirs_x):
    return [
        (field_ref, 0, of_one(mine), of_one(mine_x)),
        (field_ref, 1, of_one(theirs), of_one(theirs_x)),
    ]


def early_kernel(walkers, field_here, field_one, field_two, own, own_theirs, *refs):
    blocks, summed_ref = refs[:-1], refs[-1]
    _, _, x = place()
    sources = [
        (field_here, 0, of_pair(own, x), of_pair(own, 1 - x)),
        (field_here, 1, of_pair(own_theirs, x), of_pair(own_theirs, 1 - x)),
    ]
    sources += both_cores(field_one, *blocks[:4]) + both_cores(field_two, *blocks[4:])

    def body(picked):
        tiles = block_operators(x, walkers, sources, picked)
        for w in range(walkers):
            parts = [block[w].astype(wide) for block in tiles]
            summed_ref[(w, *picked)] = sum(parts[1:], parts[0])

    over_tiles(*summed_ref.shape[1:], body)


def early_operator(walkers, fields, own, own_theirs, blocks):
    rows, order = blocks[0].shape
    return pl.pallas_call(
        functools.partial(early_kernel, walkers),
        out_shape=jax.ShapeDtypeStruct((walkers, rows, order), wide),
        in_specs=[vmem_spec] * (5 + len(blocks)),
        out_specs=vmem_spec,
        compiler_params=large,
        name="early_operator",
    )(*fields, own, own_theirs, *blocks)


def late_kernel(summed_ref, field_ref, *refs):
    blocks, operator_ref = refs[:-1], refs[-1]
    walkers, rows, order = summed_ref.shape
    _, _, x = place()
    sources = both_cores(field_ref, *blocks)

    def body(picked):
        tiles = block_operators(x, walkers, sources, picked)
        row, column = picked
        for w in range(walkers):
            value = summed_ref[(w, *picked)]
            for block in tiles:
                value = value + block[w].astype(wide)
            top = value.astype(narrow)
            operator_ref[w, row, column] = top
            rest = (value - top.astype(wide)).astype(narrow)
            operator_ref[w, pl.ds(rows + row.start, row.size), column] = rest

    over_tiles(rows, order, body)


def split_operator(summed, field, blocks):
    walkers, rows, order = summed.shape
    return pl.pallas_call(
        late_kernel,
        out_shape=jax.ShapeDtypeStruct((walkers, 2 * rows, order), narrow),
        in_specs=[vmem_spec] * (2 + len(blocks)),
        out_specs=vmem_spec,
        compiler_params=large,
        name="split_operator",
    )(summed, field, *blocks)


def applied(operator_ref, vector_ref, step, mine, theirs):
    z, k, _ = place()
    _, rows, _ = mine.shape
    vector_ref[:, pl.ds(pl.multiple_of(k * rows, rows), rows), :] = mine[...]
    vector_ref[:, pl.ds(pl.multiple_of((1 - k) * rows, rows), rows), :] = theirs[...]
    start = pl.multiple_of(flipped(z, step) * 2 * rows, 2 * rows)

    def of_walker(w):
        both = jnp.dot(
            operator_ref[w, :, pl.ds(start, 2 * rows)],
            vector_ref[w],
            preferred_element_type=wide,
        )
        return both[:rows] + both[rows:]

    return of_walker


def near_kernel(operator_ref, *refs):
    pieces, (out_ref, vector_ref) = refs[:6], refs[6:]
    parts = [
        applied(operator_ref, vector_ref.at[step], step, pieces[step], pieces[3 + step])
        for step in range(3)
    ]
    for w in range(out_ref.shape[0]):
        out_ref[w] = parts[0](w) + parts[1](w) + parts[2](w)


def near_application(operator, pieces):
    walkers, rows, occupied = pieces[0].shape
    return pl.pallas_call(
        near_kernel,
        out_shape=jax.ShapeDtypeStruct((walkers, rows, occupied), wide),
        in_specs=[vmem_spec] * 7,
        out_specs=vmem_spec,
        scratch_shapes=[pltpu.VMEM((3, walkers, 2 * rows, occupied), narrow)],
        compiler_params=small,
        name="near_application",
    )(operator, *pieces)


def first_kernel(operator_ref, partial_ref, mine, theirs, first_ref, narrow_ref, vector_ref):
    part = applied(operator_ref, vector_ref, 3, mine, theirs)
    for w in range(first_ref.shape[0]):
        term = partial_ref[w] + part(w)
        first_ref[w] = term
        narrow_ref[w] = term.astype(narrow)


def first_application(operator, partial, mine, theirs):
    walkers, rows, occupied = mine.shape
    return pl.pallas_call(
        first_kernel,
        out_shape=[
            jax.ShapeDtypeStruct((walkers, rows, occupied), wide),
            jax.ShapeDtypeStruct((walkers, rows, occupied), narrow),
        ],
        in_specs=[vmem_spec] * 4,
        out_specs=[vmem_spec] * 2,
        scratch_shapes=[pltpu.VMEM((walkers, 2 * rows, occupied), narrow)],
        compiler_params=small,
        name="first_application",
    )(operator, partial, mine, theirs)


def second_kernel(operator_ref, partial_ref, first_ref, orbitals_ref, mine, theirs, out_ref, vector_ref):
    part = applied(operator_ref, vector_ref, 3, mine, theirs)
    for w in range(first_ref.shape[0]):
        second = partial_ref[w] + part(w)
        out_ref[0, :, w, :] = orbitals_ref[0, :, w, :] + first_ref[w] + 0.5 * second


def second_application(operator, partial, first_term, orbitals, mine, theirs):
    walkers, rows, occupied = mine.shape
    return pl.pallas_call(
        second_kernel,
        out_shape=jax.ShapeDtypeStruct(orbitals.shape, wide),
        in_specs=[vmem_spec] * 6,
        out_specs=vmem_spec,
        scratch_shapes=[pltpu.VMEM((walkers, 2 * rows, occupied), narrow)],
        compiler_params=small,
        name="second_application",
    )(operator, partial, first_term, orbitals, mine, theirs)


def to_chip(value, step):
    return lax.ppermute(value, "chol", [(i, i ^ (2 * step)) for i in range(8)])


def to_core(value):
    return lax.ppermute(value, "chol", [(i, i ^ 1) for i in range(8)])


def across(value):
    return lax.ppermute(value, "walk", [(0, 1), (1, 0)])


def row_device(green_blocks, half_chol, full_chol, meanfield, noise_draws, orbitals):
    walkers, rows, _ = green_blocks.shape
    vectors = half_chol.shape[0]

    green_two, green_one = to_chip(green_blocks, 2), to_chip(green_blocks, 1)
    half_theirs = to_core(half_chol)
    constants = jnp.concatenate([noise_draws.T.reshape(-1), jnp.repeat(meanfield, walkers)])
    constants = jnp.broadcast_to(constants[:, None], (2 * vectors * walkers, 128))
    constants_theirs = to_core(constants)

    green_three = to_chip(green_two, 1)

    cross, straight = {}, {}
    cross[2], straight[2] = cut(rows, full_chol, ((2, True, False), (2, False, False)))
    cross[3], straight[3], cross[1], straight[1], own, own_cross = cut(
        rows,
        after(full_chol, cross[2]),
        (
            (3, True, False),
            (3, False, False),
            (1, True, False),
            (1, False, False),
            (0, False, True),
            (0, True, True),
        ),
    )
    own_theirs = to_core(own_cross)

    green = (green_blocks, green_one, green_two, green_three)
    bias = chip_bias(green, half_chol, half_theirs)
    bias_shift, field = chip_field(bias, to_core(bias), constants, constants_theirs, walkers)
    field_one, field_two, field_three = (to_chip(field, step) for step in (1, 2, 3))

    cross_mine, mine = {}, {}
    cross_mine[2], mine[2] = to_chip(cross[2], 2), to_chip(straight[2], 2)
    cross_mine[3] = to_chip(cross[3], 3)
    mine[3] = to_chip(after(straight[3], cross_mine[2]), 3)
    cross_mine[1] = to_chip(after(cross[1], green_three), 1)
    mine[1] = to_chip(after(straight[1], field_one), 1)
    blocks = {}
    for step in (2, 3, 1):
        theirs = to_core(cross_mine[step])
        blocks[step] = (mine[step], across(mine[step]), theirs, across(theirs))

    start = after(walker_major(orbitals), mine[2], cross_mine[3])
    start_two, start_one = to_chip(start, 2), to_chip(start, 1)
    start_three = to_chip(start_two, 1)

    summed = early_operator(
        walkers,
        (field, field_one, field_two),
        own,
        own_theirs,
        (*blocks[1], *blocks[2]),
    )
    operator = split_operator(summed, field_three, blocks[3])

    near = [start, start_one, start_two]
    partial = near_application(operator, [*near, *[to_core(piece) for piece in near]])
    first_term, first_narrow = first_application(
        operator, partial, start_three, to_core(start_three)
    )
    first_two, first_one = to_chip(first_narrow, 2), to_chip(first_narrow, 1)
    first_three = to_chip(first_two, 1)
    near = [first_narrow, first_one, first_two]
    partial = near_application(operator, [*near, *[to_core(piece) for piece in near]])
    walkers_next = second_application(
        operator, partial, first_term, orbitals, first_three, to_core(first_three)
    )
    return (walkers_next, bias_shift)


def solution(mesh):
    placed = (
        P(("grp", "walk"), "chol", "orb"),
        P(("grp", "chol"), None, "orb"),
        P(("grp", "chol"), "orb", None),
        P(("grp", "chol")),
        P(("grp", "walk"), "chol"),
        P("orb", "chol", ("grp", "walk"), None),
    )
    sizes = mesh.shape
    if sizes["orb"] == 1 and sizes["walk"] == 2 and sizes["chol"] == 8:
        per_device = row_device
    else:
        per_device = general_device
    return jax.shard_map(
        per_device,
        mesh=mesh,
        in_specs=placed,
        out_specs=(P("orb", "chol", ("grp", "walk"), None), P(("grp", "walk"), "chol")),
        check_vma=False,
    )
```

```python
import functools

import jax
import jax.numpy as jnp
from jax import lax
from jax.experimental import pallas as pl
from jax.experimental.pallas import tpu as pltpu
from jax.sharding import PartitionSpec as P

time_root = 0.1


def general_device(green_blocks, half_chol, full_chol, meanfield, noise_draws, orbitals):
    walkers_here = green_blocks.shape[0]
    chol_here = half_chol.shape[0]
    half_rows = full_chol.shape[1]
    orbital_count = full_chol.shape[2]
    occupied = orbitals.shape[3]
    rows_here = orbitals.shape[1]
    partial_bias = jnp.einsum(
        "wki,cki->wc",
        lax.all_gather(green_blocks, "chol", axis=1, tiled=True),
        half_chol,
        preferred_element_type=jnp.float32,
    )
    force_bias = lax.psum(partial_bias, "orb")
    bias_shift = jnp.clip(time_root * (force_bias - meanfield[None, :]), -1.0, 1.0)
    shifted_field = noise_draws - bias_shift
    combined = jnp.zeros((walkers_here, half_rows, orbital_count), jnp.float32)
    for chol_index in range(chol_here):
        combined = combined + shifted_field[:, chol_index, None, None] * full_chol[chol_index][
            None
        ].astype(jnp.float32)
    operator_rows = (time_root * combined).astype(jnp.bfloat16)

    def apply_operator(vector):
        both_halves = lax.all_gather(vector, "orb", axis=0, tiled=True)
        running = jnp.zeros((walkers_here, half_rows, occupied), jnp.float32)
        shard_piece = lax.all_gather(both_halves, "chol", axis=1, tiled=True)
        row_count = shard_piece.shape[1]
        for half_index in range(shard_piece.shape[0]):
            col_block = lax.dynamic_slice_in_dim(
                operator_rows, half_index * half_rows, row_count, 2
            )
            running = running + lax.dot_general(
                col_block,
                shard_piece[half_index],
                (((2,), (0,)), ((0,), (1,))),
                preferred_element_type=jnp.float32,
            )
        summed = lax.psum(running, "chol")
        chol_slot = lax.axis_index("chol")
        owned_rows = lax.dynamic_slice_in_dim(summed, chol_slot * rows_here, rows_here, 1)
        return jnp.transpose(owned_rows, (1, 0, 2))[None]

    first_term = apply_operator(orbitals.astype(jnp.bfloat16))
    second_term = apply_operator(first_term.astype(jnp.bfloat16))
    walkers_next = orbitals + first_term + 0.5 * second_term
    return (walkers_next, bias_shift)


vmem_spec = pl.BlockSpec(memory_space=pltpu.VMEM)
hbm_spec = pl.BlockSpec(memory_space=pltpu.HBM)
wide = jnp.float32
narrow = jnp.bfloat16
small = pltpu.CompilerParams(vmem_limit_bytes=8 << 20)
large = pltpu.CompilerParams(vmem_limit_bytes=16 << 20)


def after(value, *others):
    return lax.optimization_barrier((value, *others))[0]


def place():
    slot = lax.axis_index("chol")
    return slot // 2, slot % 2, lax.axis_index("walk")


def flipped(z, step):
    return lax.bitwise_xor(z, jnp.int32(step))


def cut_kernel(rows, wanted, full_ref, *refs):
    z, k, x = place()
    outs, sem = refs[:-1], refs[-1]
    copies = []
    for index, (step, crossed, both) in enumerate(wanted):
        core = 1 - k if crossed else k
        start = pl.multiple_of((2 * flipped(z, step) + core) * rows, rows)
        picked = pl.ds(start, rows)
        source = full_ref.at[:, picked, :] if both else full_ref.at[x, picked, :]
        copies.append(pltpu.make_async_copy(source, outs[index], sem.at[index]))
        copies[-1].start()
    for copy in copies:
        copy.wait()


def cut(rows, full_chol, wanted):
    order = full_chol.shape[2]
    shapes = [
        jax.ShapeDtypeStruct((2, rows, order) if both else (rows, order), narrow)
        for _, _, both in wanted
    ]
    return pl.pallas_call(
        functools.partial(cut_kernel, rows, wanted),
        out_shape=shapes,
        in_specs=[hbm_spec],
        out_specs=[vmem_spec] * len(wanted),
        scratch_shapes=[pltpu.SemaphoreType.DMA((len(wanted),))],
        compiler_params=small,
        name="cut_rows",
    )(full_chol)


def start_kernel(orbitals_ref, out_ref):
    for walker in range(out_ref.shape[0]):
        out_ref[walker] = orbitals_ref[0, :, walker, :].astype(narrow)


def walker_major(orbitals):
    _, rows, walkers, occupied = orbitals.shape
    return pl.pallas_call(
        start_kernel,
        out_shape=jax.ShapeDtypeStruct((walkers, rows, occupied), narrow),
        in_specs=[vmem_spec],
        out_specs=vmem_spec,
        compiler_params=small,
        name="walker_major",
    )(orbitals)


def bias_kernel(here_ref, one_ref, two_ref, three_ref, mine_ref, theirs_ref, out_ref):
    z, k, _ = place()
    walkers, rows, occupied = here_ref.shape
    vectors = mine_ref.shape[0]
    step_rows = 16
    totals = [jnp.zeros((8, 128), wide) for _ in range(2 * vectors * walkers)]
    for step, green in enumerate((here_ref, one_ref, two_ref, three_ref)):
        base = (2 * flipped(z, step) + k) * rows

        def add(index, totals, base=base, green=green):
            here = pl.multiple_of(index * step_rows, step_rows)
            there = pl.multiple_of(base + index * step_rows, step_rows)
            picked = pl.ds(here, step_rows)
            greens = [green[w, picked, :] for w in range(walkers)]
            greens = [g.astype(wide) for g in greens]
            totals = list(totals)
            for c in range(2 * vectors):
                chol_ref = mine_ref if c < vectors else theirs_ref
                chol = chol_ref[c % vectors, pl.ds(there, step_rows), :].astype(wide)
                for w in range(walkers):
                    product = greens[w] * chol
                    tiles = [
                        product[r : r + 8, n : n + 128]
                        for r in range(0, step_rows, 8)
                        for n in range(0, occupied, 128)
                    ]
                    totals[c * walkers + w] = totals[c * walkers + w] + sum(tiles[1:], tiles[0])
            return tuple(totals)

        totals = lax.fori_loop(0, rows // step_rows, add, tuple(totals))
    for index, total in enumerate(totals):
        value = jnp.sum(jnp.sum(total, axis=0, keepdims=True), axis=1, keepdims=True)
        out_ref[pl.ds(index, 1), :] = jnp.broadcast_to(value, (1, 128))


def chip_bias(green, mine, theirs):
    entries = 2 * mine.shape[0] * green[0].shape[0]
    return pl.pallas_call(
        bias_kernel,
        out_shape=jax.ShapeDtypeStruct((entries, 128), wide),
        in_specs=[vmem_spec] * 6,
        out_specs=vmem_spec,
        compiler_params=small,
        name="chip_bias",
    )(*green, mine, theirs)


def field_kernel(mine_ref, theirs_ref, noise_ref, noise_there_ref, shift_ref, field_ref):
    half = mine_ref.shape[0] // 2
    low, high = pl.ds(0, half), pl.ds(half, half)
    for rows, other, consts in ((low, high, noise_ref), (high, low, noise_there_ref)):
        force = mine_ref[rows, :] + theirs_ref[other, :]
        shift = jnp.clip(time_root * (force - consts[high, :]), -1.0, 1.0)
        field_ref[rows, :] = consts[low, :] - shift
        if rows is low:
            walkers, vectors = shift_ref.shape
            for vector in range(vectors):
                part = shift[vector * walkers : (vector + 1) * walkers, :1]
                shift_ref[:, vector : vector + 1] = part


def chip_field(mine, theirs, noise, noise_there, walkers):
    entries = mine.shape[0]
    return pl.pallas_call(
        field_kernel,
        out_shape=[
            jax.ShapeDtypeStruct((walkers, entries // 2 // walkers), wide),
            jax.ShapeDtypeStruct((entries, 128), wide),
        ],
        in_specs=[vmem_spec] * 4,
        out_specs=[vmem_spec] * 2,
        compiler_params=small,
        name="chip_field",
    )(mine, theirs, noise, noise_there)


def block_operators(x, walkers, sources, picked):
    tiles = []
    for field_ref, crossed, near, other in sources:
        first = 2 * walkers * crossed
        one, two = near(picked).astype(wide), other(picked).astype(wide)
        copies = one.shape[1] // 128
        tiles.append([])
        for w in range(walkers):
            scale_one = field_ref[pl.ds(first + x * walkers + w, 1), :]
            scale_two = field_ref[pl.ds(first + (1 - x) * walkers + w, 1), :]
            scale_one = jnp.concatenate([scale_one] * copies, 1)
            scale_two = jnp.concatenate([scale_two] * copies, 1)
            block = time_root * (scale_one * one + scale_two * two)
            tiles[-1].append(block.astype(narrow))
    return tiles


def over_tiles(rows, order, body):
    high, across = 16, 256
    columns = order // across

    def tile(index, carry):
        row = pl.multiple_of((index // columns) * high, high)
        column = pl.multiple_of((index % columns) * across, across)
        body((pl.ds(row, high), pl.ds(column, across)))
        return carry

    lax.fori_loop(0, (rows // high) * columns, tile, 0)


def of_pair(ref, index):
    return lambda picked: ref[(index, *picked)]


def of_one(ref):
    return lambda picked: ref[picked]


def both_cores(field_ref, mine, mine_x, theirs, theirs_x):
    return [
        (field_ref, 0, of_one(mine), of_one(mine_x)),
        (field_ref, 1, of_one(theirs), of_one(theirs_x)),
    ]


def early_kernel(walkers, field_here, field_one, field_two, own, own_theirs, *refs):
    blocks, summed_ref = refs[:-1], refs[-1]
    _, _, x = place()
    sources = [
        (field_here, 0, of_pair(own, x), of_pair(own, 1 - x)),
        (field_here, 1, of_pair(own_theirs, x), of_pair(own_theirs, 1 - x)),
    ]
    sources += both_cores(field_one, *blocks[:4]) + both_cores(field_two, *blocks[4:])

    def body(picked):
        tiles = block_operators(x, walkers, sources, picked)
        for w in range(walkers):
            parts = [block[w].astype(wide) for block in tiles]
            summed_ref[(w, *picked)] = sum(parts[1:], parts[0])

    over_tiles(*summed_ref.shape[1:], body)


def early_operator(walkers, fields, own, own_theirs, blocks):
    rows, order = blocks[0].shape
    return pl.pallas_call(
        functools.partial(early_kernel, walkers),
        out_shape=jax.ShapeDtypeStruct((walkers, rows, order), wide),
        in_specs=[vmem_spec] * (5 + len(blocks)),
        out_specs=vmem_spec,
        compiler_params=large,
        name="early_operator",
    )(*fields, own, own_theirs, *blocks)


def late_kernel(summed_ref, field_ref, *refs):
    blocks, operator_ref = refs[:-1], refs[-1]
    walkers, rows, order = summed_ref.shape
    _, _, x = place()
    sources = both_cores(field_ref, *blocks)

    def body(picked):
        tiles = block_operators(x, walkers, sources, picked)
        row, column = picked
        for w in range(walkers):
            value = summed_ref[(w, *picked)]
            for block in tiles:
                value = value + block[w].astype(wide)
            top = value.astype(narrow)
            operator_ref[w, row, column] = top
            rest = (value - top.astype(wide)).astype(narrow)
            operator_ref[w, pl.ds(rows + row.start, row.size), column] = rest

    over_tiles(rows, order, body)


def split_operator(summed, field, blocks):
    walkers, rows, order = summed.shape
    return pl.pallas_call(
        late_kernel,
        out_shape=jax.ShapeDtypeStruct((walkers, 2 * rows, order), narrow),
        in_specs=[vmem_spec] * (2 + len(blocks)),
        out_specs=vmem_spec,
        compiler_params=large,
        name="split_operator",
    )(summed, field, *blocks)


def applied(operator_ref, vector_ref, step, mine, theirs):
    z, k, _ = place()
    _, rows, _ = mine.shape
    vector_ref[:, pl.ds(pl.multiple_of(k * rows, rows), rows), :] = mine[...]
    vector_ref[:, pl.ds(pl.multiple_of((1 - k) * rows, rows), rows), :] = theirs[...]
    start = pl.multiple_of(flipped(z, step) * 2 * rows, 2 * rows)

    def of_walker(w):
        both = jnp.dot(
            operator_ref[w, :, pl.ds(start, 2 * rows)],
            vector_ref[w],
            preferred_element_type=wide,
        )
        return both[:rows] + both[rows:]

    return of_walker


def near_kernel(operator_ref, *refs):
    pieces, (out_ref, vector_ref) = refs[:6], refs[6:]
    parts = [
        applied(operator_ref, vector_ref.at[step], step, pieces[step], pieces[3 + step])
        for step in range(3)
    ]
    for w in range(out_ref.shape[0]):
        out_ref[w] = parts[0](w) + parts[1](w) + parts[2](w)


def near_application(operator, pieces):
    walkers, rows, occupied = pieces[0].shape
    return pl.pallas_call(
        near_kernel,
        out_shape=jax.ShapeDtypeStruct((walkers, rows, occupied), wide),
        in_specs=[vmem_spec] * 7,
        out_specs=vmem_spec,
        scratch_shapes=[pltpu.VMEM((3, walkers, 2 * rows, occupied), narrow)],
        compiler_params=small,
        name="near_application",
    )(operator, *pieces)


def first_kernel(operator_ref, partial_ref, mine, theirs, first_ref, narrow_ref, vector_ref):
    part = applied(operator_ref, vector_ref, 3, mine, theirs)
    for w in range(first_ref.shape[0]):
        term = partial_ref[w] + part(w)
        first_ref[w] = term
        narrow_ref[w] = term.astype(narrow)


def first_application(operator, partial, mine, theirs):
    walkers, rows, occupied = mine.shape
    return pl.pallas_call(
        first_kernel,
        out_shape=[
            jax.ShapeDtypeStruct((walkers, rows, occupied), wide),
            jax.ShapeDtypeStruct((walkers, rows, occupied), narrow),
        ],
        in_specs=[vmem_spec] * 4,
        out_specs=[vmem_spec] * 2,
        scratch_shapes=[pltpu.VMEM((walkers, 2 * rows, occupied), narrow)],
        compiler_params=small,
        name="first_application",
    )(operator, partial, mine, theirs)


def base_kernel(operator_ref, first_ref, orbitals_ref, *refs):
    pieces, (out_ref, vector_ref) = refs[:6], refs[6:]
    parts = [
        applied(operator_ref, vector_ref.at[step], step, pieces[step], pieces[3 + step])
        for step in range(3)
    ]
    for w in range(first_ref.shape[0]):
        second = parts[0](w) + parts[1](w) + parts[2](w)
        out_ref[w] = orbitals_ref[0, :, w, :] + first_ref[w] + 0.5 * second


def base_application(operator, first_term, orbitals, pieces):
    walkers, rows, occupied = first_term.shape
    return pl.pallas_call(
        base_kernel,
        out_shape=jax.ShapeDtypeStruct(first_term.shape, wide),
        in_specs=[vmem_spec] * 9,
        out_specs=vmem_spec,
        scratch_shapes=[pltpu.VMEM((3, walkers, 2 * rows, occupied), narrow)],
        compiler_params=small,
        name="base_application",
    )(operator, first_term, orbitals, *pieces)


def second_kernel(operator_ref, base_ref, mine, theirs, out_ref, vector_ref):
    part = applied(operator_ref, vector_ref, 3, mine, theirs)
    for w in range(base_ref.shape[0]):
        out_ref[0, :, w, :] = base_ref[w] + 0.5 * part(w)


def second_application(operator, base, mine, theirs):
    walkers, rows, occupied = mine.shape
    return pl.pallas_call(
        second_kernel,
        out_shape=jax.ShapeDtypeStruct((1, rows, walkers, occupied), wide),
        in_specs=[vmem_spec] * 4,
        out_specs=vmem_spec,
        scratch_shapes=[pltpu.VMEM((walkers, 2 * rows, occupied), narrow)],
        compiler_params=small,
        name="second_application",
    )(operator, base, mine, theirs)


def to_chip(value, step):
    return lax.ppermute(value, "chol", [(i, i ^ (2 * step)) for i in range(8)])


def to_core(value):
    return lax.ppermute(value, "chol", [(i, i ^ 1) for i in range(8)])


def across(value):
    return lax.ppermute(value, "walk", [(0, 1), (1, 0)])


def row_device(green_blocks, half_chol, full_chol, meanfield, noise_draws, orbitals):
    walkers, rows, _ = green_blocks.shape
    vectors = half_chol.shape[0]

    green_two, green_one = to_chip(green_blocks, 2), to_chip(green_blocks, 1)
    half_theirs = to_core(half_chol)
    constants = jnp.concatenate([noise_draws.T.reshape(-1), jnp.repeat(meanfield, walkers)])
    constants = jnp.broadcast_to(constants[:, None], (2 * vectors * walkers, 128))
    constants_theirs = to_core(constants)

    green_three = to_chip(green_two, 1)

    cross, straight = {}, {}
    cross[2], straight[2] = cut(rows, full_chol, ((2, True, False), (2, False, False)))
    cross[3], straight[3], cross[1], straight[1], own, own_cross = cut(
        rows,
        after(full_chol, cross[2]),
        (
            (3, True, False),
            (3, False, False),
            (1, True, False),
            (1, False, False),
            (0, False, True),
            (0, True, True),
        ),
    )
    own_theirs = to_core(own_cross)

    green = (green_blocks, green_one, green_two, green_three)
    bias = chip_bias(green, half_chol, half_theirs)
    bias_shift, field = chip_field(bias, to_core(bias), constants, constants_theirs, walkers)
    field_one, field_two, field_three = (to_chip(field, step) for step in (1, 2, 3))

    cross_mine, mine, theirs, mine_x, theirs_x = {}, {}, {}, {}, {}
    cross_mine[2], mine[2] = to_chip(cross[2], 2), to_chip(straight[2], 2)
    cross_mine[3] = to_chip(cross[3], 3)
    theirs[2] = to_core(after(cross_mine[2], field))
    mine[3] = to_chip(after(straight[3], theirs[2]), 3)
    cross[1], straight[1] = after((cross[1], straight[1]), field_one)
    cross_mine[1], mine[1] = to_chip(cross[1], 1), to_chip(straight[1], 1)
    theirs_x[2] = across(after(theirs[2], field_one))
    mine_x[2] = across(mine[2])
    for step in (3, 1):
        theirs[step] = to_core(cross_mine[step])
        theirs_x[step], mine_x[step] = across(theirs[step]), across(mine[step])
    blocks = {step: (mine[step], mine_x[step], theirs[step], theirs_x[step]) for step in mine}

    start = after(walker_major(orbitals), theirs_x[2], theirs[3], field_two, field_three)
    start_two, start_one = to_chip(start, 2), to_chip(start, 1)
    hops = (mine_x[2], theirs_x[3], mine_x[1], theirs_x[1], mine[3])
    start_three = to_chip(after(start_two, *hops), 1)

    summed = early_operator(
        walkers,
        (field, field_one, field_two),
        own,
        own_theirs,
        (*blocks[1], *blocks[2]),
    )
    operator = split_operator(summed, field_three, blocks[3])

    near = [start, start_one, start_two]
    partial = near_application(operator, [*near, *[to_core(piece) for piece in near]])
    first_term, first_narrow = first_application(
        operator, partial, start_three, to_core(after(start_three, partial))
    )
    first_two, first_one = to_chip(first_narrow, 2), to_chip(first_narrow, 1)
    first_three = to_chip(first_two, 1)
    near = [first_narrow, first_one, first_two]
    base = base_application(
        operator, first_term, orbitals, [*near, *[to_core(piece) for piece in near]]
    )
    walkers_next = second_application(
        operator, base, first_three, to_core(after(first_three, base))
    )
    return (walkers_next, bias_shift)


def solution(mesh):
    placed = (
        P(("grp", "walk"), "chol", "orb"),
        P(("grp", "chol"), None, "orb"),
        P(("grp", "chol"), "orb", None),
        P(("grp", "chol")),
        P(("grp", "walk"), "chol"),
        P("orb", "chol", ("grp", "walk"), None),
    )
    sizes = mesh.shape
    if sizes["orb"] == 1 and sizes["walk"] == 2 and sizes["chol"] == 8:
        per_device = row_device
    else:
        per_device = general_device
    return jax.shard_map(
        per_device,
        mesh=mesh,
        in_specs=placed,
        out_specs=(P("orb", "chol", ("grp", "walk"), None), P(("grp", "walk"), "chol")),
        check_vma=False,
    )
```

```python
import functools

import jax
import jax.numpy as jnp
from jax import lax
from jax.experimental import pallas as pl
from jax.experimental.pallas import tpu as pltpu
from jax.sharding import PartitionSpec as P

time_root = 0.1


def general_device(green_blocks, half_chol, full_chol, meanfield, noise_draws, orbitals):
    walkers_here = green_blocks.shape[0]
    chol_here = half_chol.shape[0]
    half_rows = full_chol.shape[1]
    orbital_count = full_chol.shape[2]
    occupied = orbitals.shape[3]
    rows_here = orbitals.shape[1]
    partial_bias = jnp.einsum(
        "wki,cki->wc",
        lax.all_gather(green_blocks, "chol", axis=1, tiled=True),
        half_chol,
        preferred_element_type=jnp.float32,
    )
    force_bias = lax.psum(partial_bias, "orb")
    bias_shift = jnp.clip(time_root * (force_bias - meanfield[None, :]), -1.0, 1.0)
    shifted_field = noise_draws - bias_shift
    combined = jnp.zeros((walkers_here, half_rows, orbital_count), jnp.float32)
    for chol_index in range(chol_here):
        combined = combined + shifted_field[:, chol_index, None, None] * full_chol[chol_index][
            None
        ].astype(jnp.float32)
    operator_rows = (time_root * combined).astype(jnp.bfloat16)

    def apply_operator(vector):
        both_halves = lax.all_gather(vector, "orb", axis=0, tiled=True)
        running = jnp.zeros((walkers_here, half_rows, occupied), jnp.float32)
        shard_piece = lax.all_gather(both_halves, "chol", axis=1, tiled=True)
        row_count = shard_piece.shape[1]
        for half_index in range(shard_piece.shape[0]):
            col_block = lax.dynamic_slice_in_dim(
                operator_rows, half_index * half_rows, row_count, 2
            )
            running = running + lax.dot_general(
                col_block,
                shard_piece[half_index],
                (((2,), (0,)), ((0,), (1,))),
                preferred_element_type=jnp.float32,
            )
        summed = lax.psum(running, "chol")
        chol_slot = lax.axis_index("chol")
        owned_rows = lax.dynamic_slice_in_dim(summed, chol_slot * rows_here, rows_here, 1)
        return jnp.transpose(owned_rows, (1, 0, 2))[None]

    first_term = apply_operator(orbitals.astype(jnp.bfloat16))
    second_term = apply_operator(first_term.astype(jnp.bfloat16))
    walkers_next = orbitals + first_term + 0.5 * second_term
    return (walkers_next, bias_shift)


vmem_spec = pl.BlockSpec(memory_space=pltpu.VMEM)
hbm_spec = pl.BlockSpec(memory_space=pltpu.HBM)
wide = jnp.float32
narrow = jnp.bfloat16
small = pltpu.CompilerParams(vmem_limit_bytes=8 << 20)
large = pltpu.CompilerParams(vmem_limit_bytes=16 << 20)
brief = pl.CostEstimate(flops=0, bytes_accessed=0, transcendentals=0)


def after(value, *others):
    return lax.optimization_barrier((value, *others))[0]


def place():
    slot = lax.axis_index("chol")
    return slot // 2, slot % 2, lax.axis_index("walk")


def flipped(z, step):
    return lax.bitwise_xor(z, jnp.int32(step))


def cut_kernel(rows, wanted, full_ref, *refs):
    z, k, x = place()
    outs, sem = refs[:-1], refs[-1]
    copies = []
    for index, (step, crossed, both) in enumerate(wanted):
        core = 1 - k if crossed else k
        start = pl.multiple_of((2 * flipped(z, step) + core) * rows, rows)
        picked = pl.ds(start, rows)
        source = full_ref.at[:, picked, :] if both else full_ref.at[x, picked, :]
        copies.append(pltpu.make_async_copy(source, outs[index], sem.at[index]))
        copies[-1].start()
    for copy in copies:
        copy.wait()


def cut(rows, full_chol, wanted):
    order = full_chol.shape[2]
    shapes = [
        jax.ShapeDtypeStruct((2, rows, order) if both else (rows, order), narrow)
        for _, _, both in wanted
    ]
    return pl.pallas_call(
        functools.partial(cut_kernel, rows, wanted),
        out_shape=shapes,
        in_specs=[hbm_spec],
        out_specs=[vmem_spec] * len(wanted),
        scratch_shapes=[pltpu.SemaphoreType.DMA((len(wanted),))],
        compiler_params=small,
        cost_estimate=brief,
        name="cut_rows",
    )(full_chol)


def start_kernel(orbitals_ref, out_ref):
    for walker in range(out_ref.shape[0]):
        out_ref[walker] = orbitals_ref[0, :, walker, :].astype(narrow)


def walker_major(orbitals):
    _, rows, walkers, occupied = orbitals.shape
    return pl.pallas_call(
        start_kernel,
        out_shape=jax.ShapeDtypeStruct((walkers, rows, occupied), narrow),
        in_specs=[vmem_spec],
        out_specs=vmem_spec,
        compiler_params=small,
        cost_estimate=brief,
        name="walker_major",
    )(orbitals)


def bias_kernel(here_ref, one_ref, two_ref, three_ref, mine_ref, theirs_ref, out_ref):
    z, k, _ = place()
    walkers, rows, occupied = here_ref.shape
    vectors = mine_ref.shape[0]
    step_rows = 16
    totals = [jnp.zeros((8, 128), wide) for _ in range(2 * vectors * walkers)]
    for step, green in enumerate((here_ref, one_ref, two_ref, three_ref)):
        base = (2 * flipped(z, step) + k) * rows

        def add(index, totals, base=base, green=green):
            here = pl.multiple_of(index * step_rows, step_rows)
            there = pl.multiple_of(base + index * step_rows, step_rows)
            picked = pl.ds(here, step_rows)
            greens = [green[w, picked, :] for w in range(walkers)]
            greens = [g.astype(wide) for g in greens]
            totals = list(totals)
            for c in range(2 * vectors):
                chol_ref = mine_ref if c < vectors else theirs_ref
                chol = chol_ref[c % vectors, pl.ds(there, step_rows), :].astype(wide)
                for w in range(walkers):
                    product = greens[w] * chol
                    tiles = [
                        product[r : r + 8, n : n + 128]
                        for r in range(0, step_rows, 8)
                        for n in range(0, occupied, 128)
                    ]
                    totals[c * walkers + w] = totals[c * walkers + w] + sum(tiles[1:], tiles[0])
            return tuple(totals)

        totals = lax.fori_loop(0, rows // step_rows, add, tuple(totals))
    for index, total in enumerate(totals):
        value = jnp.sum(jnp.sum(total, axis=0, keepdims=True), axis=1, keepdims=True)
        out_ref[pl.ds(index, 1), :] = jnp.broadcast_to(value, (1, 128))


def chip_bias(green, mine, theirs):
    entries = 2 * mine.shape[0] * green[0].shape[0]
    return pl.pallas_call(
        bias_kernel,
        out_shape=jax.ShapeDtypeStruct((entries, 128), wide),
        in_specs=[vmem_spec] * 6,
        out_specs=vmem_spec,
        compiler_params=small,
        cost_estimate=brief,
        name="chip_bias",
    )(*green, mine, theirs)


def field_kernel(mine_ref, theirs_ref, noise_ref, noise_there_ref, shift_ref, field_ref):
    half = mine_ref.shape[0] // 2
    low, high = pl.ds(0, half), pl.ds(half, half)
    for rows, other, consts in ((low, high, noise_ref), (high, low, noise_there_ref)):
        force = mine_ref[rows, :] + theirs_ref[other, :]
        shift = jnp.clip(time_root * (force - consts[high, :]), -1.0, 1.0)
        field_ref[rows, :] = consts[low, :] - shift
        if rows is low:
            vectors, walkers = shift_ref.shape
            row = lax.broadcasted_iota(jnp.int32, (walkers, 128), 0)
            lane = lax.broadcasted_iota(jnp.int32, (walkers, 128), 1)
            for vector in range(vectors):
                part = shift[vector * walkers : (vector + 1) * walkers, :]
                picked = jnp.sum(jnp.where(row == lane, part, 0.0), axis=0, keepdims=True)
                shift_ref[vector : vector + 1, :] = picked[:, :walkers]


def chip_field(mine, theirs, noise, noise_there, walkers):
    entries = mine.shape[0]
    return pl.pallas_call(
        field_kernel,
        out_shape=[
            jax.ShapeDtypeStruct((entries // 2 // walkers, walkers), wide),
            jax.ShapeDtypeStruct((entries, 128), wide),
        ],
        in_specs=[vmem_spec] * 4,
        out_specs=[vmem_spec] * 2,
        compiler_params=small,
        cost_estimate=brief,
        name="chip_field",
    )(mine, theirs, noise, noise_there)


def block_operators(x, walkers, sources, picked):
    tiles = []
    for field_ref, crossed, near, other in sources:
        first = 2 * walkers * crossed
        one, two = near(picked).astype(wide), other(picked).astype(wide)
        copies = one.shape[1] // 128
        tiles.append([])
        for w in range(walkers):
            scale_one = field_ref[pl.ds(first + x * walkers + w, 1), :]
            scale_two = field_ref[pl.ds(first + (1 - x) * walkers + w, 1), :]
            scale_one = jnp.concatenate([scale_one] * copies, 1)
            scale_two = jnp.concatenate([scale_two] * copies, 1)
            block = time_root * (scale_one * one + scale_two * two)
            tiles[-1].append(block.astype(narrow))
    return tiles


def over_tiles(rows, order, body):
    high, across = 16, 256
    columns = order // across

    def tile(index, carry):
        row = pl.multiple_of((index // columns) * high, high)
        column = pl.multiple_of((index % columns) * across, across)
        body((pl.ds(row, high), pl.ds(column, across)))
        return carry

    lax.fori_loop(0, (rows // high) * columns, tile, 0)


def of_pair(ref, index):
    return lambda picked: ref[(index, *picked)]


def of_one(ref):
    return lambda picked: ref[picked]


def both_cores(field_ref, mine, mine_x, theirs, theirs_x):
    return [
        (field_ref, 0, of_one(mine), of_one(mine_x)),
        (field_ref, 1, of_one(theirs), of_one(theirs_x)),
    ]


def early_kernel(walkers, field_here, field_one, field_two, own, own_theirs, *refs):
    blocks, summed_ref = refs[:-1], refs[-1]
    _, _, x = place()
    sources = [
        (field_here, 0, of_pair(own, x), of_pair(own, 1 - x)),
        (field_here, 1, of_pair(own_theirs, x), of_pair(own_theirs, 1 - x)),
    ]
    sources += both_cores(field_one, *blocks[:4]) + both_cores(field_two, *blocks[4:])

    def body(picked):
        tiles = block_operators(x, walkers, sources, picked)
        for w in range(walkers):
            parts = [block[w].astype(wide) for block in tiles]
            summed_ref[(w, *picked)] = sum(parts[1:], parts[0])

    over_tiles(*summed_ref.shape[1:], body)


def early_operator(walkers, fields, own, own_theirs, blocks):
    rows, order = blocks[0].shape
    return pl.pallas_call(
        functools.partial(early_kernel, walkers),
        out_shape=jax.ShapeDtypeStruct((walkers, rows, order), wide),
        in_specs=[vmem_spec] * (5 + len(blocks)),
        out_specs=vmem_spec,
        compiler_params=large,
        cost_estimate=brief,
        name="early_operator",
    )(*fields, own, own_theirs, *blocks)


def late_kernel(summed_ref, field_ref, *refs):
    blocks, operator_ref = refs[:-1], refs[-1]
    walkers, rows, order = summed_ref.shape
    _, _, x = place()
    sources = both_cores(field_ref, *blocks)

    def body(picked):
        tiles = block_operators(x, walkers, sources, picked)
        row, column = picked
        for w in range(walkers):
            value = summed_ref[(w, *picked)]
            for block in tiles:
                value = value + block[w].astype(wide)
            top = value.astype(narrow)
            operator_ref[w, row, column] = top
            rest = (value - top.astype(wide)).astype(narrow)
            operator_ref[w, pl.ds(rows + row.start, row.size), column] = rest

    over_tiles(rows, order, body)


def split_operator(summed, field, blocks):
    walkers, rows, order = summed.shape
    return pl.pallas_call(
        late_kernel,
        out_shape=jax.ShapeDtypeStruct((walkers, 2 * rows, order), narrow),
        in_specs=[vmem_spec] * (2 + len(blocks)),
        out_specs=vmem_spec,
        compiler_params=large,
        cost_estimate=brief,
        name="split_operator",
    )(summed, field, *blocks)


def applied(operator_ref, vector_ref, step, mine, theirs):
    z, k, _ = place()
    _, rows, _ = mine.shape
    vector_ref[:, pl.ds(pl.multiple_of(k * rows, rows), rows), :] = mine[...]
    vector_ref[:, pl.ds(pl.multiple_of((1 - k) * rows, rows), rows), :] = theirs[...]
    start = pl.multiple_of(flipped(z, step) * 2 * rows, 2 * rows)

    def of_walker(w):
        both = jnp.dot(
            operator_ref[w, :, pl.ds(start, 2 * rows)],
            vector_ref[w],
            preferred_element_type=wide,
        )
        return both[:rows] + both[rows:]

    return of_walker


def near_kernel(operator_ref, *refs):
    pieces, (out_ref, vector_ref) = refs[:6], refs[6:]
    parts = [
        applied(operator_ref, vector_ref.at[step], step, pieces[step], pieces[3 + step])
        for step in range(3)
    ]
    for w in range(out_ref.shape[0]):
        out_ref[w] = parts[0](w) + parts[1](w) + parts[2](w)


def near_application(operator, pieces):
    walkers, rows, occupied = pieces[0].shape
    return pl.pallas_call(
        near_kernel,
        out_shape=jax.ShapeDtypeStruct((walkers, rows, occupied), wide),
        in_specs=[vmem_spec] * 7,
        out_specs=vmem_spec,
        scratch_shapes=[pltpu.VMEM((3, walkers, 2 * rows, occupied), narrow)],
        compiler_params=small,
        cost_estimate=brief,
        name="near_application",
    )(operator, *pieces)


def first_kernel(operator_ref, partial_ref, mine, theirs, first_ref, narrow_ref, vector_ref):
    part = applied(operator_ref, vector_ref, 3, mine, theirs)
    for w in range(first_ref.shape[0]):
        term = partial_ref[w] + part(w)
        first_ref[w] = term
        narrow_ref[w] = term.astype(narrow)


def first_application(operator, partial, mine, theirs):
    walkers, rows, occupied = mine.shape
    return pl.pallas_call(
        first_kernel,
        out_shape=[
            jax.ShapeDtypeStruct((walkers, rows, occupied), wide),
            jax.ShapeDtypeStruct((walkers, rows, occupied), narrow),
        ],
        in_specs=[vmem_spec] * 4,
        out_specs=[vmem_spec] * 2,
        scratch_shapes=[pltpu.VMEM((walkers, 2 * rows, occupied), narrow)],
        compiler_params=small,
        cost_estimate=brief,
        name="first_application",
    )(operator, partial, mine, theirs)


def base_kernel(operator_ref, first_ref, orbitals_ref, *refs):
    pieces, (out_ref, vector_ref) = refs[:6], refs[6:]
    parts = [
        applied(operator_ref, vector_ref.at[step], step, pieces[step], pieces[3 + step])
        for step in range(3)
    ]
    for w in range(first_ref.shape[0]):
        second = parts[0](w) + parts[1](w) + parts[2](w)
        out_ref[w] = orbitals_ref[0, :, w, :] + first_ref[w] + 0.5 * second


def base_application(operator, first_term, orbitals, pieces):
    walkers, rows, occupied = first_term.shape
    return pl.pallas_call(
        base_kernel,
        out_shape=jax.ShapeDtypeStruct(first_term.shape, wide),
        in_specs=[vmem_spec] * 9,
        out_specs=vmem_spec,
        scratch_shapes=[pltpu.VMEM((3, walkers, 2 * rows, occupied), narrow)],
        compiler_params=small,
        cost_estimate=brief,
        name="base_application",
    )(operator, first_term, orbitals, *pieces)


def second_kernel(operator_ref, base_ref, mine, theirs, out_ref, vector_ref):
    part = applied(operator_ref, vector_ref, 3, mine, theirs)
    for w in range(base_ref.shape[0]):
        out_ref[0, :, w, :] = base_ref[w] + 0.5 * part(w)


def second_application(operator, base, mine, theirs):
    walkers, rows, occupied = mine.shape
    return pl.pallas_call(
        second_kernel,
        out_shape=jax.ShapeDtypeStruct((1, rows, walkers, occupied), wide),
        in_specs=[vmem_spec] * 4,
        out_specs=vmem_spec,
        scratch_shapes=[pltpu.VMEM((walkers, 2 * rows, occupied), narrow)],
        compiler_params=small,
        cost_estimate=brief,
        name="second_application",
    )(operator, base, mine, theirs)


def to_chip(value, step):
    return lax.ppermute(value, "chol", [(i, i ^ (2 * step)) for i in range(8)])


def to_core(value):
    return lax.ppermute(value, "chol", [(i, i ^ 1) for i in range(8)])


def across(value):
    return lax.ppermute(value, "walk", [(0, 1), (1, 0)])


def row_device(green_blocks, half_chol, full_chol, meanfield, noise_draws, orbitals):
    walkers, rows, _ = green_blocks.shape
    vectors = half_chol.shape[0]

    green_two, green_one = to_chip(green_blocks, 2), to_chip(green_blocks, 1)
    half_theirs = to_core(half_chol)
    constants = jnp.concatenate([noise_draws.T.reshape(-1), jnp.repeat(meanfield, walkers)])
    constants = jnp.broadcast_to(constants[:, None], (2 * vectors * walkers, 128))
    constants_theirs = to_core(constants)

    green_three = to_chip(green_two, 1)

    cross, straight = {}, {}
    wanted = [(step, crossed, False) for step in (2, 3, 1) for crossed in (True, False)]
    wanted += [(0, False, True), (0, True, True)]
    pieces = cut(rows, after(full_chol, half_theirs), wanted)
    for index, step in enumerate((2, 3, 1)):
        cross[step], straight[step] = pieces[2 * index : 2 * index + 2]
    own, own_cross = pieces[6:]
    own_theirs = to_core(own_cross)

    green = (green_blocks, green_one, green_two, green_three)
    bias = chip_bias(green, half_chol, half_theirs)
    bias_shift, field = chip_field(bias, to_core(bias), constants, constants_theirs, walkers)
    field_one, field_two, field_three = (to_chip(field, step) for step in (1, 2, 3))

    cross_mine, mine, theirs, mine_x, theirs_x = {}, {}, {}, {}, {}
    cross_mine[2], mine[2] = to_chip(cross[2], 2), to_chip(straight[2], 2)
    cross_mine[3] = to_chip(cross[3], 3)
    theirs[2] = to_core(after(cross_mine[2], field, own_theirs))
    mine[3] = to_chip(after(straight[3], theirs[2]), 3)
    cross[1], straight[1] = after((cross[1], straight[1]), field_one)
    cross_mine[1], mine[1] = to_chip(cross[1], 1), to_chip(straight[1], 1)
    theirs_x[2] = across(after(theirs[2], field_one))
    mine_x[2] = across(mine[2])
    for step in (3, 1):
        theirs[step] = to_core(cross_mine[step])
        theirs_x[step], mine_x[step] = across(theirs[step]), across(mine[step])
    blocks = {step: (mine[step], mine_x[step], theirs[step], theirs_x[step]) for step in mine}

    start = after(walker_major(orbitals), theirs_x[2], theirs[3], field_two, field_three)
    start_two, start_one = to_chip(start, 2), to_chip(start, 1)
    hops = (mine_x[2], theirs_x[3], mine_x[1], theirs_x[1], mine[3])
    start_three = to_chip(after(start_two, *hops), 1)

    summed = early_operator(
        walkers,
        (field, field_one, field_two),
        own,
        own_theirs,
        (*blocks[1], *blocks[2]),
    )
    operator = split_operator(summed, field_three, blocks[3])

    near = [start, start_one, start_two]
    partial = near_application(operator, [*near, *[to_core(piece) for piece in near]])
    first_term, first_narrow = first_application(
        operator, partial, start_three, to_core(after(start_three, partial))
    )
    first_two, first_one = to_chip(first_narrow, 2), to_chip(first_narrow, 1)
    first_three = to_chip(first_two, 1)
    near = [first_narrow, first_one, first_two]
    base = base_application(
        operator, first_term, orbitals, [*near, *[to_core(piece) for piece in near]]
    )
    walkers_next = second_application(
        operator, base, first_three, to_core(after(first_three, base))
    )
    return (walkers_next, bias_shift.T)


def solution(mesh):
    placed = (
        P(("grp", "walk"), "chol", "orb"),
        P(("grp", "chol"), None, "orb"),
        P(("grp", "chol"), "orb", None),
        P(("grp", "chol")),
        P(("grp", "walk"), "chol"),
        P("orb", "chol", ("grp", "walk"), None),
    )
    sizes = mesh.shape
    if sizes["orb"] == 1 and sizes["walk"] == 2 and sizes["chol"] == 8:
        per_device = row_device
    else:
        per_device = general_device
    return jax.shard_map(
        per_device,
        mesh=mesh,
        in_specs=placed,
        out_specs=(P("orb", "chol", ("grp", "walk"), None), P(("grp", "walk"), "chol")),
        check_vma=False,
    )
```

```python
import functools

import jax
import jax.numpy as jnp
from jax import lax
from jax.experimental import pallas as pl
from jax.experimental.pallas import tpu as pltpu
from jax.sharding import PartitionSpec as P

time_root = 0.1


def general_device(green_blocks, half_chol, full_chol, meanfield, noise_draws, orbitals):
    walkers_here = green_blocks.shape[0]
    chol_here = half_chol.shape[0]
    half_rows = full_chol.shape[1]
    orbital_count = full_chol.shape[2]
    occupied = orbitals.shape[3]
    rows_here = orbitals.shape[1]
    partial_bias = jnp.einsum(
        "wki,cki->wc",
        lax.all_gather(green_blocks, "chol", axis=1, tiled=True),
        half_chol,
        preferred_element_type=jnp.float32,
    )
    force_bias = lax.psum(partial_bias, "orb")
    bias_shift = jnp.clip(time_root * (force_bias - meanfield[None, :]), -1.0, 1.0)
    shifted_field = noise_draws - bias_shift
    combined = jnp.zeros((walkers_here, half_rows, orbital_count), jnp.float32)
    for chol_index in range(chol_here):
        combined = combined + shifted_field[:, chol_index, None, None] * full_chol[chol_index][
            None
        ].astype(jnp.float32)
    operator_rows = (time_root * combined).astype(jnp.bfloat16)

    def apply_operator(vector):
        both_halves = lax.all_gather(vector, "orb", axis=0, tiled=True)
        running = jnp.zeros((walkers_here, half_rows, occupied), jnp.float32)
        shard_piece = lax.all_gather(both_halves, "chol", axis=1, tiled=True)
        row_count = shard_piece.shape[1]
        for half_index in range(shard_piece.shape[0]):
            col_block = lax.dynamic_slice_in_dim(
                operator_rows, half_index * half_rows, row_count, 2
            )
            running = running + lax.dot_general(
                col_block,
                shard_piece[half_index],
                (((2,), (0,)), ((0,), (1,))),
                preferred_element_type=jnp.float32,
            )
        summed = lax.psum(running, "chol")
        chol_slot = lax.axis_index("chol")
        owned_rows = lax.dynamic_slice_in_dim(summed, chol_slot * rows_here, rows_here, 1)
        return jnp.transpose(owned_rows, (1, 0, 2))[None]

    first_term = apply_operator(orbitals.astype(jnp.bfloat16))
    second_term = apply_operator(first_term.astype(jnp.bfloat16))
    walkers_next = orbitals + first_term + 0.5 * second_term
    return (walkers_next, bias_shift)


vmem_spec = pl.BlockSpec(memory_space=pltpu.VMEM)
hbm_spec = pl.BlockSpec(memory_space=pltpu.HBM)
wide = jnp.float32
narrow = jnp.bfloat16
small = pltpu.CompilerParams(vmem_limit_bytes=8 << 20)
large = pltpu.CompilerParams(vmem_limit_bytes=16 << 20)


def after(value, *others):
    return lax.optimization_barrier((value, *others))[0]


def place():
    slot = lax.axis_index("chol")
    return slot // 2, slot % 2, lax.axis_index("walk")


def flipped(z, step):
    return lax.bitwise_xor(z, jnp.int32(step))


def pack_kernel(full_ref, green_ref, one_ref, two_ref, three_ref, own_ref, cross_ref, sem):
    z, k, x = place()
    walkers, rows, occupied = green_ref.shape
    copies = []

    def copy(source, target):
        copies.append(pltpu.make_async_copy(source, target, sem.at[len(copies)]))
        copies[-1].start()

    def of_chip(step, core):
        return pl.ds(pl.multiple_of((2 * flipped(z, step) + core) * rows, rows), rows)

    for step, message, top in ((2, two_ref, rows), (1, one_ref, rows), (3, three_ref, 0)):
        for index, core in enumerate((1 - k, k)):
            copy(
                full_ref.at[x, of_chip(step, core), :],
                message.at[pl.ds(top + index * rows, rows), :],
            )
    copy(full_ref.at[:, of_chip(0, k), :], own_ref)
    copy(full_ref.at[:, of_chip(0, 1 - k), :], cross_ref)
    for each in copies:
        each.wait()
    for message in (two_ref, one_ref):
        for w in range(walkers):
            message[:rows, w * occupied : (w + 1) * occupied] = green_ref[w]


def packed(full_chol, green_blocks):
    order = full_chol.shape[2]
    rows = green_blocks.shape[1]
    shapes = [(3 * rows, order), (3 * rows, order), (2 * rows, order)] + [(2, rows, order)] * 2
    return pl.pallas_call(
        pack_kernel,
        out_shape=[jax.ShapeDtypeStruct(shape, narrow) for shape in shapes],
        in_specs=[hbm_spec, vmem_spec],
        out_specs=[vmem_spec] * 5,
        scratch_shapes=[pltpu.SemaphoreType.DMA((8,))],
        compiler_params=small,
        name="packed",
    )(full_chol, green_blocks)


def start_kernel(orbitals_ref, out_ref):
    for walker in range(out_ref.shape[0]):
        out_ref[walker] = orbitals_ref[0, :, walker, :].astype(narrow)


def walker_major(orbitals):
    _, rows, walkers, occupied = orbitals.shape
    return pl.pallas_call(
        start_kernel,
        out_shape=jax.ShapeDtypeStruct((walkers, rows, occupied), narrow),
        in_specs=[vmem_spec],
        out_specs=vmem_spec,
        compiler_params=small,
        name="walker_major",
    )(orbitals)


def bias_kernel(here_ref, one_ref, two_ref, three_ref, mine_ref, theirs_ref, out_ref):
    z, k, _ = place()
    walkers, rows, occupied = here_ref.shape
    vectors = mine_ref.shape[0]
    step_rows = 16
    totals = [jnp.zeros((8, 128), wide) for _ in range(2 * vectors * walkers)]
    for step, green in enumerate((here_ref, one_ref, two_ref, three_ref)):
        base = (2 * flipped(z, step) + k) * rows

        def add(index, totals, step=step, base=base, green=green):
            here = pl.multiple_of(index * step_rows, step_rows)
            there = pl.multiple_of(base + index * step_rows, step_rows)
            picked = pl.ds(here, step_rows)
            if step == 0:
                greens = [green[w, picked, :] for w in range(walkers)]
            else:
                greens = [green[picked, w * occupied : (w + 1) * occupied] for w in range(walkers)]
            greens = [g.astype(wide) for g in greens]
            totals = list(totals)
            for c in range(2 * vectors):
                chol_ref = mine_ref if c < vectors else theirs_ref
                chol = chol_ref[c % vectors, pl.ds(there, step_rows), :].astype(wide)
                for w in range(walkers):
                    product = greens[w] * chol
                    tiles = [
                        product[r : r + 8, n : n + 128]
                        for r in range(0, step_rows, 8)
                        for n in range(0, occupied, 128)
                    ]
                    totals[c * walkers + w] = totals[c * walkers + w] + sum(tiles[1:], tiles[0])
            return tuple(totals)

        totals = lax.fori_loop(0, rows // step_rows, add, tuple(totals))
    for index, total in enumerate(totals):
        value = jnp.sum(jnp.sum(total, axis=0, keepdims=True), axis=1, keepdims=True)
        out_ref[pl.ds(index, 1), :] = jnp.broadcast_to(value, (1, 128))


def chip_bias(green, mine, theirs):
    entries = 2 * mine.shape[0] * green[0].shape[0]
    return pl.pallas_call(
        bias_kernel,
        out_shape=jax.ShapeDtypeStruct((entries, 128), wide),
        in_specs=[vmem_spec] * 6,
        out_specs=vmem_spec,
        compiler_params=small,
        name="chip_bias",
    )(*green, mine, theirs)


def field_kernel(mine_ref, theirs_ref, noise_ref, noise_there_ref, shift_ref, field_ref):
    half = mine_ref.shape[0] // 2
    low, high = pl.ds(0, half), pl.ds(half, half)
    for rows, other, consts in ((low, high, noise_ref), (high, low, noise_there_ref)):
        force = mine_ref[rows, :] + theirs_ref[other, :]
        shift = jnp.clip(time_root * (force - consts[high, :]), -1.0, 1.0)
        field_ref[rows, :] = consts[low, :] - shift
        if rows is low:
            vectors, walkers = shift_ref.shape
            row = lax.broadcasted_iota(jnp.int32, (walkers, 128), 0)
            lane = lax.broadcasted_iota(jnp.int32, (walkers, 128), 1)
            for vector in range(vectors):
                part = shift[vector * walkers : (vector + 1) * walkers, :]
                picked = jnp.sum(jnp.where(row == lane, part, 0.0), axis=0, keepdims=True)
                shift_ref[vector : vector + 1, :] = picked[:, :walkers]


def chip_field(mine, theirs, noise, noise_there, vectors):
    entries = mine.shape[0]
    return pl.pallas_call(
        field_kernel,
        out_shape=[
            jax.ShapeDtypeStruct((vectors, entries // 2 // vectors), wide),
            jax.ShapeDtypeStruct((entries, 128), wide),
        ],
        in_specs=[vmem_spec] * 4,
        out_specs=[vmem_spec] * 2,
        compiler_params=small,
        name="chip_field",
    )(mine, theirs, noise, noise_there)


def block_operators(x, walkers, sources, picked):
    tiles = []
    for field_ref, crossed, near, other in sources:
        first = 2 * walkers * crossed
        one, two = near(picked).astype(wide), other(picked).astype(wide)
        copies = one.shape[1] // 128
        tiles.append([])
        for w in range(walkers):
            scale_one = field_ref[pl.ds(first + x * walkers + w, 1), :]
            scale_two = field_ref[pl.ds(first + (1 - x) * walkers + w, 1), :]
            scale_one = jnp.concatenate([scale_one] * copies, 1)
            scale_two = jnp.concatenate([scale_two] * copies, 1)
            block = time_root * (scale_one * one + scale_two * two)
            tiles[-1].append(block.astype(narrow))
    return tiles


def over_tiles(rows, order, body):
    high, across = 16, 256
    columns = order // across

    def tile(index, carry):
        row = pl.multiple_of((index // columns) * high, high)
        column = pl.multiple_of((index % columns) * across, across)
        body((pl.ds(row, high), pl.ds(column, across)))
        return carry

    lax.fori_loop(0, (rows // high) * columns, tile, 0)


def of_pair(ref, index):
    return lambda picked: ref[(index, *picked)]


def below(ref, top):
    return lambda picked: ref[pl.ds(top + picked[0].start, picked[0].size), picked[1]]


def both_cores(field_ref, rows, mine, mine_x, theirs, theirs_x):
    top = mine.shape[0] - 2 * rows
    return [
        (field_ref, 0, below(mine, top + rows), below(mine_x, rows)),
        (field_ref, 1, below(theirs, top), below(theirs_x, 0)),
    ]


def early_kernel(walkers, field_here, field_one, field_two, own, own_theirs, *refs):
    blocks, summed_ref = refs[:-1], refs[-1]
    _, _, x = place()
    sources = [
        (field_here, 0, of_pair(own, x), of_pair(own, 1 - x)),
        (field_here, 1, of_pair(own_theirs, x), of_pair(own_theirs, 1 - x)),
    ]
    rows = own.shape[1]
    sources += both_cores(field_one, rows, *blocks[:4])
    sources += both_cores(field_two, rows, *blocks[4:])

    def body(picked):
        tiles = block_operators(x, walkers, sources, picked)
        for w in range(walkers):
            parts = [block[w].astype(wide) for block in tiles]
            summed_ref[(w, *picked)] = sum(parts[1:], parts[0])

    over_tiles(*summed_ref.shape[1:], body)


def early_operator(walkers, fields, own, own_theirs, blocks):
    _, rows, order = own.shape
    return pl.pallas_call(
        functools.partial(early_kernel, walkers),
        out_shape=jax.ShapeDtypeStruct((walkers, rows, order), wide),
        in_specs=[vmem_spec] * (5 + len(blocks)),
        out_specs=vmem_spec,
        compiler_params=large,
        name="early_operator",
    )(*fields, own, own_theirs, *blocks)


def late_kernel(summed_ref, field_ref, *refs):
    blocks, operator_ref = refs[:-1], refs[-1]
    walkers, rows, order = summed_ref.shape
    _, _, x = place()
    sources = both_cores(field_ref, rows, *blocks)

    def body(picked):
        tiles = block_operators(x, walkers, sources, picked)
        row, column = picked
        for w in range(walkers):
            value = summed_ref[(w, *picked)]
            for block in tiles:
                value = value + block[w].astype(wide)
            top = value.astype(narrow)
            operator_ref[w, row, column] = top
            rest = (value - top.astype(wide)).astype(narrow)
            operator_ref[w, pl.ds(rows + row.start, row.size), column] = rest

    over_tiles(rows, order, body)


def split_operator(summed, field, blocks):
    walkers, rows, order = summed.shape
    return pl.pallas_call(
        late_kernel,
        out_shape=jax.ShapeDtypeStruct((walkers, 2 * rows, order), narrow),
        in_specs=[vmem_spec] * (2 + len(blocks)),
        out_specs=vmem_spec,
        compiler_params=large,
        name="split_operator",
    )(summed, field, *blocks)


def applied(operator_ref, vector_ref, step, mine, theirs):
    z, k, _ = place()
    _, rows, _ = mine.shape
    vector_ref[:, pl.ds(pl.multiple_of(k * rows, rows), rows), :] = mine[...]
    vector_ref[:, pl.ds(pl.multiple_of((1 - k) * rows, rows), rows), :] = theirs[...]
    start = pl.multiple_of(flipped(z, step) * 2 * rows, 2 * rows)

    def of_walker(w):
        both = jnp.dot(
            operator_ref[w, :, pl.ds(start, 2 * rows)],
            vector_ref[w],
            preferred_element_type=wide,
        )
        return both[:rows] + both[rows:]

    return of_walker


def near_kernel(operator_ref, *refs):
    pieces, (out_ref, vector_ref) = refs[:6], refs[6:]
    parts = [
        applied(operator_ref, vector_ref.at[step], step, pieces[step], pieces[3 + step])
        for step in range(3)
    ]
    for w in range(out_ref.shape[0]):
        out_ref[w] = parts[0](w) + parts[1](w) + parts[2](w)


def near_application(operator, pieces):
    walkers, rows, occupied = pieces[0].shape
    return pl.pallas_call(
        near_kernel,
        out_shape=jax.ShapeDtypeStruct((walkers, rows, occupied), wide),
        in_specs=[vmem_spec] * 7,
        out_specs=vmem_spec,
        scratch_shapes=[pltpu.VMEM((3, walkers, 2 * rows, occupied), narrow)],
        compiler_params=small,
        name="near_application",
    )(operator, *pieces)


def first_kernel(operator_ref, partial_ref, mine, theirs, first_ref, narrow_ref, vector_ref):
    part = applied(operator_ref, vector_ref, 3, mine, theirs)
    for w in range(first_ref.shape[0]):
        term = partial_ref[w] + part(w)
        first_ref[w] = term
        narrow_ref[w] = term.astype(narrow)


def first_application(operator, partial, mine, theirs):
    walkers, rows, occupied = mine.shape
    return pl.pallas_call(
        first_kernel,
        out_shape=[
            jax.ShapeDtypeStruct((walkers, rows, occupied), wide),
            jax.ShapeDtypeStruct((walkers, rows, occupied), narrow),
        ],
        in_specs=[vmem_spec] * 4,
        out_specs=[vmem_spec] * 2,
        scratch_shapes=[pltpu.VMEM((walkers, 2 * rows, occupied), narrow)],
        compiler_params=small,
        name="first_application",
    )(operator, partial, mine, theirs)


def base_kernel(operator_ref, first_ref, orbitals_ref, *refs):
    pieces, (out_ref, vector_ref) = refs[:6], refs[6:]
    parts = [
        applied(operator_ref, vector_ref.at[step], step, pieces[step], pieces[3 + step])
        for step in range(3)
    ]
    for w in range(first_ref.shape[0]):
        second = parts[0](w) + parts[1](w) + parts[2](w)
        out_ref[w] = orbitals_ref[0, :, w, :] + first_ref[w] + 0.5 * second


def base_application(operator, first_term, orbitals, pieces):
    walkers, rows, occupied = first_term.shape
    return pl.pallas_call(
        base_kernel,
        out_shape=jax.ShapeDtypeStruct(first_term.shape, wide),
        in_specs=[vmem_spec] * 9,
        out_specs=vmem_spec,
        scratch_shapes=[pltpu.VMEM((3, walkers, 2 * rows, occupied), narrow)],
        compiler_params=small,
        name="base_application",
    )(operator, first_term, orbitals, *pieces)


def second_kernel(operator_ref, base_ref, mine, theirs, out_ref, vector_ref):
    part = applied(operator_ref, vector_ref, 3, mine, theirs)
    for w in range(base_ref.shape[0]):
        out_ref[0, :, w, :] = base_ref[w] + 0.5 * part(w)


def second_application(operator, base, mine, theirs):
    walkers, rows, occupied = mine.shape
    return pl.pallas_call(
        second_kernel,
        out_shape=jax.ShapeDtypeStruct((1, rows, walkers, occupied), wide),
        in_specs=[vmem_spec] * 4,
        out_specs=vmem_spec,
        scratch_shapes=[pltpu.VMEM((walkers, 2 * rows, occupied), narrow)],
        compiler_params=small,
        name="second_application",
    )(operator, base, mine, theirs)


def to_chip(value, step):
    return lax.ppermute(value, "chol", [(i, i ^ (2 * step)) for i in range(8)])


def to_core(value):
    return lax.ppermute(value, "chol", [(i, i ^ 1) for i in range(8)])


def across(value):
    return lax.ppermute(value, "walk", [(0, 1), (1, 0)])


def row_device(green_blocks, half_chol, full_chol, meanfield, noise_draws, orbitals):
    walkers, rows, _ = green_blocks.shape
    vectors = half_chol.shape[0]

    half_theirs = to_core(half_chol)
    constants = jnp.concatenate([noise_draws.T.reshape(-1), jnp.repeat(meanfield, walkers)])
    constants = jnp.broadcast_to(constants[:, None], (2 * vectors * walkers, 128))
    constants_theirs = to_core(constants)
    one, two, three, own, own_cross = packed(full_chol, green_blocks)
    two, one = to_chip(two, 2), to_chip(one, 1)
    own_theirs = to_core(own_cross)
    three = to_chip(after(three, one, half_theirs, own_theirs, constants_theirs), 3)
    green_three = to_chip(two[:rows], 1)

    one_x = across(one[rows:])
    two_x = across(after(two[rows:], one_x))
    three_x = across(after(three, two_x))
    messages = {1: (one, one_x), 2: (two, two_x), 3: (three, three_x)}
    blocks = {step: [*both, *[to_core(each) for each in both]] for step, both in messages.items()}

    bias = chip_bias((green_blocks, one, two, green_three), half_chol, half_theirs)
    bias_shift, field = chip_field(bias, to_core(bias), constants, constants_theirs, vectors)
    field_one, field_two, field_three = (to_chip(field, step) for step in (1, 2, 3))

    start = after(walker_major(orbitals), two)
    start_two, start_one = to_chip(start, 2), to_chip(start, 1)
    start_three = to_chip(start_two, 1)

    summed = early_operator(
        walkers,
        (field, field_one, field_two),
        own,
        own_theirs,
        (*blocks[1], *blocks[2]),
    )
    operator = split_operator(summed, field_three, blocks[3])

    near = [start, start_one, start_two]
    partial = near_application(operator, [*near, *[to_core(piece) for piece in near]])
    first_term, first_narrow = first_application(
        operator, partial, start_three, to_core(after(start_three, partial))
    )
    first_two, first_one = to_chip(first_narrow, 2), to_chip(first_narrow, 1)
    first_three = to_chip(first_two, 1)
    near = [first_narrow, first_one, first_two]
    base = base_application(
        operator, first_term, orbitals, [*near, *[to_core(piece) for piece in near]]
    )
    walkers_next = second_application(
        operator, base, first_three, to_core(after(first_three, base))
    )
    return (walkers_next, bias_shift.T)


def solution(mesh):
    placed = (
        P(("grp", "walk"), "chol", "orb"),
        P(("grp", "chol"), None, "orb"),
        P(("grp", "chol"), "orb", None),
        P(("grp", "chol")),
        P(("grp", "walk"), "chol"),
        P("orb", "chol", ("grp", "walk"), None),
    )
    sizes = mesh.shape
    if sizes["orb"] == 1 and sizes["walk"] == 2 and sizes["chol"] == 8:
        per_device = row_device
    else:
        per_device = general_device
    return jax.shard_map(
        per_device,
        mesh=mesh,
        in_specs=placed,
        out_specs=(P("orb", "chol", ("grp", "walk"), None), P(("grp", "walk"), "chol")),
        check_vma=False,
    )
```

```python
import functools

import jax
import jax.numpy as jnp
from jax import lax
from jax.experimental import pallas as pl
from jax.experimental.pallas import tpu as pltpu
from jax.sharding import PartitionSpec as P

time_root = 0.1


def general_device(green_blocks, half_chol, full_chol, meanfield, noise_draws, orbitals):
    walkers_here = green_blocks.shape[0]
    chol_here = half_chol.shape[0]
    half_rows = full_chol.shape[1]
    orbital_count = full_chol.shape[2]
    occupied = orbitals.shape[3]
    rows_here = orbitals.shape[1]
    partial_bias = jnp.einsum(
        "wki,cki->wc",
        lax.all_gather(green_blocks, "chol", axis=1, tiled=True),
        half_chol,
        preferred_element_type=jnp.float32,
    )
    force_bias = lax.psum(partial_bias, "orb")
    bias_shift = jnp.clip(time_root * (force_bias - meanfield[None, :]), -1.0, 1.0)
    shifted_field = noise_draws - bias_shift
    combined = jnp.zeros((walkers_here, half_rows, orbital_count), jnp.float32)
    for chol_index in range(chol_here):
        combined = combined + shifted_field[:, chol_index, None, None] * full_chol[chol_index][
            None
        ].astype(jnp.float32)
    operator_rows = (time_root * combined).astype(jnp.bfloat16)

    def apply_operator(vector):
        both_halves = lax.all_gather(vector, "orb", axis=0, tiled=True)
        running = jnp.zeros((walkers_here, half_rows, occupied), jnp.float32)
        shard_piece = lax.all_gather(both_halves, "chol", axis=1, tiled=True)
        row_count = shard_piece.shape[1]
        for half_index in range(shard_piece.shape[0]):
            col_block = lax.dynamic_slice_in_dim(
                operator_rows, half_index * half_rows, row_count, 2
            )
            running = running + lax.dot_general(
                col_block,
                shard_piece[half_index],
                (((2,), (0,)), ((0,), (1,))),
                preferred_element_type=jnp.float32,
            )
        summed = lax.psum(running, "chol")
        chol_slot = lax.axis_index("chol")
        owned_rows = lax.dynamic_slice_in_dim(summed, chol_slot * rows_here, rows_here, 1)
        return jnp.transpose(owned_rows, (1, 0, 2))[None]

    first_term = apply_operator(orbitals.astype(jnp.bfloat16))
    second_term = apply_operator(first_term.astype(jnp.bfloat16))
    walkers_next = orbitals + first_term + 0.5 * second_term
    return (walkers_next, bias_shift)


vmem_spec = pl.BlockSpec(memory_space=pltpu.VMEM)
hbm_spec = pl.BlockSpec(memory_space=pltpu.HBM)
wide = jnp.float32
narrow = jnp.bfloat16
small = pltpu.CompilerParams(vmem_limit_bytes=8 << 20)
large = pltpu.CompilerParams(vmem_limit_bytes=16 << 20)


def after(value, *others):
    return lax.optimization_barrier((value, *others))[0]


def place():
    slot = lax.axis_index("chol")
    return slot // 2, slot % 2, lax.axis_index("walk")


def flipped(z, step):
    return lax.bitwise_xor(z, jnp.int32(step))


def pack_kernel(full_ref, green_ref, one_ref, two_ref, three_ref, own_ref, cross_ref, sem):
    z, k, x = place()
    walkers, rows, occupied = green_ref.shape
    copies = []

    def copy(source, target):
        copies.append(pltpu.make_async_copy(source, target, sem.at[len(copies)]))
        copies[-1].start()

    def of_chip(step, core):
        return pl.ds(pl.multiple_of((2 * flipped(z, step) + core) * rows, rows), rows)

    for step, message, top in ((2, two_ref, rows), (1, one_ref, rows), (3, three_ref, 0)):
        for index, core in enumerate((1 - k, k)):
            copy(
                full_ref.at[x, of_chip(step, core), :],
                message.at[pl.ds(top + index * rows, rows), :],
            )
    copy(full_ref.at[:, of_chip(0, k), :], own_ref)
    copy(full_ref.at[:, of_chip(0, 1 - k), :], cross_ref)
    for each in copies:
        each.wait()
    for message in (two_ref, one_ref):
        for w in range(walkers):
            message[:rows, w * occupied : (w + 1) * occupied] = green_ref[w]


def packed(full_chol, green_blocks):
    order = full_chol.shape[2]
    rows = green_blocks.shape[1]
    shapes = [(3 * rows, order), (3 * rows, order), (2 * rows, order)] + [(2, rows, order)] * 2
    return pl.pallas_call(
        pack_kernel,
        out_shape=[jax.ShapeDtypeStruct(shape, narrow) for shape in shapes],
        in_specs=[hbm_spec, vmem_spec],
        out_specs=[vmem_spec] * 5,
        scratch_shapes=[pltpu.SemaphoreType.DMA((8,))],
        name="packed",
    )(full_chol, green_blocks)


def start_kernel(orbitals_ref, out_ref):
    for walker in range(out_ref.shape[0]):
        out_ref[walker] = orbitals_ref[0, :, walker, :].astype(narrow)


def walker_major(orbitals):
    _, rows, walkers, occupied = orbitals.shape
    return pl.pallas_call(
        start_kernel,
        out_shape=jax.ShapeDtypeStruct((walkers, rows, occupied), narrow),
        in_specs=[vmem_spec],
        out_specs=vmem_spec,
        compiler_params=small,
        name="walker_major",
    )(orbitals)


def bias_kernel(here_ref, one_ref, two_ref, three_ref, mine_ref, theirs_ref, out_ref):
    z, k, _ = place()
    walkers, rows, occupied = here_ref.shape
    vectors = mine_ref.shape[0]
    step_rows = 16
    totals = [jnp.zeros((8, 128), wide) for _ in range(2 * vectors * walkers)]
    for step, green in enumerate((here_ref, one_ref, two_ref, three_ref)):
        base = (2 * flipped(z, step) + k) * rows

        def add(index, totals, step=step, base=base, green=green):
            here = pl.multiple_of(index * step_rows, step_rows)
            there = pl.multiple_of(base + index * step_rows, step_rows)
            picked = pl.ds(here, step_rows)
            if step == 0:
                greens = [green[w, picked, :] for w in range(walkers)]
            else:
                greens = [green[picked, w * occupied : (w + 1) * occupied] for w in range(walkers)]
            greens = [g.astype(wide) for g in greens]
            totals = list(totals)
            for c in range(2 * vectors):
                chol_ref = mine_ref if c < vectors else theirs_ref
                chol = chol_ref[c % vectors, pl.ds(there, step_rows), :].astype(wide)
                for w in range(walkers):
                    product = greens[w] * chol
                    tiles = [
                        product[r : r + 8, n : n + 128]
                        for r in range(0, step_rows, 8)
                        for n in range(0, occupied, 128)
                    ]
                    totals[c * walkers + w] = totals[c * walkers + w] + sum(tiles[1:], tiles[0])
            return tuple(totals)

        totals = lax.fori_loop(0, rows // step_rows, add, tuple(totals))
    for index, total in enumerate(totals):
        value = jnp.sum(jnp.sum(total, axis=0, keepdims=True), axis=1, keepdims=True)
        out_ref[pl.ds(index, 1), :] = jnp.broadcast_to(value, (1, 128))


def chip_bias(green, mine, theirs):
    entries = 2 * mine.shape[0] * green[0].shape[0]
    return pl.pallas_call(
        bias_kernel,
        out_shape=jax.ShapeDtypeStruct((entries, 128), wide),
        in_specs=[vmem_spec] * 6,
        out_specs=vmem_spec,
        compiler_params=small,
        name="chip_bias",
    )(*green, mine, theirs)


def field_kernel(mine_ref, theirs_ref, noise_ref, noise_there_ref, shift_ref, field_ref):
    half = mine_ref.shape[0] // 2
    low, high = pl.ds(0, half), pl.ds(half, half)
    for rows, other, consts in ((low, high, noise_ref), (high, low, noise_there_ref)):
        force = mine_ref[rows, :] + theirs_ref[other, :]
        shift = jnp.clip(time_root * (force - consts[high, :]), -1.0, 1.0)
        field_ref[rows, :] = consts[low, :] - shift
        if rows is low:
            vectors, walkers = shift_ref.shape
            row = lax.broadcasted_iota(jnp.int32, (walkers, 128), 0)
            lane = lax.broadcasted_iota(jnp.int32, (walkers, 128), 1)
            for vector in range(vectors):
                part = shift[vector * walkers : (vector + 1) * walkers, :]
                picked = jnp.sum(jnp.where(row == lane, part, 0.0), axis=0, keepdims=True)
                shift_ref[vector : vector + 1, :] = picked[:, :walkers]


def chip_field(mine, theirs, noise, noise_there, vectors):
    entries = mine.shape[0]
    return pl.pallas_call(
        field_kernel,
        out_shape=[
            jax.ShapeDtypeStruct((vectors, entries // 2 // vectors), wide),
            jax.ShapeDtypeStruct((entries, 128), wide),
        ],
        in_specs=[vmem_spec] * 4,
        out_specs=[vmem_spec] * 2,
        compiler_params=small,
        name="chip_field",
    )(mine, theirs, noise, noise_there)


def block_operators(x, walkers, sources, picked):
    tiles = []
    for field_ref, crossed, near, other in sources:
        first = 2 * walkers * crossed
        one, two = near(picked).astype(wide), other(picked).astype(wide)
        copies = one.shape[1] // 128
        tiles.append([])
        for w in range(walkers):
            scale_one = field_ref[pl.ds(first + x * walkers + w, 1), :]
            scale_two = field_ref[pl.ds(first + (1 - x) * walkers + w, 1), :]
            scale_one = jnp.concatenate([scale_one] * copies, 1)
            scale_two = jnp.concatenate([scale_two] * copies, 1)
            block = time_root * (scale_one * one + scale_two * two)
            tiles[-1].append(block.astype(narrow))
    return tiles


def over_tiles(rows, order, body):
    high, across = 16, 256
    columns = order // across

    def tile(index, carry):
        row = pl.multiple_of((index // columns) * high, high)
        column = pl.multiple_of((index % columns) * across, across)
        body((pl.ds(row, high), pl.ds(column, across)))
        return carry

    lax.fori_loop(0, (rows // high) * columns, tile, 0)


def of_pair(ref, index):
    return lambda picked: ref[(index, *picked)]


def below(ref, top):
    return lambda picked: ref[pl.ds(top + picked[0].start, picked[0].size), picked[1]]


def both_cores(field_ref, rows, mine, mine_x, theirs, theirs_x):
    top = mine.shape[0] - 2 * rows
    return [
        (field_ref, 0, below(mine, top + rows), below(mine_x, rows)),
        (field_ref, 1, below(theirs, top), below(theirs_x, 0)),
    ]


def early_kernel(walkers, field_here, field_one, field_two, own, own_theirs, *refs):
    blocks, summed_ref = refs[:-1], refs[-1]
    _, _, x = place()
    sources = [
        (field_here, 0, of_pair(own, x), of_pair(own, 1 - x)),
        (field_here, 1, of_pair(own_theirs, x), of_pair(own_theirs, 1 - x)),
    ]
    rows = own.shape[1]
    sources += both_cores(field_one, rows, *blocks[:4])
    sources += both_cores(field_two, rows, *blocks[4:])

    def body(picked):
        tiles = block_operators(x, walkers, sources, picked)
        for w in range(walkers):
            parts = [block[w].astype(wide) for block in tiles]
            summed_ref[(w, *picked)] = sum(parts[1:], parts[0])

    over_tiles(*summed_ref.shape[1:], body)


def early_operator(walkers, fields, own, own_theirs, blocks):
    _, rows, order = own.shape
    return pl.pallas_call(
        functools.partial(early_kernel, walkers),
        out_shape=jax.ShapeDtypeStruct((walkers, rows, order), wide),
        in_specs=[vmem_spec] * (5 + len(blocks)),
        out_specs=vmem_spec,
        compiler_params=large,
        name="early_operator",
    )(*fields, own, own_theirs, *blocks)


def late_kernel(summed_ref, field_ref, *refs):
    blocks, operator_ref = refs[:-1], refs[-1]
    walkers, rows, order = summed_ref.shape
    _, _, x = place()
    sources = both_cores(field_ref, rows, *blocks)

    def body(picked):
        tiles = block_operators(x, walkers, sources, picked)
        row, column = picked
        for w in range(walkers):
            value = summed_ref[(w, *picked)]
            for block in tiles:
                value = value + block[w].astype(wide)
            top = value.astype(narrow)
            operator_ref[w, row, column] = top
            rest = (value - top.astype(wide)).astype(narrow)
            operator_ref[w, pl.ds(rows + row.start, row.size), column] = rest

    over_tiles(rows, order, body)


def split_operator(summed, field, blocks):
    walkers, rows, order = summed.shape
    return pl.pallas_call(
        late_kernel,
        out_shape=jax.ShapeDtypeStruct((walkers, 2 * rows, order), narrow),
        in_specs=[vmem_spec] * (2 + len(blocks)),
        out_specs=vmem_spec,
        compiler_params=large,
        name="split_operator",
    )(summed, field, *blocks)


def applied(operator_ref, vector_ref, step, mine, theirs):
    z, k, _ = place()
    _, rows, _ = mine.shape
    vector_ref[:, pl.ds(pl.multiple_of(k * rows, rows), rows), :] = mine[...]
    vector_ref[:, pl.ds(pl.multiple_of((1 - k) * rows, rows), rows), :] = theirs[...]
    start = pl.multiple_of(flipped(z, step) * 2 * rows, 2 * rows)

    def of_walker(w):
        both = jnp.dot(
            operator_ref[w, :, pl.ds(start, 2 * rows)],
            vector_ref[w],
            preferred_element_type=wide,
        )
        return both[:rows] + both[rows:]

    return of_walker


def near_kernel(operator_ref, *refs):
    pieces, (out_ref, vector_ref) = refs[:6], refs[6:]
    parts = [
        applied(operator_ref, vector_ref.at[step], step, pieces[step], pieces[3 + step])
        for step in range(3)
    ]
    for w in range(out_ref.shape[0]):
        out_ref[w] = parts[0](w) + parts[1](w) + parts[2](w)


def near_application(operator, pieces):
    walkers, rows, occupied = pieces[0].shape
    return pl.pallas_call(
        near_kernel,
        out_shape=jax.ShapeDtypeStruct((walkers, rows, occupied), wide),
        in_specs=[vmem_spec] * 7,
        out_specs=vmem_spec,
        scratch_shapes=[pltpu.VMEM((3, walkers, 2 * rows, occupied), narrow)],
        compiler_params=small,
        name="near_application",
    )(operator, *pieces)


def first_kernel(operator_ref, partial_ref, mine, theirs, first_ref, narrow_ref, vector_ref):
    part = applied(operator_ref, vector_ref, 3, mine, theirs)
    for w in range(first_ref.shape[0]):
        term = partial_ref[w] + part(w)
        first_ref[w] = term
        narrow_ref[w] = term.astype(narrow)


def first_application(operator, partial, mine, theirs):
    walkers, rows, occupied = mine.shape
    return pl.pallas_call(
        first_kernel,
        out_shape=[
            jax.ShapeDtypeStruct((walkers, rows, occupied), wide),
            jax.ShapeDtypeStruct((walkers, rows, occupied), narrow),
        ],
        in_specs=[vmem_spec] * 4,
        out_specs=[vmem_spec] * 2,
        scratch_shapes=[pltpu.VMEM((walkers, 2 * rows, occupied), narrow)],
        compiler_params=small,
        name="first_application",
    )(operator, partial, mine, theirs)


def base_kernel(operator_ref, first_ref, orbitals_ref, *refs):
    pieces, (out_ref, vector_ref) = refs[:6], refs[6:]
    parts = [
        applied(operator_ref, vector_ref.at[step], step, pieces[step], pieces[3 + step])
        for step in range(3)
    ]
    for w in range(first_ref.shape[0]):
        second = parts[0](w) + parts[1](w) + parts[2](w)
        out_ref[w] = orbitals_ref[0, :, w, :] + first_ref[w] + 0.5 * second


def base_application(operator, first_term, orbitals, pieces):
    walkers, rows, occupied = first_term.shape
    return pl.pallas_call(
        base_kernel,
        out_shape=jax.ShapeDtypeStruct(first_term.shape, wide),
        in_specs=[vmem_spec] * 9,
        out_specs=vmem_spec,
        scratch_shapes=[pltpu.VMEM((3, walkers, 2 * rows, occupied), narrow)],
        compiler_params=small,
        name="base_application",
    )(operator, first_term, orbitals, *pieces)


def second_kernel(operator_ref, base_ref, mine, theirs, out_ref, vector_ref):
    part = applied(operator_ref, vector_ref, 3, mine, theirs)
    for w in range(base_ref.shape[0]):
        out_ref[0, :, w, :] = base_ref[w] + 0.5 * part(w)


def second_application(operator, base, mine, theirs):
    walkers, rows, occupied = mine.shape
    return pl.pallas_call(
        second_kernel,
        out_shape=jax.ShapeDtypeStruct((1, rows, walkers, occupied), wide),
        in_specs=[vmem_spec] * 4,
        out_specs=vmem_spec,
        scratch_shapes=[pltpu.VMEM((walkers, 2 * rows, occupied), narrow)],
        compiler_params=small,
        name="second_application",
    )(operator, base, mine, theirs)


def to_chip(value, step):
    return lax.ppermute(value, "chol", [(i, i ^ (2 * step)) for i in range(8)])


def to_core(value):
    return lax.ppermute(value, "chol", [(i, i ^ 1) for i in range(8)])


def across(value):
    return lax.ppermute(value, "walk", [(0, 1), (1, 0)])


def row_device(green_blocks, half_chol, full_chol, meanfield, noise_draws, orbitals):
    walkers, rows, _ = green_blocks.shape
    vectors = half_chol.shape[0]

    half_theirs = to_core(half_chol)
    constants = jnp.concatenate([noise_draws.T.reshape(-1), jnp.repeat(meanfield, walkers)])
    constants = jnp.broadcast_to(constants[:, None], (2 * vectors * walkers, 128))
    constants_theirs = to_core(constants)
    one, two, three, own, own_cross = packed(full_chol, green_blocks)
    two, one = to_chip(two, 2), to_chip(one, 1)
    own_theirs = to_core(own_cross)
    three = to_chip(after(three, one, half_theirs, own_theirs, constants_theirs), 3)
    green_three = to_chip(two[:rows], 1)

    one_x, two_x, three_x = across(one[rows:]), across(two[rows:]), across(three)
    messages = {1: (one, one_x), 2: (two, two_x), 3: (three, three_x)}
    blocks = {step: [*both, *[to_core(each) for each in both]] for step, both in messages.items()}

    bias = chip_bias((green_blocks, one, two, green_three), half_chol, half_theirs)
    bias_shift, field = chip_field(bias, to_core(bias), constants, constants_theirs, vectors)
    field_one, field_two, field_three = (to_chip(field, step) for step in (1, 2, 3))

    start = after(walker_major(orbitals), field_two, blocks[1][2], blocks[2][2])
    start_two, start_one = to_chip(start, 2), to_chip(start, 1)
    start_three = to_chip(after(start_two, blocks[1][3], blocks[2][3], blocks[3][2]), 1)

    summed = early_operator(
        walkers,
        (field, field_one, field_two),
        own,
        own_theirs,
        (*blocks[1], *blocks[2]),
    )
    operator = split_operator(summed, field_three, blocks[3])

    near = [start, start_one, start_two]
    partial = near_application(operator, [*near, *[to_core(piece) for piece in near]])
    first_term, first_narrow = first_application(
        operator, partial, start_three, to_core(after(start_three, partial))
    )
    first_two, first_one = to_chip(first_narrow, 2), to_chip(first_narrow, 1)
    first_three = to_chip(first_two, 1)
    near = [first_narrow, first_one, first_two]
    base = base_application(
        operator, first_term, orbitals, [*near, *[to_core(piece) for piece in near]]
    )
    walkers_next = second_application(
        operator, base, first_three, to_core(after(first_three, base))
    )
    return (walkers_next, bias_shift.T)


def solution(mesh):
    placed = (
        P(("grp", "walk"), "chol", "orb"),
        P(("grp", "chol"), None, "orb"),
        P(("grp", "chol"), "orb", None),
        P(("grp", "chol")),
        P(("grp", "walk"), "chol"),
        P("orb", "chol", ("grp", "walk"), None),
    )
    sizes = mesh.shape
    if sizes["orb"] == 1 and sizes["walk"] == 2 and sizes["chol"] == 8:
        per_device = row_device
    else:
        per_device = general_device
    return jax.shard_map(
        per_device,
        mesh=mesh,
        in_specs=placed,
        out_specs=(P("orb", "chol", ("grp", "walk"), None), P(("grp", "walk"), "chol")),
        check_vma=False,
    )
```

```python
import functools

import jax
import jax.numpy as jnp
from jax import lax
from jax.experimental import pallas as pl
from jax.experimental.pallas import tpu as pltpu
from jax.sharding import PartitionSpec as P

time_root = 0.1


def general_device(green_blocks, half_chol, full_chol, meanfield, noise_draws, orbitals):
    walkers_here = green_blocks.shape[0]
    chol_here = half_chol.shape[0]
    half_rows = full_chol.shape[1]
    orbital_count = full_chol.shape[2]
    occupied = orbitals.shape[3]
    rows_here = orbitals.shape[1]
    partial_bias = jnp.einsum(
        "wki,cki->wc",
        lax.all_gather(green_blocks, "chol", axis=1, tiled=True),
        half_chol,
        preferred_element_type=jnp.float32,
    )
    force_bias = lax.psum(partial_bias, "orb")
    bias_shift = jnp.clip(time_root * (force_bias - meanfield[None, :]), -1.0, 1.0)
    shifted_field = noise_draws - bias_shift
    combined = jnp.zeros((walkers_here, half_rows, orbital_count), jnp.float32)
    for chol_index in range(chol_here):
        combined = combined + shifted_field[:, chol_index, None, None] * full_chol[chol_index][
            None
        ].astype(jnp.float32)
    operator_rows = (time_root * combined).astype(jnp.bfloat16)

    def apply_operator(vector):
        both_halves = lax.all_gather(vector, "orb", axis=0, tiled=True)
        running = jnp.zeros((walkers_here, half_rows, occupied), jnp.float32)
        shard_piece = lax.all_gather(both_halves, "chol", axis=1, tiled=True)
        row_count = shard_piece.shape[1]
        for half_index in range(shard_piece.shape[0]):
            col_block = lax.dynamic_slice_in_dim(
                operator_rows, half_index * half_rows, row_count, 2
            )
            running = running + lax.dot_general(
                col_block,
                shard_piece[half_index],
                (((2,), (0,)), ((0,), (1,))),
                preferred_element_type=jnp.float32,
            )
        summed = lax.psum(running, "chol")
        chol_slot = lax.axis_index("chol")
        owned_rows = lax.dynamic_slice_in_dim(summed, chol_slot * rows_here, rows_here, 1)
        return jnp.transpose(owned_rows, (1, 0, 2))[None]

    first_term = apply_operator(orbitals.astype(jnp.bfloat16))
    second_term = apply_operator(first_term.astype(jnp.bfloat16))
    walkers_next = orbitals + first_term + 0.5 * second_term
    return (walkers_next, bias_shift)


vmem_spec = pl.BlockSpec(memory_space=pltpu.VMEM)
hbm_spec = pl.BlockSpec(memory_space=pltpu.HBM)
wide = jnp.float32
narrow = jnp.bfloat16
small = pltpu.CompilerParams(vmem_limit_bytes=8 << 20)
large = pltpu.CompilerParams(vmem_limit_bytes=16 << 20)


def after(value, *others):
    return lax.optimization_barrier((value, *others))[0]


def place():
    slot = lax.axis_index("chol")
    return slot // 2, slot % 2, lax.axis_index("walk")


def flipped(z, step):
    return lax.bitwise_xor(z, jnp.int32(step))


def pack_kernel(full_ref, green_ref, one_ref, two_ref, three_ref, own_ref, cross_ref, sem):
    z, k, x = place()
    walkers, rows, occupied = green_ref.shape
    copies = []

    def copy(source, target):
        copies.append(pltpu.make_async_copy(source, target, sem.at[len(copies)]))
        copies[-1].start()

    def of_chip(step, core):
        return pl.ds(pl.multiple_of((2 * flipped(z, step) + core) * rows, rows), rows)

    for step, message, top in ((2, two_ref, rows), (1, one_ref, rows), (3, three_ref, 0)):
        for index, core in enumerate((1 - k, k)):
            copy(
                full_ref.at[x, of_chip(step, core), :],
                message.at[pl.ds(top + index * rows, rows), :],
            )
    copy(full_ref.at[:, of_chip(0, k), :], own_ref)
    copy(full_ref.at[:, of_chip(0, 1 - k), :], cross_ref)
    for each in copies:
        each.wait()
    for message in (two_ref, one_ref):
        for w in range(walkers):
            message[:rows, w * occupied : (w + 1) * occupied] = green_ref[w]


def packed(full_chol, green_blocks):
    order = full_chol.shape[2]
    rows = green_blocks.shape[1]
    shapes = [(3 * rows, order), (3 * rows, order), (2 * rows, order)] + [(2, rows, order)] * 2
    return pl.pallas_call(
        pack_kernel,
        out_shape=[jax.ShapeDtypeStruct(shape, narrow) for shape in shapes],
        in_specs=[hbm_spec, vmem_spec],
        out_specs=[vmem_spec] * 5,
        scratch_shapes=[pltpu.SemaphoreType.DMA((8,))],
        name="packed",
    )(full_chol, green_blocks)


def start_kernel(orbitals_ref, out_ref):
    for walker in range(out_ref.shape[0]):
        out_ref[walker] = orbitals_ref[0, :, walker, :].astype(narrow)


def walker_major(orbitals):
    _, rows, walkers, occupied = orbitals.shape
    return pl.pallas_call(
        start_kernel,
        out_shape=jax.ShapeDtypeStruct((walkers, rows, occupied), narrow),
        in_specs=[vmem_spec],
        out_specs=vmem_spec,
        compiler_params=small,
        name="walker_major",
    )(orbitals)


def bias_kernel(here_ref, one_ref, two_ref, three_ref, mine_ref, theirs_ref, out_ref):
    z, k, _ = place()
    walkers, rows, occupied = here_ref.shape
    vectors = mine_ref.shape[0]
    step_rows = 16
    totals = [jnp.zeros((8, 128), wide) for _ in range(2 * vectors * walkers)]
    for step, green in enumerate((here_ref, one_ref, two_ref, three_ref)):
        base = (2 * flipped(z, step) + k) * rows

        def add(index, totals, step=step, base=base, green=green):
            here = pl.multiple_of(index * step_rows, step_rows)
            there = pl.multiple_of(base + index * step_rows, step_rows)
            picked = pl.ds(here, step_rows)
            if step == 0:
                greens = [green[w, picked, :] for w in range(walkers)]
            else:
                greens = [green[picked, w * occupied : (w + 1) * occupied] for w in range(walkers)]
            greens = [g.astype(wide) for g in greens]
            totals = list(totals)
            for c in range(2 * vectors):
                chol_ref = mine_ref if c < vectors else theirs_ref
                chol = chol_ref[c % vectors, pl.ds(there, step_rows), :].astype(wide)
                for w in range(walkers):
                    product = greens[w] * chol
                    tiles = [
                        product[r : r + 8, n : n + 128]
                        for r in range(0, step_rows, 8)
                        for n in range(0, occupied, 128)
                    ]
                    totals[c * walkers + w] = totals[c * walkers + w] + sum(tiles[1:], tiles[0])
            return tuple(totals)

        totals = lax.fori_loop(0, rows // step_rows, add, tuple(totals))
    for index, total in enumerate(totals):
        value = jnp.sum(jnp.sum(total, axis=0, keepdims=True), axis=1, keepdims=True)
        out_ref[pl.ds(index, 1), :] = jnp.broadcast_to(value, (1, 128))


def chip_bias(green, mine, theirs):
    entries = 2 * mine.shape[0] * green[0].shape[0]
    return pl.pallas_call(
        bias_kernel,
        out_shape=jax.ShapeDtypeStruct((entries, 128), wide),
        in_specs=[vmem_spec] * 6,
        out_specs=vmem_spec,
        compiler_params=small,
        name="chip_bias",
    )(*green, mine, theirs)


def field_kernel(mine_ref, theirs_ref, noise_ref, noise_there_ref, shift_ref, field_ref):
    half = mine_ref.shape[0] // 2
    low, high = pl.ds(0, half), pl.ds(half, half)
    for rows, other, consts in ((low, high, noise_ref), (high, low, noise_there_ref)):
        force = mine_ref[rows, :] + theirs_ref[other, :]
        shift = jnp.clip(time_root * (force - consts[high, :]), -1.0, 1.0)
        field_ref[rows, :] = consts[low, :] - shift
        if rows is low:
            vectors, walkers = shift_ref.shape
            row = lax.broadcasted_iota(jnp.int32, (walkers, 128), 0)
            lane = lax.broadcasted_iota(jnp.int32, (walkers, 128), 1)
            for vector in range(vectors):
                part = shift[vector * walkers : (vector + 1) * walkers, :]
                picked = jnp.sum(jnp.where(row == lane, part, 0.0), axis=0, keepdims=True)
                shift_ref[vector : vector + 1, :] = picked[:, :walkers]


def chip_field(mine, theirs, noise, noise_there, vectors):
    entries = mine.shape[0]
    return pl.pallas_call(
        field_kernel,
        out_shape=[
            jax.ShapeDtypeStruct((vectors, entries // 2 // vectors), wide),
            jax.ShapeDtypeStruct((entries, 128), wide),
        ],
        in_specs=[vmem_spec] * 4,
        out_specs=[vmem_spec] * 2,
        compiler_params=small,
        name="chip_field",
    )(mine, theirs, noise, noise_there)


def block_operators(x, walkers, sources, picked):
    tiles = []
    for field_ref, crossed, near, other in sources:
        first = 2 * walkers * crossed
        one, two = near(picked).astype(wide), other(picked).astype(wide)
        copies = one.shape[1] // 128
        tiles.append([])
        for w in range(walkers):
            scale_one = field_ref[pl.ds(first + x * walkers + w, 1), :]
            scale_two = field_ref[pl.ds(first + (1 - x) * walkers + w, 1), :]
            scale_one = jnp.concatenate([scale_one] * copies, 1)
            scale_two = jnp.concatenate([scale_two] * copies, 1)
            block = time_root * (scale_one * one + scale_two * two)
            tiles[-1].append(block.astype(narrow))
    return tiles


def over_tiles(rows, order, body):
    high, across = 16, 256
    columns = order // across

    def tile(index, carry):
        row = pl.multiple_of((index // columns) * high, high)
        column = pl.multiple_of((index % columns) * across, across)
        body((pl.ds(row, high), pl.ds(column, across)))
        return carry

    lax.fori_loop(0, (rows // high) * columns, tile, 0)


def of_pair(ref, index):
    return lambda picked: ref[(index, *picked)]


def below(ref, top):
    return lambda picked: ref[pl.ds(top + picked[0].start, picked[0].size), picked[1]]


def both_cores(field_ref, rows, mine, mine_x, theirs, theirs_x):
    top = mine.shape[0] - 2 * rows
    return [
        (field_ref, 0, below(mine, top + rows), below(mine_x, rows)),
        (field_ref, 1, below(theirs, top), below(theirs_x, 0)),
    ]


def early_kernel(walkers, field_here, field_one, field_two, own, own_theirs, *refs):
    blocks, summed_ref = refs[:-1], refs[-1]
    _, _, x = place()
    sources = [
        (field_here, 0, of_pair(own, x), of_pair(own, 1 - x)),
        (field_here, 1, of_pair(own_theirs, x), of_pair(own_theirs, 1 - x)),
    ]
    rows = own.shape[1]
    sources += both_cores(field_one, rows, *blocks[:4])
    sources += both_cores(field_two, rows, *blocks[4:])

    def body(picked):
        tiles = block_operators(x, walkers, sources, picked)
        for w in range(walkers):
            parts = [block[w].astype(wide) for block in tiles]
            summed_ref[(w, *picked)] = sum(parts[1:], parts[0])

    over_tiles(*summed_ref.shape[1:], body)


def early_operator(walkers, fields, own, own_theirs, blocks):
    _, rows, order = own.shape
    return pl.pallas_call(
        functools.partial(early_kernel, walkers),
        out_shape=jax.ShapeDtypeStruct((walkers, rows, order), wide),
        in_specs=[vmem_spec] * (5 + len(blocks)),
        out_specs=vmem_spec,
        compiler_params=large,
        name="early_operator",
    )(*fields, own, own_theirs, *blocks)


def late_kernel(summed_ref, field_ref, *refs):
    blocks, operator_ref = refs[:-1], refs[-1]
    walkers, rows, order = summed_ref.shape
    _, _, x = place()
    sources = both_cores(field_ref, rows, *blocks)

    def body(picked):
        tiles = block_operators(x, walkers, sources, picked)
        row, column = picked
        for w in range(walkers):
            value = summed_ref[(w, *picked)]
            for block in tiles:
                value = value + block[w].astype(wide)
            top = value.astype(narrow)
            operator_ref[w, row, column] = top
            rest = (value - top.astype(wide)).astype(narrow)
            operator_ref[w, pl.ds(rows + row.start, row.size), column] = rest

    over_tiles(rows, order, body)


def split_operator(summed, field, blocks):
    walkers, rows, order = summed.shape
    return pl.pallas_call(
        late_kernel,
        out_shape=jax.ShapeDtypeStruct((walkers, 2 * rows, order), narrow),
        in_specs=[vmem_spec] * (2 + len(blocks)),
        out_specs=vmem_spec,
        compiler_params=large,
        name="split_operator",
    )(summed, field, *blocks)


def applied(operator_ref, vector_ref, step, mine, theirs):
    z, k, _ = place()
    _, rows, _ = mine.shape
    vector_ref[:, pl.ds(pl.multiple_of(k * rows, rows), rows), :] = mine[...]
    vector_ref[:, pl.ds(pl.multiple_of((1 - k) * rows, rows), rows), :] = theirs[...]
    start = pl.multiple_of(flipped(z, step) * 2 * rows, 2 * rows)

    def of_walker(w):
        both = jnp.dot(
            operator_ref[w, :, pl.ds(start, 2 * rows)],
            vector_ref[w],
            preferred_element_type=wide,
        )
        return both[:rows] + both[rows:]

    return of_walker


def near_kernel(operator_ref, *refs):
    pieces, (out_ref, vector_ref) = refs[:6], refs[6:]
    parts = [
        applied(operator_ref, vector_ref.at[step], step, pieces[step], pieces[3 + step])
        for step in range(3)
    ]
    for w in range(out_ref.shape[0]):
        out_ref[w] = parts[0](w) + parts[1](w) + parts[2](w)


def near_application(operator, pieces):
    walkers, rows, occupied = pieces[0].shape
    return pl.pallas_call(
        near_kernel,
        out_shape=jax.ShapeDtypeStruct((walkers, rows, occupied), wide),
        in_specs=[vmem_spec] * 7,
        out_specs=vmem_spec,
        scratch_shapes=[pltpu.VMEM((3, walkers, 2 * rows, occupied), narrow)],
        compiler_params=small,
        name="near_application",
    )(operator, *pieces)


def first_kernel(operator_ref, partial_ref, mine, theirs, first_ref, narrow_ref, vector_ref):
    part = applied(operator_ref, vector_ref, 3, mine, theirs)
    for w in range(first_ref.shape[0]):
        term = partial_ref[w] + part(w)
        first_ref[w] = term
        narrow_ref[w] = term.astype(narrow)


def first_application(operator, partial, mine, theirs):
    walkers, rows, occupied = mine.shape
    return pl.pallas_call(
        first_kernel,
        out_shape=[
            jax.ShapeDtypeStruct((walkers, rows, occupied), wide),
            jax.ShapeDtypeStruct((walkers, rows, occupied), narrow),
        ],
        in_specs=[vmem_spec] * 4,
        out_specs=[vmem_spec] * 2,
        scratch_shapes=[pltpu.VMEM((walkers, 2 * rows, occupied), narrow)],
        compiler_params=small,
        name="first_application",
    )(operator, partial, mine, theirs)


def base_kernel(operator_ref, first_ref, orbitals_ref, *refs):
    pieces, (out_ref, vector_ref) = refs[:6], refs[6:]
    parts = [
        applied(operator_ref, vector_ref.at[step], step, pieces[step], pieces[3 + step])
        for step in range(3)
    ]
    for w in range(first_ref.shape[0]):
        second = parts[0](w) + parts[1](w) + parts[2](w)
        out_ref[w] = orbitals_ref[0, :, w, :] + first_ref[w] + 0.5 * second


def base_application(operator, first_term, orbitals, pieces):
    walkers, rows, occupied = first_term.shape
    return pl.pallas_call(
        base_kernel,
        out_shape=jax.ShapeDtypeStruct(first_term.shape, wide),
        in_specs=[vmem_spec] * 9,
        out_specs=vmem_spec,
        scratch_shapes=[pltpu.VMEM((3, walkers, 2 * rows, occupied), narrow)],
        compiler_params=small,
        name="base_application",
    )(operator, first_term, orbitals, *pieces)


def second_kernel(operator_ref, base_ref, mine, theirs, out_ref, vector_ref):
    part = applied(operator_ref, vector_ref, 3, mine, theirs)
    for w in range(base_ref.shape[0]):
        out_ref[0, :, w, :] = base_ref[w] + 0.5 * part(w)


def second_application(operator, base, mine, theirs):
    walkers, rows, occupied = mine.shape
    return pl.pallas_call(
        second_kernel,
        out_shape=jax.ShapeDtypeStruct((1, rows, walkers, occupied), wide),
        in_specs=[vmem_spec] * 4,
        out_specs=vmem_spec,
        scratch_shapes=[pltpu.VMEM((walkers, 2 * rows, occupied), narrow)],
        compiler_params=small,
        name="second_application",
    )(operator, base, mine, theirs)


def to_chip(value, step):
    return lax.ppermute(value, "chol", [(i, i ^ (2 * step)) for i in range(8)])


def to_core(value):
    return lax.ppermute(value, "chol", [(i, i ^ 1) for i in range(8)])


def across(value):
    return lax.ppermute(value, "walk", [(0, 1), (1, 0)])


def row_device(green_blocks, half_chol, full_chol, meanfield, noise_draws, orbitals):
    walkers, rows, _ = green_blocks.shape
    vectors = half_chol.shape[0]

    half_theirs = to_core(half_chol)
    constants = jnp.concatenate([noise_draws.T.reshape(-1), jnp.repeat(meanfield, walkers)])
    constants = jnp.broadcast_to(constants[:, None], (2 * vectors * walkers, 128))
    constants_theirs = to_core(constants)
    one, two, three, own, own_cross = packed(full_chol, green_blocks)
    two, one = to_chip(two, 2), to_chip(one, 1)
    own_theirs = to_core(own_cross)

    one_theirs = to_core(after(one, half_theirs, own_theirs, constants_theirs))
    one_x = across(one[rows:])
    three = to_chip(after(three, one_theirs), 3)
    two_x = across(two[rows:])
    green_three = to_chip(two[:rows], 1)
    two_theirs = to_core(two)

    bias = chip_bias((green_blocks, one, two, green_three), half_chol, half_theirs)
    bias_theirs = to_core(after(bias, two_theirs))
    bias_shift, field = chip_field(bias, bias_theirs, constants, constants_theirs, vectors)
    one_x_theirs = to_core(after(one_x, field))

    start = after(walker_major(orbitals), one_x_theirs)
    start_two, start_one = to_chip(start, 2), to_chip(start, 1)
    two_x_theirs = to_core(two_x)
    three_x, three_theirs = across(three), to_core(three)
    late_field = after(field, two_x_theirs, three_theirs)
    field_one, field_two, field_three = (to_chip(late_field, step) for step in (1, 2, 3))
    start_three = to_chip(after(start_two, field_one, field_two, field_three), 1)
    three_x_theirs = to_core(three_x)
    blocks = {
        1: (one, one_x, one_theirs, one_x_theirs),
        2: (two, two_x, two_theirs, two_x_theirs),
        3: (three, three_x, three_theirs, three_x_theirs),
    }

    summed = early_operator(
        walkers,
        (field, field_one, field_two),
        own,
        own_theirs,
        (*blocks[1], *blocks[2]),
    )
    operator = split_operator(summed, field_three, blocks[3])

    near = [start, start_one, start_two]
    partial = near_application(operator, [*near, *[to_core(piece) for piece in near]])
    first_term, first_narrow = first_application(
        operator, partial, start_three, to_core(after(start_three, partial))
    )
    first_two, first_one = to_chip(first_narrow, 2), to_chip(first_narrow, 1)
    first_three = to_chip(first_two, 1)
    near = [first_narrow, first_one, first_two]
    base = base_application(
        operator, first_term, orbitals, [*near, *[to_core(piece) for piece in near]]
    )
    walkers_next = second_application(
        operator, base, first_three, to_core(after(first_three, base))
    )
    return (walkers_next, bias_shift.T)


def solution(mesh):
    placed = (
        P(("grp", "walk"), "chol", "orb"),
        P(("grp", "chol"), None, "orb"),
        P(("grp", "chol"), "orb", None),
        P(("grp", "chol")),
        P(("grp", "walk"), "chol"),
        P("orb", "chol", ("grp", "walk"), None),
    )
    sizes = mesh.shape
    if sizes["orb"] == 1 and sizes["walk"] == 2 and sizes["chol"] == 8:
        per_device = row_device
    else:
        per_device = general_device
    return jax.shard_map(
        per_device,
        mesh=mesh,
        in_specs=placed,
        out_specs=(P("orb", "chol", ("grp", "walk"), None), P(("grp", "walk"), "chol")),
        check_vma=False,
    )
```

```python
import functools

import jax
import jax.numpy as jnp
from jax import lax
from jax.experimental import pallas as pl
from jax.experimental.pallas import tpu as pltpu
from jax.sharding import PartitionSpec as P

time_root = 0.1


def general_device(green_blocks, half_chol, full_chol, meanfield, noise_draws, orbitals):
    walkers_here = green_blocks.shape[0]
    chol_here = half_chol.shape[0]
    half_rows = full_chol.shape[1]
    orbital_count = full_chol.shape[2]
    occupied = orbitals.shape[3]
    rows_here = orbitals.shape[1]
    partial_bias = jnp.einsum(
        "wki,cki->wc",
        lax.all_gather(green_blocks, "chol", axis=1, tiled=True),
        half_chol,
        preferred_element_type=jnp.float32,
    )
    force_bias = lax.psum(partial_bias, "orb")
    bias_shift = jnp.clip(time_root * (force_bias - meanfield[None, :]), -1.0, 1.0)
    shifted_field = noise_draws - bias_shift
    combined = jnp.zeros((walkers_here, half_rows, orbital_count), jnp.float32)
    for chol_index in range(chol_here):
        combined = combined + shifted_field[:, chol_index, None, None] * full_chol[chol_index][
            None
        ].astype(jnp.float32)
    operator_rows = (time_root * combined).astype(jnp.bfloat16)

    def apply_operator(vector):
        both_halves = lax.all_gather(vector, "orb", axis=0, tiled=True)
        running = jnp.zeros((walkers_here, half_rows, occupied), jnp.float32)
        shard_piece = lax.all_gather(both_halves, "chol", axis=1, tiled=True)
        row_count = shard_piece.shape[1]
        for half_index in range(shard_piece.shape[0]):
            col_block = lax.dynamic_slice_in_dim(
                operator_rows, half_index * half_rows, row_count, 2
            )
            running = running + lax.dot_general(
                col_block,
                shard_piece[half_index],
                (((2,), (0,)), ((0,), (1,))),
                preferred_element_type=jnp.float32,
            )
        summed = lax.psum(running, "chol")
        chol_slot = lax.axis_index("chol")
        owned_rows = lax.dynamic_slice_in_dim(summed, chol_slot * rows_here, rows_here, 1)
        return jnp.transpose(owned_rows, (1, 0, 2))[None]

    first_term = apply_operator(orbitals.astype(jnp.bfloat16))
    second_term = apply_operator(first_term.astype(jnp.bfloat16))
    walkers_next = orbitals + first_term + 0.5 * second_term
    return (walkers_next, bias_shift)


vmem_spec = pl.BlockSpec(memory_space=pltpu.VMEM)
hbm_spec = pl.BlockSpec(memory_space=pltpu.HBM)
wide = jnp.float32
narrow = jnp.bfloat16
small = pltpu.CompilerParams(vmem_limit_bytes=8 << 20)
large = pltpu.CompilerParams(vmem_limit_bytes=16 << 20)


def after(value, *others):
    return lax.optimization_barrier((value, *others))[0]


def place():
    slot = lax.axis_index("chol")
    return slot // 2, slot % 2, lax.axis_index("walk")


def flipped(z, step):
    return lax.bitwise_xor(z, jnp.int32(step))


def pack_kernel(full_ref, one_ref, two_ref, three_ref, own_ref, cross_ref, sem):
    z, k, x = place()
    rows = own_ref.shape[1]
    copies = []

    def copy(source, target):
        copies.append(pltpu.make_async_copy(source, target, sem.at[len(copies)]))
        copies[-1].start()

    def of_chip(step, core):
        return pl.ds(pl.multiple_of((2 * flipped(z, step) + core) * rows, rows), rows)

    for step, message in ((2, two_ref), (1, one_ref), (3, three_ref)):
        for index, core in enumerate((1 - k, k)):
            target = message.at[pl.ds(index * rows, rows), :]
            copy(full_ref.at[x, of_chip(step, core), :], target)
    copy(full_ref.at[:, of_chip(0, k), :], own_ref)
    copy(full_ref.at[:, of_chip(0, 1 - k), :], cross_ref)
    for each in copies:
        each.wait()


def packed(full_chol, rows):
    order = full_chol.shape[2]
    shapes = [(2 * rows, order)] * 3 + [(2, rows, order)] * 2
    return pl.pallas_call(
        pack_kernel,
        out_shape=[jax.ShapeDtypeStruct(shape, narrow) for shape in shapes],
        in_specs=[hbm_spec],
        out_specs=[vmem_spec] * 5,
        scratch_shapes=[pltpu.SemaphoreType.DMA((8,))],
        name="packed",
    )(full_chol)


field_rows = 16


def start_kernel(orbitals_ref, field_ref, out_ref):
    _, rows, walkers, occupied = orbitals_ref.shape
    for w in range(walkers):
        columns = slice(w * occupied, (w + 1) * occupied)
        out_ref[:rows, columns] = orbitals_ref[0, :, w, :].astype(narrow)
    rest = field_ref[...]
    lanes = rest.shape[1]
    for term in range(3):
        part = rest.astype(narrow)
        out_ref[rows:, term * lanes : (term + 1) * lanes] = part
        rest = rest - part.astype(wide)


def start_message(orbitals, field):
    _, rows, walkers, occupied = orbitals.shape
    return pl.pallas_call(
        start_kernel,
        out_shape=jax.ShapeDtypeStruct((rows + field_rows, walkers * occupied), narrow),
        in_specs=[vmem_spec] * 2,
        out_specs=vmem_spec,
        compiler_params=small,
        name="start_message",
    )(orbitals, field)


def field_of(message_ref, rows):
    lanes = 128
    terms = [
        message_ref[rows:, term * lanes : (term + 1) * lanes].astype(wide) for term in range(3)
    ]
    return terms[0] + terms[1] + terms[2]


def bias_kernel(here_ref, one_ref, two_ref, three_ref, mine_ref, theirs_ref, out_ref):
    z, k, _ = place()
    walkers, rows, occupied = here_ref.shape
    vectors = mine_ref.shape[0]
    step_rows = 16
    totals = [jnp.zeros((8, 128), wide) for _ in range(2 * vectors * walkers)]
    for step, green in enumerate((here_ref, one_ref, two_ref, three_ref)):
        base = (2 * flipped(z, step) + k) * rows

        def add(index, totals, base=base, green=green):
            here = pl.multiple_of(index * step_rows, step_rows)
            there = pl.multiple_of(base + index * step_rows, step_rows)
            picked = pl.ds(here, step_rows)
            greens = [green[w, picked, :] for w in range(walkers)]
            greens = [g.astype(wide) for g in greens]
            totals = list(totals)
            for c in range(2 * vectors):
                chol_ref = mine_ref if c < vectors else theirs_ref
                chol = chol_ref[c % vectors, pl.ds(there, step_rows), :].astype(wide)
                for w in range(walkers):
                    product = greens[w] * chol
                    tiles = [
                        product[r : r + 8, n : n + 128]
                        for r in range(0, step_rows, 8)
                        for n in range(0, occupied, 128)
                    ]
                    totals[c * walkers + w] = totals[c * walkers + w] + sum(tiles[1:], tiles[0])
            return tuple(totals)

        totals = lax.fori_loop(0, rows // step_rows, add, tuple(totals))
    for index, total in enumerate(totals):
        value = jnp.sum(jnp.sum(total, axis=0, keepdims=True), axis=1, keepdims=True)
        out_ref[pl.ds(index, 1), :] = jnp.broadcast_to(value, (1, 128))


def chip_bias(green, mine, theirs):
    entries = 2 * mine.shape[0] * green[0].shape[0]
    return pl.pallas_call(
        bias_kernel,
        out_shape=jax.ShapeDtypeStruct((entries, 128), wide),
        in_specs=[vmem_spec] * 6,
        out_specs=vmem_spec,
        compiler_params=small,
        name="chip_bias",
    )(*green, mine, theirs)


def field_kernel(mine_ref, theirs_ref, noise_ref, noise_there_ref, shift_ref, field_ref):
    half = mine_ref.shape[0] // 2
    low, high = pl.ds(0, half), pl.ds(half, half)
    for rows, other, consts in ((low, high, noise_ref), (high, low, noise_there_ref)):
        force = mine_ref[rows, :] + theirs_ref[other, :]
        shift = jnp.clip(time_root * (force - consts[high, :]), -1.0, 1.0)
        field_ref[rows, :] = consts[low, :] - shift
        if rows is low:
            vectors, walkers = shift_ref.shape
            row = lax.broadcasted_iota(jnp.int32, (walkers, 128), 0)
            lane = lax.broadcasted_iota(jnp.int32, (walkers, 128), 1)
            for vector in range(vectors):
                part = shift[vector * walkers : (vector + 1) * walkers, :]
                picked = jnp.sum(jnp.where(row == lane, part, 0.0), axis=0, keepdims=True)
                shift_ref[vector : vector + 1, :] = picked[:, :walkers]


def chip_field(mine, theirs, noise, noise_there, vectors):
    entries = mine.shape[0]
    return pl.pallas_call(
        field_kernel,
        out_shape=[
            jax.ShapeDtypeStruct((vectors, entries // 2 // vectors), wide),
            jax.ShapeDtypeStruct((entries, 128), wide),
        ],
        in_specs=[vmem_spec] * 4,
        out_specs=[vmem_spec] * 2,
        compiler_params=small,
        name="chip_field",
    )(mine, theirs, noise, noise_there)


def block_operators(x, walkers, sources, picked):
    tiles = []
    for field_ref, crossed, near, other in sources:
        first = 2 * walkers * crossed
        one, two = near(picked).astype(wide), other(picked).astype(wide)
        copies = one.shape[1] // 128
        tiles.append([])
        for w in range(walkers):
            scale_one = field_ref[pl.ds(first + x * walkers + w, 1), :]
            scale_two = field_ref[pl.ds(first + (1 - x) * walkers + w, 1), :]
            scale_one = jnp.concatenate([scale_one] * copies, 1)
            scale_two = jnp.concatenate([scale_two] * copies, 1)
            block = time_root * (scale_one * one + scale_two * two)
            tiles[-1].append(block.astype(narrow))
    return tiles


def over_tiles(rows, order, body):
    high, across = 16, 256
    columns = order // across

    def tile(index, carry):
        row = pl.multiple_of((index // columns) * high, high)
        column = pl.multiple_of((index % columns) * across, across)
        body((pl.ds(row, high), pl.ds(column, across)))
        return carry

    lax.fori_loop(0, (rows // high) * columns, tile, 0)


def of_pair(ref, index):
    return lambda picked: ref[(index, *picked)]


def below(ref, top):
    return lambda picked: ref[pl.ds(top + picked[0].start, picked[0].size), picked[1]]


def both_cores(field_ref, rows, mine, mine_x, theirs, theirs_x):
    return [
        (field_ref, 0, below(mine, rows), below(mine_x, rows)),
        (field_ref, 1, below(theirs, 0), below(theirs_x, 0)),
    ]


def early_kernel(walkers, field_here, start_one, start_two, own, own_theirs, *refs):
    blocks, (summed_ref, field_one, field_two) = refs[:8], refs[8:]
    _, _, x = place()
    rows = own.shape[1]
    field_one[...] = field_of(start_one, rows)
    field_two[...] = field_of(start_two, rows)
    sources = [
        (field_here, 0, of_pair(own, x), of_pair(own, 1 - x)),
        (field_here, 1, of_pair(own_theirs, x), of_pair(own_theirs, 1 - x)),
    ]
    sources += both_cores(field_one, rows, *blocks[:4])
    sources += both_cores(field_two, rows, *blocks[4:])

    def body(picked):
        tiles = block_operators(x, walkers, sources, picked)
        for w in range(walkers):
            parts = [block[w].astype(wide) for block in tiles]
            summed_ref[(w, *picked)] = sum(parts[1:], parts[0])

    over_tiles(*summed_ref.shape[1:], body)


def early_operator(walkers, field, start_one, start_two, own, own_theirs, blocks):
    _, rows, order = own.shape
    return pl.pallas_call(
        functools.partial(early_kernel, walkers),
        out_shape=jax.ShapeDtypeStruct((walkers, rows, order), wide),
        in_specs=[vmem_spec] * (5 + len(blocks)),
        out_specs=vmem_spec,
        scratch_shapes=[pltpu.VMEM((field_rows, 128), wide)] * 2,
        compiler_params=large,
        name="early_operator",
    )(field, start_one, start_two, own, own_theirs, *blocks)


def late_kernel(summed_ref, start_three, *refs):
    blocks, (operator_ref, field_ref) = refs[:4], refs[4:]
    walkers, rows, order = summed_ref.shape
    _, _, x = place()
    field_ref[...] = field_of(start_three, rows)
    sources = both_cores(field_ref, rows, *blocks)

    def body(picked):
        tiles = block_operators(x, walkers, sources, picked)
        row, column = picked
        for w in range(walkers):
            value = summed_ref[(w, *picked)]
            for block in tiles:
                value = value + block[w].astype(wide)
            top = value.astype(narrow)
            operator_ref[w, row, column] = top
            rest = (value - top.astype(wide)).astype(narrow)
            operator_ref[w, pl.ds(rows + row.start, row.size), column] = rest

    over_tiles(rows, order, body)


def split_operator(summed, start_three, blocks):
    walkers, rows, order = summed.shape
    return pl.pallas_call(
        late_kernel,
        out_shape=jax.ShapeDtypeStruct((walkers, 2 * rows, order), narrow),
        in_specs=[vmem_spec] * (2 + len(blocks)),
        out_specs=vmem_spec,
        scratch_shapes=[pltpu.VMEM((field_rows, 128), wide)],
        compiler_params=large,
        name="split_operator",
    )(summed, start_three, *blocks)


def applied(operator_ref, vector_ref, step, mine, theirs):
    z, k, _ = place()
    walkers, rows = operator_ref.shape[0], operator_ref.shape[1] // 2
    occupied = mine.shape[1] // walkers
    vector_ref[pl.ds(pl.multiple_of(k * rows, rows), rows), :] = mine[:rows, :]
    vector_ref[pl.ds(pl.multiple_of((1 - k) * rows, rows), rows), :] = theirs[:rows, :]
    start = pl.multiple_of(flipped(z, step) * 2 * rows, 2 * rows)

    def of_walker(w):
        both = jnp.dot(
            operator_ref[w, :, pl.ds(start, 2 * rows)],
            vector_ref[:, w * occupied : (w + 1) * occupied],
            preferred_element_type=wide,
        )
        return both[:rows] + both[rows:]

    return of_walker


def near_kernel(operator_ref, *refs):
    pieces, (out_ref, vector_ref) = refs[:6], refs[6:]
    parts = [
        applied(operator_ref, vector_ref.at[step], step, pieces[step], pieces[3 + step])
        for step in range(3)
    ]
    for w in range(out_ref.shape[0]):
        out_ref[w] = parts[0](w) + parts[1](w) + parts[2](w)


def near_application(operator, pieces):
    walkers, rows = operator.shape[0], operator.shape[1] // 2
    width = pieces[0].shape[1]
    return pl.pallas_call(
        near_kernel,
        out_shape=jax.ShapeDtypeStruct((walkers, rows, width // walkers), wide),
        in_specs=[vmem_spec] * 7,
        out_specs=vmem_spec,
        scratch_shapes=[pltpu.VMEM((3, 2 * rows, width), narrow)],
        compiler_params=small,
        name="near_application",
    )(operator, *pieces)


def first_kernel(operator_ref, partial_ref, mine, theirs, first_ref, narrow_ref, vector_ref):
    part = applied(operator_ref, vector_ref, 3, mine, theirs)
    walkers, _, occupied = first_ref.shape
    for w in range(walkers):
        term = partial_ref[w] + part(w)
        first_ref[w] = term
        narrow_ref[:, w * occupied : (w + 1) * occupied] = term.astype(narrow)


def first_application(operator, partial, mine, theirs):
    _, rows, _ = partial.shape
    width = mine.shape[1]
    return pl.pallas_call(
        first_kernel,
        out_shape=[
            jax.ShapeDtypeStruct(partial.shape, wide),
            jax.ShapeDtypeStruct((rows, width), narrow),
        ],
        in_specs=[vmem_spec] * 4,
        out_specs=[vmem_spec] * 2,
        scratch_shapes=[pltpu.VMEM((2 * rows, width), narrow)],
        compiler_params=small,
        name="first_application",
    )(operator, partial, mine, theirs)


def base_kernel(operator_ref, first_ref, orbitals_ref, *refs):
    pieces, (out_ref, vector_ref) = refs[:6], refs[6:]
    parts = [
        applied(operator_ref, vector_ref.at[step], step, pieces[step], pieces[3 + step])
        for step in range(3)
    ]
    for w in range(first_ref.shape[0]):
        second = parts[0](w) + parts[1](w) + parts[2](w)
        out_ref[w] = orbitals_ref[0, :, w, :] + first_ref[w] + 0.5 * second


def base_application(operator, first_term, orbitals, pieces):
    rows, width = pieces[0].shape
    return pl.pallas_call(
        base_kernel,
        out_shape=jax.ShapeDtypeStruct(first_term.shape, wide),
        in_specs=[vmem_spec] * 9,
        out_specs=vmem_spec,
        scratch_shapes=[pltpu.VMEM((3, 2 * rows, width), narrow)],
        compiler_params=small,
        name="base_application",
    )(operator, first_term, orbitals, *pieces)


def second_kernel(operator_ref, base_ref, mine, theirs, out_ref, vector_ref):
    part = applied(operator_ref, vector_ref, 3, mine, theirs)
    for w in range(base_ref.shape[0]):
        out_ref[0, :, w, :] = base_ref[w] + 0.5 * part(w)


def second_application(operator, base, mine, theirs):
    walkers, rows, occupied = base.shape
    return pl.pallas_call(
        second_kernel,
        out_shape=jax.ShapeDtypeStruct((1, rows, walkers, occupied), wide),
        in_specs=[vmem_spec] * 4,
        out_specs=vmem_spec,
        scratch_shapes=[pltpu.VMEM((2 * rows, walkers * occupied), narrow)],
        compiler_params=small,
        name="second_application",
    )(operator, base, mine, theirs)


def to_chip(value, step):
    return lax.ppermute(value, "chol", [(i, i ^ (2 * step)) for i in range(8)])


def to_core(value):
    return lax.ppermute(value, "chol", [(i, i ^ 1) for i in range(8)])


def across(value):
    return lax.ppermute(value, "walk", [(0, 1), (1, 0)])


def row_device(green_blocks, half_chol, full_chol, meanfield, noise_draws, orbitals):
    walkers, rows, _ = green_blocks.shape
    vectors = half_chol.shape[0]

    green_two, green_one = to_chip(green_blocks, 2), to_chip(green_blocks, 1)
    half_theirs = to_core(half_chol)
    constants = jnp.concatenate([noise_draws.T.reshape(-1), jnp.repeat(meanfield, walkers)])
    constants = jnp.broadcast_to(constants[:, None], (2 * vectors * walkers, 128))
    constants_theirs = to_core(constants)
    green_three = to_chip(green_two, 1)

    one, two, three, own, own_cross = packed(full_chol, rows)
    own_theirs = to_core(own_cross)
    two = to_chip(two, 2)

    green = (green_blocks, green_one, green_two, green_three)
    bias = chip_bias(green, half_chol, after(half_theirs, own_theirs, constants_theirs))
    bias_shift, field = chip_field(bias, to_core(bias), constants, constants_theirs, vectors)

    one = to_chip(after(one, green_three), 1)
    three = to_chip(after(three, two, field), 3)
    two_x, two_theirs = across(two), to_core(two)
    one_x, one_theirs = across(one), to_core(one)

    start = after(start_message(orbitals, field), two_x, two_theirs, one_theirs)
    start_two, start_one = to_chip(start, 2), to_chip(start, 1)
    two_x_theirs, one_x_theirs = to_core(two_x), to_core(one_x)
    three_x, three_theirs = across(three), to_core(three)
    hops = (two_x_theirs, one_x_theirs, three_theirs)
    start_three = to_chip(after(start_two, *hops), 1)
    three_x_theirs = to_core(three_x)

    summed = early_operator(
        walkers,
        field,
        start_one,
        start_two,
        own,
        own_theirs,
        (one, one_x, one_theirs, one_x_theirs, two, two_x, two_theirs, two_x_theirs),
    )
    operator = split_operator(
        summed, start_three, (three, three_x, three_theirs, three_x_theirs)
    )

    near = [start, start_one, start_two]
    partial = near_application(operator, [*near, *[to_core(piece) for piece in near]])
    first_term, first_narrow = first_application(
        operator, partial, start_three, to_core(start_three)
    )
    first_two, first_one = to_chip(first_narrow, 2), to_chip(first_narrow, 1)
    first_three = to_chip(first_two, 1)
    near = [first_narrow, first_one, first_two]
    base = base_application(
        operator, first_term, orbitals, [*near, *[to_core(piece) for piece in near]]
    )
    walkers_next = second_application(
        operator, base, first_three, to_core(after(first_three, base))
    )
    return (walkers_next, bias_shift.T)


def solution(mesh):
    placed = (
        P(("grp", "walk"), "chol", "orb"),
        P(("grp", "chol"), None, "orb"),
        P(("grp", "chol"), "orb", None),
        P(("grp", "chol")),
        P(("grp", "walk"), "chol"),
        P("orb", "chol", ("grp", "walk"), None),
    )
    sizes = mesh.shape
    if sizes["orb"] == 1 and sizes["walk"] == 2 and sizes["chol"] == 8:
        per_device = row_device
    else:
        per_device = general_device
    return jax.shard_map(
        per_device,
        mesh=mesh,
        in_specs=placed,
        out_specs=(P("orb", "chol", ("grp", "walk"), None), P(("grp", "walk"), "chol")),
        check_vma=False,
    )
```

```python
import functools

import jax
import jax.numpy as jnp
from jax import lax
from jax.experimental import pallas as pl
from jax.experimental.pallas import tpu as pltpu
from jax.sharding import PartitionSpec as P

time_root = 0.1


def general_device(green_blocks, half_chol, full_chol, meanfield, noise_draws, orbitals):
    walkers_here = green_blocks.shape[0]
    chol_here = half_chol.shape[0]
    half_rows = full_chol.shape[1]
    orbital_count = full_chol.shape[2]
    occupied = orbitals.shape[3]
    rows_here = orbitals.shape[1]
    partial_bias = jnp.einsum(
        "wki,cki->wc",
        lax.all_gather(green_blocks, "chol", axis=1, tiled=True),
        half_chol,
        preferred_element_type=jnp.float32,
    )
    force_bias = lax.psum(partial_bias, "orb")
    bias_shift = jnp.clip(time_root * (force_bias - meanfield[None, :]), -1.0, 1.0)
    shifted_field = noise_draws - bias_shift
    combined = jnp.zeros((walkers_here, half_rows, orbital_count), jnp.float32)
    for chol_index in range(chol_here):
        combined = combined + shifted_field[:, chol_index, None, None] * full_chol[chol_index][
            None
        ].astype(jnp.float32)
    operator_rows = (time_root * combined).astype(jnp.bfloat16)

    def apply_operator(vector):
        both_halves = lax.all_gather(vector, "orb", axis=0, tiled=True)
        running = jnp.zeros((walkers_here, half_rows, occupied), jnp.float32)
        shard_piece = lax.all_gather(both_halves, "chol", axis=1, tiled=True)
        row_count = shard_piece.shape[1]
        for half_index in range(shard_piece.shape[0]):
            col_block = lax.dynamic_slice_in_dim(
                operator_rows, half_index * half_rows, row_count, 2
            )
            running = running + lax.dot_general(
                col_block,
                shard_piece[half_index],
                (((2,), (0,)), ((0,), (1,))),
                preferred_element_type=jnp.float32,
            )
        summed = lax.psum(running, "chol")
        chol_slot = lax.axis_index("chol")
        owned_rows = lax.dynamic_slice_in_dim(summed, chol_slot * rows_here, rows_here, 1)
        return jnp.transpose(owned_rows, (1, 0, 2))[None]

    first_term = apply_operator(orbitals.astype(jnp.bfloat16))
    second_term = apply_operator(first_term.astype(jnp.bfloat16))
    walkers_next = orbitals + first_term + 0.5 * second_term
    return (walkers_next, bias_shift)


vmem_spec = pl.BlockSpec(memory_space=pltpu.VMEM)
hbm_spec = pl.BlockSpec(memory_space=pltpu.HBM)
wide = jnp.float32
narrow = jnp.bfloat16
small = pltpu.CompilerParams(vmem_limit_bytes=8 << 20)
large = pltpu.CompilerParams(vmem_limit_bytes=16 << 20)


def after(value, *others):
    return lax.optimization_barrier((value, *others))[0]


def place():
    slot = lax.axis_index("chol")
    return slot // 2, slot % 2, lax.axis_index("walk")


def flipped(z, step):
    return lax.bitwise_xor(z, jnp.int32(step))


def pack_kernel(full_ref, green_ref, one_ref, two_ref, three_ref, own_ref, cross_ref, sem):
    z, k, x = place()
    walkers, rows, occupied = green_ref.shape
    copies = []

    def copy(source, target):
        copies.append(pltpu.make_async_copy(source, target, sem.at[len(copies)]))
        copies[-1].start()

    def of_chip(step, core):
        return pl.ds(pl.multiple_of((2 * flipped(z, step) + core) * rows, rows), rows)

    for step, message, top in ((2, two_ref, rows), (1, one_ref, rows), (3, three_ref, 0)):
        for index, core in enumerate((1 - k, k)):
            copy(
                full_ref.at[x, of_chip(step, core), :],
                message.at[pl.ds(top + index * rows, rows), :],
            )
    copy(full_ref.at[:, of_chip(0, k), :], own_ref)
    copy(full_ref.at[:, of_chip(0, 1 - k), :], cross_ref)
    for each in copies:
        each.wait()
    for message in (two_ref, one_ref):
        for w in range(walkers):
            message[:rows, w * occupied : (w + 1) * occupied] = green_ref[w]


def packed(full_chol, green_blocks):
    order = full_chol.shape[2]
    rows = green_blocks.shape[1]
    shapes = [(3 * rows, order), (3 * rows, order), (2 * rows, order)] + [(2, rows, order)] * 2
    return pl.pallas_call(
        pack_kernel,
        out_shape=[jax.ShapeDtypeStruct(shape, narrow) for shape in shapes],
        in_specs=[hbm_spec, vmem_spec],
        out_specs=[vmem_spec] * 5,
        scratch_shapes=[pltpu.SemaphoreType.DMA((8,))],
        name="packed",
    )(full_chol, green_blocks)


def start_kernel(orbitals_ref, out_ref):
    for walker in range(out_ref.shape[0]):
        out_ref[walker] = orbitals_ref[0, :, walker, :].astype(narrow)


def walker_major(orbitals):
    _, rows, walkers, occupied = orbitals.shape
    return pl.pallas_call(
        start_kernel,
        out_shape=jax.ShapeDtypeStruct((walkers, rows, occupied), narrow),
        in_specs=[vmem_spec],
        out_specs=vmem_spec,
        compiler_params=small,
        name="walker_major",
    )(orbitals)


def bias_kernel(here_ref, one_ref, two_ref, three_ref, mine_ref, theirs_ref, out_ref):
    z, k, _ = place()
    walkers, rows, occupied = here_ref.shape
    vectors = mine_ref.shape[0]
    step_rows = 16
    totals = [jnp.zeros((8, 128), wide) for _ in range(2 * vectors * walkers)]
    for step, green in enumerate((here_ref, one_ref, two_ref, three_ref)):
        base = (2 * flipped(z, step) + k) * rows

        def add(index, totals, step=step, base=base, green=green):
            here = pl.multiple_of(index * step_rows, step_rows)
            there = pl.multiple_of(base + index * step_rows, step_rows)
            picked = pl.ds(here, step_rows)
            if step == 0:
                greens = [green[w, picked, :] for w in range(walkers)]
            else:
                greens = [green[picked, w * occupied : (w + 1) * occupied] for w in range(walkers)]
            greens = [g.astype(wide) for g in greens]
            totals = list(totals)
            for c in range(2 * vectors):
                chol_ref = mine_ref if c < vectors else theirs_ref
                chol = chol_ref[c % vectors, pl.ds(there, step_rows), :].astype(wide)
                for w in range(walkers):
                    product = greens[w] * chol
                    tiles = [
                        product[r : r + 8, n : n + 128]
                        for r in range(0, step_rows, 8)
                        for n in range(0, occupied, 128)
                    ]
                    totals[c * walkers + w] = totals[c * walkers + w] + sum(tiles[1:], tiles[0])
            return tuple(totals)

        totals = lax.fori_loop(0, rows // step_rows, add, tuple(totals))
    for index, total in enumerate(totals):
        value = jnp.sum(jnp.sum(total, axis=0, keepdims=True), axis=1, keepdims=True)
        out_ref[pl.ds(index, 1), :] = jnp.broadcast_to(value, (1, 128))


def chip_bias(green, mine, theirs):
    entries = 2 * mine.shape[0] * green[0].shape[0]
    return pl.pallas_call(
        bias_kernel,
        out_shape=jax.ShapeDtypeStruct((entries, 128), wide),
        in_specs=[vmem_spec] * 6,
        out_specs=vmem_spec,
        compiler_params=small,
        name="chip_bias",
    )(*green, mine, theirs)


def field_kernel(mine_ref, theirs_ref, noise_ref, noise_there_ref, shift_ref, field_ref):
    half = mine_ref.shape[0] // 2
    low, high = pl.ds(0, half), pl.ds(half, half)
    for rows, other, consts in ((low, high, noise_ref), (high, low, noise_there_ref)):
        force = mine_ref[rows, :] + theirs_ref[other, :]
        shift = jnp.clip(time_root * (force - consts[high, :]), -1.0, 1.0)
        field_ref[rows, :] = consts[low, :] - shift
        if rows is low:
            vectors, walkers = shift_ref.shape
            row = lax.broadcasted_iota(jnp.int32, (walkers, 128), 0)
            lane = lax.broadcasted_iota(jnp.int32, (walkers, 128), 1)
            for vector in range(vectors):
                part = shift[vector * walkers : (vector + 1) * walkers, :]
                picked = jnp.sum(jnp.where(row == lane, part, 0.0), axis=0, keepdims=True)
                shift_ref[vector : vector + 1, :] = picked[:, :walkers]


def chip_field(mine, theirs, noise, noise_there, vectors):
    entries = mine.shape[0]
    return pl.pallas_call(
        field_kernel,
        out_shape=[
            jax.ShapeDtypeStruct((vectors, entries // 2 // vectors), wide),
            jax.ShapeDtypeStruct((entries, 128), wide),
        ],
        in_specs=[vmem_spec] * 4,
        out_specs=[vmem_spec] * 2,
        compiler_params=small,
        name="chip_field",
    )(mine, theirs, noise, noise_there)


def block_operators(x, walkers, sources, picked):
    tiles = []
    for field_ref, crossed, near, other in sources:
        first = 2 * walkers * crossed
        one, two = near(picked).astype(wide), other(picked).astype(wide)
        copies = one.shape[1] // 128
        tiles.append([])
        for w in range(walkers):
            scale_one = field_ref[pl.ds(first + x * walkers + w, 1), :]
            scale_two = field_ref[pl.ds(first + (1 - x) * walkers + w, 1), :]
            scale_one = jnp.concatenate([scale_one] * copies, 1)
            scale_two = jnp.concatenate([scale_two] * copies, 1)
            block = time_root * (scale_one * one + scale_two * two)
            tiles[-1].append(block.astype(narrow))
    return tiles


def over_tiles(rows, order, body):
    high, across = 16, 256
    columns = order // across

    def tile(index, carry):
        row = pl.multiple_of((index // columns) * high, high)
        column = pl.multiple_of((index % columns) * across, across)
        body((pl.ds(row, high), pl.ds(column, across)))
        return carry

    lax.fori_loop(0, (rows // high) * columns, tile, 0)


def of_pair(ref, index):
    return lambda picked: ref[(index, *picked)]


def below(ref, top):
    return lambda picked: ref[pl.ds(top + picked[0].start, picked[0].size), picked[1]]


def both_cores(field_ref, rows, mine, mine_x, theirs, theirs_x):
    top = mine.shape[0] - 2 * rows
    return [
        (field_ref, 0, below(mine, top + rows), below(mine_x, rows)),
        (field_ref, 1, below(theirs, top), below(theirs_x, 0)),
    ]


def early_kernel(walkers, field_here, field_one, field_two, own, own_theirs, *refs):
    blocks, summed_ref = refs[:-1], refs[-1]
    _, _, x = place()
    sources = [
        (field_here, 0, of_pair(own, x), of_pair(own, 1 - x)),
        (field_here, 1, of_pair(own_theirs, x), of_pair(own_theirs, 1 - x)),
    ]
    rows = own.shape[1]
    sources += both_cores(field_one, rows, *blocks[:4])
    sources += both_cores(field_two, rows, *blocks[4:])

    def body(picked):
        tiles = block_operators(x, walkers, sources, picked)
        for w in range(walkers):
            parts = [block[w].astype(wide) for block in tiles]
            summed_ref[(w, *picked)] = sum(parts[1:], parts[0])

    over_tiles(*summed_ref.shape[1:], body)


def early_operator(walkers, fields, own, own_theirs, blocks):
    _, rows, order = own.shape
    return pl.pallas_call(
        functools.partial(early_kernel, walkers),
        out_shape=jax.ShapeDtypeStruct((walkers, rows, order), wide),
        in_specs=[vmem_spec] * (5 + len(blocks)),
        out_specs=vmem_spec,
        compiler_params=large,
        name="early_operator",
    )(*fields, own, own_theirs, *blocks)


def late_kernel(summed_ref, field_ref, *refs):
    blocks, operator_ref = refs[:-1], refs[-1]
    walkers, rows, order = summed_ref.shape
    _, _, x = place()
    sources = both_cores(field_ref, rows, *blocks)

    def body(picked):
        tiles = block_operators(x, walkers, sources, picked)
        row, column = picked
        for w in range(walkers):
            value = summed_ref[(w, *picked)]
            for block in tiles:
                value = value + block[w].astype(wide)
            top = value.astype(narrow)
            operator_ref[w, row, column] = top
            rest = (value - top.astype(wide)).astype(narrow)
            operator_ref[w, pl.ds(rows + row.start, row.size), column] = rest

    over_tiles(rows, order, body)


def split_operator(summed, field, blocks):
    walkers, rows, order = summed.shape
    return pl.pallas_call(
        late_kernel,
        out_shape=jax.ShapeDtypeStruct((walkers, 2 * rows, order), narrow),
        in_specs=[vmem_spec] * (2 + len(blocks)),
        out_specs=vmem_spec,
        compiler_params=large,
        name="split_operator",
    )(summed, field, *blocks)


def applied(operator_ref, vector_ref, step, mine, theirs):
    z, k, _ = place()
    _, rows, _ = mine.shape
    vector_ref[:, pl.ds(pl.multiple_of(k * rows, rows), rows), :] = mine[...]
    vector_ref[:, pl.ds(pl.multiple_of((1 - k) * rows, rows), rows), :] = theirs[...]
    start = pl.multiple_of(flipped(z, step) * 2 * rows, 2 * rows)

    def of_walker(w):
        both = jnp.dot(
            operator_ref[w, :, pl.ds(start, 2 * rows)],
            vector_ref[w],
            preferred_element_type=wide,
        )
        return both[:rows] + both[rows:]

    return of_walker


def near_kernel(operator_ref, *refs):
    pieces, (out_ref, vector_ref) = refs[:6], refs[6:]
    parts = [
        applied(operator_ref, vector_ref.at[step], step, pieces[step], pieces[3 + step])
        for step in range(3)
    ]
    for w in range(out_ref.shape[0]):
        out_ref[w] = parts[0](w) + parts[1](w) + parts[2](w)


def near_application(operator, pieces):
    walkers, rows, occupied = pieces[0].shape
    return pl.pallas_call(
        near_kernel,
        out_shape=jax.ShapeDtypeStruct((walkers, rows, occupied), wide),
        in_specs=[vmem_spec] * 7,
        out_specs=vmem_spec,
        scratch_shapes=[pltpu.VMEM((3, walkers, 2 * rows, occupied), narrow)],
        compiler_params=small,
        name="near_application",
    )(operator, *pieces)


def first_kernel(operator_ref, partial_ref, mine, theirs, first_ref, narrow_ref, vector_ref):
    part = applied(operator_ref, vector_ref, 3, mine, theirs)
    for w in range(first_ref.shape[0]):
        term = partial_ref[w] + part(w)
        first_ref[w] = term
        narrow_ref[w] = term.astype(narrow)


def first_application(operator, partial, mine, theirs):
    walkers, rows, occupied = mine.shape
    return pl.pallas_call(
        first_kernel,
        out_shape=[
            jax.ShapeDtypeStruct((walkers, rows, occupied), wide),
            jax.ShapeDtypeStruct((walkers, rows, occupied), narrow),
        ],
        in_specs=[vmem_spec] * 4,
        out_specs=[vmem_spec] * 2,
        scratch_shapes=[pltpu.VMEM((walkers, 2 * rows, occupied), narrow)],
        compiler_params=small,
        name="first_application",
    )(operator, partial, mine, theirs)


def base_kernel(operator_ref, first_ref, orbitals_ref, *refs):
    pieces, (out_ref, vector_ref) = refs[:6], refs[6:]
    parts = [
        applied(operator_ref, vector_ref.at[step], step, pieces[step], pieces[3 + step])
        for step in range(3)
    ]
    for w in range(first_ref.shape[0]):
        second = parts[0](w) + parts[1](w) + parts[2](w)
        out_ref[w] = orbitals_ref[0, :, w, :] + first_ref[w] + 0.5 * second


def base_application(operator, first_term, orbitals, pieces):
    walkers, rows, occupied = first_term.shape
    return pl.pallas_call(
        base_kernel,
        out_shape=jax.ShapeDtypeStruct(first_term.shape, wide),
        in_specs=[vmem_spec] * 9,
        out_specs=vmem_spec,
        scratch_shapes=[pltpu.VMEM((3, walkers, 2 * rows, occupied), narrow)],
        compiler_params=small,
        name="base_application",
    )(operator, first_term, orbitals, *pieces)


def second_kernel(operator_ref, base_ref, mine, theirs, out_ref, vector_ref):
    part = applied(operator_ref, vector_ref, 3, mine, theirs)
    for w in range(base_ref.shape[0]):
        out_ref[0, :, w, :] = base_ref[w] + 0.5 * part(w)


def second_application(operator, base, mine, theirs):
    walkers, rows, occupied = mine.shape
    return pl.pallas_call(
        second_kernel,
        out_shape=jax.ShapeDtypeStruct((1, rows, walkers, occupied), wide),
        in_specs=[vmem_spec] * 4,
        out_specs=vmem_spec,
        scratch_shapes=[pltpu.VMEM((walkers, 2 * rows, occupied), narrow)],
        compiler_params=small,
        name="second_application",
    )(operator, base, mine, theirs)


def to_chip(value, step):
    return lax.ppermute(value, "chol", [(i, i ^ (2 * step)) for i in range(8)])


def to_core(value):
    return lax.ppermute(value, "chol", [(i, i ^ 1) for i in range(8)])


def across(value):
    return lax.ppermute(value, "walk", [(0, 1), (1, 0)])


def row_device(green_blocks, half_chol, full_chol, meanfield, noise_draws, orbitals):
    walkers, rows, _ = green_blocks.shape
    vectors = half_chol.shape[0]

    half_theirs = to_core(half_chol)
    constants = jnp.concatenate([noise_draws.T.reshape(-1), jnp.repeat(meanfield, walkers)])
    constants = jnp.broadcast_to(constants[:, None], (2 * vectors * walkers, 128))
    constants_theirs = to_core(constants)
    one, two, three, own, own_cross = packed(full_chol, green_blocks)
    two, one = to_chip(two, 2), to_chip(one, 1)
    own_theirs = to_core(own_cross)

    one_theirs = to_core(after(one, half_theirs, own_theirs, constants_theirs))
    one_x = across(one[rows:])
    three = to_chip(after(three, one_theirs), 3)
    two_x = across(two[rows:])
    green_three = to_chip(two[:rows], 1)
    two_theirs = to_core(two)

    start = after(walker_major(orbitals), one_x, two_theirs)
    start_two, start_one = to_chip(start, 2), to_chip(start, 1)
    one_x_theirs = to_core(one_x)

    green_three = after(green_three, one_x_theirs)
    bias = chip_bias((green_blocks, one, two, green_three), half_chol, half_theirs)
    bias_shift, field = chip_field(bias, to_core(bias), constants, constants_theirs, vectors)
    two_x_theirs = to_core(two_x)
    three_x, three_theirs = across(three), to_core(three)
    late_field = after(field, two_x_theirs, three_theirs)
    field_one, field_two, field_three = (to_chip(late_field, step) for step in (1, 2, 3))
    start_three = to_chip(after(start_two, field_one, field_two, field_three), 1)
    three_x_theirs = to_core(three_x)
    blocks = {
        1: (one, one_x, one_theirs, one_x_theirs),
        2: (two, two_x, two_theirs, two_x_theirs),
        3: (three, three_x, three_theirs, three_x_theirs),
    }

    summed = early_operator(
        walkers,
        (field, field_one, field_two),
        own,
        own_theirs,
        (*blocks[1], *blocks[2]),
    )
    operator = split_operator(summed, field_three, blocks[3])

    near = [start, start_one, start_two]
    partial = near_application(operator, [*near, *[to_core(piece) for piece in near]])
    first_term, first_narrow = first_application(
        operator, partial, start_three, to_core(after(start_three, partial))
    )
    first_two, first_one = to_chip(first_narrow, 2), to_chip(first_narrow, 1)
    first_three = to_chip(first_two, 1)
    near = [first_narrow, first_one, first_two]
    base = base_application(
        operator, first_term, orbitals, [*near, *[to_core(piece) for piece in near]]
    )
    walkers_next = second_application(
        operator, base, first_three, to_core(after(first_three, base))
    )
    return (walkers_next, bias_shift.T)


def solution(mesh):
    placed = (
        P(("grp", "walk"), "chol", "orb"),
        P(("grp", "chol"), None, "orb"),
        P(("grp", "chol"), "orb", None),
        P(("grp", "chol")),
        P(("grp", "walk"), "chol"),
        P("orb", "chol", ("grp", "walk"), None),
    )
    sizes = mesh.shape
    if sizes["orb"] == 1 and sizes["walk"] == 2 and sizes["chol"] == 8:
        per_device = row_device
    else:
        per_device = general_device
    return jax.shard_map(
        per_device,
        mesh=mesh,
        in_specs=placed,
        out_specs=(P("orb", "chol", ("grp", "walk"), None), P(("grp", "walk"), "chol")),
        check_vma=False,
    )
```

```python
import functools

import jax
import jax.numpy as jnp
from jax import lax
from jax.experimental import pallas as pl
from jax.experimental.pallas import tpu as pltpu
from jax.sharding import PartitionSpec as P

time_root = 0.1


def general_device(green_blocks, half_chol, full_chol, meanfield, noise_draws, orbitals):
    walkers_here = green_blocks.shape[0]
    chol_here = half_chol.shape[0]
    half_rows = full_chol.shape[1]
    orbital_count = full_chol.shape[2]
    occupied = orbitals.shape[3]
    rows_here = orbitals.shape[1]
    partial_bias = jnp.einsum(
        "wki,cki->wc",
        lax.all_gather(green_blocks, "chol", axis=1, tiled=True),
        half_chol,
        preferred_element_type=jnp.float32,
    )
    force_bias = lax.psum(partial_bias, "orb")
    bias_shift = jnp.clip(time_root * (force_bias - meanfield[None, :]), -1.0, 1.0)
    shifted_field = noise_draws - bias_shift
    combined = jnp.zeros((walkers_here, half_rows, orbital_count), jnp.float32)
    for chol_index in range(chol_here):
        combined = combined + shifted_field[:, chol_index, None, None] * full_chol[chol_index][
            None
        ].astype(jnp.float32)
    operator_rows = (time_root * combined).astype(jnp.bfloat16)

    def apply_operator(vector):
        both_halves = lax.all_gather(vector, "orb", axis=0, tiled=True)
        running = jnp.zeros((walkers_here, half_rows, occupied), jnp.float32)
        shard_piece = lax.all_gather(both_halves, "chol", axis=1, tiled=True)
        row_count = shard_piece.shape[1]
        for half_index in range(shard_piece.shape[0]):
            col_block = lax.dynamic_slice_in_dim(
                operator_rows, half_index * half_rows, row_count, 2
            )
            running = running + lax.dot_general(
                col_block,
                shard_piece[half_index],
                (((2,), (0,)), ((0,), (1,))),
                preferred_element_type=jnp.float32,
            )
        summed = lax.psum(running, "chol")
        chol_slot = lax.axis_index("chol")
        owned_rows = lax.dynamic_slice_in_dim(summed, chol_slot * rows_here, rows_here, 1)
        return jnp.transpose(owned_rows, (1, 0, 2))[None]

    first_term = apply_operator(orbitals.astype(jnp.bfloat16))
    second_term = apply_operator(first_term.astype(jnp.bfloat16))
    walkers_next = orbitals + first_term + 0.5 * second_term
    return (walkers_next, bias_shift)


vmem_spec = pl.BlockSpec(memory_space=pltpu.VMEM)
hbm_spec = pl.BlockSpec(memory_space=pltpu.HBM)
wide = jnp.float32
narrow = jnp.bfloat16
small = pltpu.CompilerParams(vmem_limit_bytes=8 << 20)
large = pltpu.CompilerParams(vmem_limit_bytes=16 << 20)
long = pl.CostEstimate(flops=10**11, bytes_accessed=0, transcendentals=0)


def after(value, *others):
    return lax.optimization_barrier((value, *others))[0]


def place():
    slot = lax.axis_index("chol")
    return slot // 2, slot % 2, lax.axis_index("walk")


def flipped(z, step):
    return lax.bitwise_xor(z, jnp.int32(step))


def chip_rows(step, core, rows):
    z, _, _ = place()
    return pl.ds(pl.multiple_of((2 * flipped(z, step) + core) * rows, rows), rows)


def started(copies, source, target, sem):
    copies.append(pltpu.make_async_copy(source, target, sem.at[len(copies)]))
    copies[-1].start()


def near_pack_kernel(full_ref, green_ref, one_ref, two_ref, sem):
    _, k, x = place()
    walkers, rows, occupied = green_ref.shape
    copies = []
    for step, message in ((2, two_ref), (1, one_ref)):
        for index, core in enumerate((1 - k, k)):
            target = message.at[pl.ds((1 + index) * rows, rows), :]
            started(copies, full_ref.at[x, chip_rows(step, core, rows), :], target, sem)
    for each in copies:
        each.wait()
    for message in (two_ref, one_ref):
        for w in range(walkers):
            message[:rows, w * occupied : (w + 1) * occupied] = green_ref[w]


def near_packed(full_chol, green_blocks):
    order = full_chol.shape[2]
    rows = green_blocks.shape[1]
    return pl.pallas_call(
        near_pack_kernel,
        out_shape=[jax.ShapeDtypeStruct((3 * rows, order), narrow)] * 2,
        in_specs=[hbm_spec, vmem_spec],
        out_specs=[vmem_spec] * 2,
        scratch_shapes=[pltpu.SemaphoreType.DMA((4,))],
        name="near_packed",
    )(full_chol, green_blocks)


def far_pack_kernel(full_ref, three_ref, own_ref, cross_ref, sem):
    _, k, x = place()
    rows = own_ref.shape[1]
    copies = []
    for index, core in enumerate((1 - k, k)):
        target = three_ref.at[pl.ds(index * rows, rows), :]
        started(copies, full_ref.at[x, chip_rows(3, core, rows), :], target, sem)
    started(copies, full_ref.at[:, chip_rows(0, k, rows), :], own_ref, sem)
    started(copies, full_ref.at[:, chip_rows(0, 1 - k, rows), :], cross_ref, sem)
    for each in copies:
        each.wait()


def far_packed(full_chol, rows):
    order = full_chol.shape[2]
    shapes = [(2 * rows, order), (2, rows, order), (2, rows, order)]
    return pl.pallas_call(
        far_pack_kernel,
        out_shape=[jax.ShapeDtypeStruct(shape, narrow) for shape in shapes],
        in_specs=[hbm_spec],
        out_specs=[vmem_spec] * 3,
        scratch_shapes=[pltpu.SemaphoreType.DMA((4,))],
        cost_estimate=long,
        name="far_packed",
    )(full_chol)


def start_kernel(orbitals_ref, out_ref):
    for walker in range(out_ref.shape[0]):
        out_ref[walker] = orbitals_ref[0, :, walker, :].astype(narrow)


def walker_major(orbitals):
    _, rows, walkers, occupied = orbitals.shape
    return pl.pallas_call(
        start_kernel,
        out_shape=jax.ShapeDtypeStruct((walkers, rows, occupied), narrow),
        in_specs=[vmem_spec],
        out_specs=vmem_spec,
        compiler_params=small,
        name="walker_major",
    )(orbitals)


def bias_kernel(here_ref, one_ref, two_ref, three_ref, mine_ref, theirs_ref, out_ref):
    z, k, _ = place()
    walkers, rows, occupied = here_ref.shape
    vectors = mine_ref.shape[0]
    step_rows = 16
    totals = [jnp.zeros((8, 128), wide) for _ in range(2 * vectors * walkers)]
    for step, green in enumerate((here_ref, one_ref, two_ref, three_ref)):
        base = (2 * flipped(z, step) + k) * rows

        def add(index, totals, step=step, base=base, green=green):
            here = pl.multiple_of(index * step_rows, step_rows)
            there = pl.multiple_of(base + index * step_rows, step_rows)
            picked = pl.ds(here, step_rows)
            if step == 0:
                greens = [green[w, picked, :] for w in range(walkers)]
            else:
                greens = [green[picked, w * occupied : (w + 1) * occupied] for w in range(walkers)]
            greens = [g.astype(wide) for g in greens]
            totals = list(totals)
            for c in range(2 * vectors):
                chol_ref = mine_ref if c < vectors else theirs_ref
                chol = chol_ref[c % vectors, pl.ds(there, step_rows), :].astype(wide)
                for w in range(walkers):
                    product = greens[w] * chol
                    tiles = [
                        product[r : r + 8, n : n + 128]
                        for r in range(0, step_rows, 8)
                        for n in range(0, occupied, 128)
                    ]
                    totals[c * walkers + w] = totals[c * walkers + w] + sum(tiles[1:], tiles[0])
            return tuple(totals)

        totals = lax.fori_loop(0, rows // step_rows, add, tuple(totals))
    for index, total in enumerate(totals):
        value = jnp.sum(jnp.sum(total, axis=0, keepdims=True), axis=1, keepdims=True)
        out_ref[pl.ds(index, 1), :] = jnp.broadcast_to(value, (1, 128))


def chip_bias(green, mine, theirs):
    entries = 2 * mine.shape[0] * green[0].shape[0]
    return pl.pallas_call(
        bias_kernel,
        out_shape=jax.ShapeDtypeStruct((entries, 128), wide),
        in_specs=[vmem_spec] * 6,
        out_specs=vmem_spec,
        compiler_params=small,
        name="chip_bias",
    )(*green, mine, theirs)


def field_kernel(mine_ref, theirs_ref, noise_ref, noise_there_ref, shift_ref, field_ref):
    half = mine_ref.shape[0] // 2
    low, high = pl.ds(0, half), pl.ds(half, half)
    for rows, other, consts in ((low, high, noise_ref), (high, low, noise_there_ref)):
        force = mine_ref[rows, :] + theirs_ref[other, :]
        shift = jnp.clip(time_root * (force - consts[high, :]), -1.0, 1.0)
        field_ref[rows, :] = consts[low, :] - shift
        if rows is low:
            vectors, walkers = shift_ref.shape
            row = lax.broadcasted_iota(jnp.int32, (walkers, 128), 0)
            lane = lax.broadcasted_iota(jnp.int32, (walkers, 128), 1)
            for vector in range(vectors):
                part = shift[vector * walkers : (vector + 1) * walkers, :]
                picked = jnp.sum(jnp.where(row == lane, part, 0.0), axis=0, keepdims=True)
                shift_ref[vector : vector + 1, :] = picked[:, :walkers]


def chip_field(mine, theirs, noise, noise_there, vectors):
    entries = mine.shape[0]
    return pl.pallas_call(
        field_kernel,
        out_shape=[
            jax.ShapeDtypeStruct((vectors, entries // 2 // vectors), wide),
            jax.ShapeDtypeStruct((entries, 128), wide),
        ],
        in_specs=[vmem_spec] * 4,
        out_specs=[vmem_spec] * 2,
        compiler_params=small,
        cost_estimate=long,
        name="chip_field",
    )(mine, theirs, noise, noise_there)


def block_operators(x, walkers, sources, picked):
    tiles = []
    for field_ref, crossed, near, other in sources:
        first = 2 * walkers * crossed
        one, two = near(picked).astype(wide), other(picked).astype(wide)
        copies = one.shape[1] // 128
        tiles.append([])
        for w in range(walkers):
            scale_one = field_ref[pl.ds(first + x * walkers + w, 1), :]
            scale_two = field_ref[pl.ds(first + (1 - x) * walkers + w, 1), :]
            scale_one = jnp.concatenate([scale_one] * copies, 1)
            scale_two = jnp.concatenate([scale_two] * copies, 1)
            block = time_root * (scale_one * one + scale_two * two)
            tiles[-1].append(block.astype(narrow))
    return tiles


def over_tiles(rows, order, body):
    high, across = 16, 256
    columns = order // across

    def tile(index, carry):
        row = pl.multiple_of((index // columns) * high, high)
        column = pl.multiple_of((index % columns) * across, across)
        body((pl.ds(row, high), pl.ds(column, across)))
        return carry

    lax.fori_loop(0, (rows // high) * columns, tile, 0)


def of_pair(ref, index):
    return lambda picked: ref[(index, *picked)]


def below(ref, top):
    return lambda picked: ref[pl.ds(top + picked[0].start, picked[0].size), picked[1]]


def both_cores(field_ref, rows, mine, mine_x, theirs, theirs_x):
    top = mine.shape[0] - 2 * rows
    return [
        (field_ref, 0, below(mine, top + rows), below(mine_x, rows)),
        (field_ref, 1, below(theirs, top), below(theirs_x, 0)),
    ]


def early_kernel(walkers, field_here, field_one, field_two, own, own_theirs, *refs):
    blocks, summed_ref = refs[:-1], refs[-1]
    _, _, x = place()
    sources = [
        (field_here, 0, of_pair(own, x), of_pair(own, 1 - x)),
        (field_here, 1, of_pair(own_theirs, x), of_pair(own_theirs, 1 - x)),
    ]
    rows = own.shape[1]
    sources += both_cores(field_one, rows, *blocks[:4])
    sources += both_cores(field_two, rows, *blocks[4:])

    def body(picked):
        tiles = block_operators(x, walkers, sources, picked)
        for w in range(walkers):
            parts = [block[w].astype(wide) for block in tiles]
            summed_ref[(w, *picked)] = sum(parts[1:], parts[0])

    over_tiles(*summed_ref.shape[1:], body)


def early_operator(walkers, fields, own, own_theirs, blocks):
    _, rows, order = own.shape
    return pl.pallas_call(
        functools.partial(early_kernel, walkers),
        out_shape=jax.ShapeDtypeStruct((walkers, rows, order), wide),
        in_specs=[vmem_spec] * (5 + len(blocks)),
        out_specs=vmem_spec,
        compiler_params=large,
        cost_estimate=long,
        name="early_operator",
    )(*fields, own, own_theirs, *blocks)


def late_kernel(summed_ref, field_ref, *refs):
    blocks, operator_ref = refs[:-1], refs[-1]
    walkers, rows, order = summed_ref.shape
    _, _, x = place()
    sources = both_cores(field_ref, rows, *blocks)

    def body(picked):
        tiles = block_operators(x, walkers, sources, picked)
        row, column = picked
        for w in range(walkers):
            value = summed_ref[(w, *picked)]
            for block in tiles:
                value = value + block[w].astype(wide)
            top = value.astype(narrow)
            operator_ref[w, row, column] = top
            rest = (value - top.astype(wide)).astype(narrow)
            operator_ref[w, pl.ds(rows + row.start, row.size), column] = rest

    over_tiles(rows, order, body)


def split_operator(summed, field, blocks):
    walkers, rows, order = summed.shape
    return pl.pallas_call(
        late_kernel,
        out_shape=jax.ShapeDtypeStruct((walkers, 2 * rows, order), narrow),
        in_specs=[vmem_spec] * (2 + len(blocks)),
        out_specs=vmem_spec,
        compiler_params=large,
        name="split_operator",
    )(summed, field, *blocks)


def applied(operator_ref, vector_ref, step, mine, theirs):
    z, k, _ = place()
    for core, refs in ((k, mine), (1 - k, theirs)):
        first = 0
        for ref in refs:
            count, rows, _ = ref.shape
            here = pl.ds(pl.multiple_of(core * rows, rows), rows)
            vector_ref[first : first + count, here, :] = ref[...]
            first += count
    start = pl.multiple_of(flipped(z, step) * 2 * rows, 2 * rows)

    def of_walker(w):
        both = jnp.dot(
            operator_ref[w, :, pl.ds(start, 2 * rows)],
            vector_ref[w],
            preferred_element_type=wide,
        )
        return both[:rows] + both[rows:]

    return of_walker


def flat(groups):
    return [each for group in groups for each in group]


def grouped(counts, refs):
    groups, refs = [], list(refs)
    for count in counts:
        groups.append(refs[:count])
        refs = refs[count:]
    return groups, refs


def near_parts(counts, operator_ref, refs):
    groups, (out_ref, vector_ref) = grouped(counts, refs)
    parts = [
        applied(operator_ref, vector_ref.at[step], step, groups[step], groups[3 + step])
        for step in range(3)
    ]
    return (lambda w: parts[0](w) + parts[1](w) + parts[2](w)), out_ref


def near_kernel(counts, operator_ref, *refs):
    part, out_ref = near_parts(counts, operator_ref, refs)
    for w in range(out_ref.shape[0]):
        out_ref[w] = part(w)


def base_kernel(counts, operator_ref, first_ref, orbitals_ref, *refs):
    part, out_ref = near_parts(counts, operator_ref, refs)
    for w in range(first_ref.shape[0]):
        out_ref[w] = orbitals_ref[0, :, w, :] + first_ref[w] + 0.5 * part(w)


def near_application(operator, groups, first_term=None, orbitals=None):
    walkers, rows = operator.shape[0], operator.shape[1] // 2
    occupied = groups[0][0].shape[2]
    counts = [len(group) for group in groups]
    kernel, name, more = near_kernel, "near_application", ()
    if first_term is not None:
        kernel, name, more = base_kernel, "base_application", (first_term, orbitals)
    pieces = flat(groups)
    return pl.pallas_call(
        functools.partial(kernel, counts),
        out_shape=jax.ShapeDtypeStruct((walkers, rows, occupied), wide),
        in_specs=[vmem_spec] * (1 + len(more) + len(pieces)),
        out_specs=vmem_spec,
        scratch_shapes=[pltpu.VMEM((3, walkers, 2 * rows, occupied), narrow)],
        compiler_params=small,
        name=name,
    )(operator, *more, *pieces)


def first_kernel(counts, operator_ref, partial_ref, *refs):
    (mine, theirs), (first_ref, narrow_ref, vector_ref) = grouped(counts, refs)
    part = applied(operator_ref, vector_ref, 3, mine, theirs)
    for w in range(first_ref.shape[0]):
        term = partial_ref[w] + part(w)
        first_ref[w] = term
        narrow_ref[w] = term.astype(narrow)


def first_application(operator, partial, mine, theirs):
    walkers, rows, occupied = partial.shape
    counts, pieces = [len(mine), len(theirs)], [*mine, *theirs]
    return pl.pallas_call(
        functools.partial(first_kernel, counts),
        out_shape=[
            jax.ShapeDtypeStruct((walkers, rows, occupied), wide),
            jax.ShapeDtypeStruct((walkers, rows, occupied), narrow),
        ],
        in_specs=[vmem_spec] * (2 + len(pieces)),
        out_specs=[vmem_spec] * 2,
        scratch_shapes=[pltpu.VMEM((walkers, 2 * rows, occupied), narrow)],
        compiler_params=small,
        name="first_application",
    )(operator, partial, *pieces)


def second_kernel(counts, operator_ref, base_ref, *refs):
    (mine, theirs), (out_ref, vector_ref) = grouped(counts, refs)
    part = applied(operator_ref, vector_ref, 3, mine, theirs)
    for w in range(base_ref.shape[0]):
        out_ref[0, :, w, :] = base_ref[w] + 0.5 * part(w)


def second_application(operator, base, mine, theirs):
    walkers, rows, occupied = base.shape
    counts, pieces = [len(mine), len(theirs)], [*mine, *theirs]
    return pl.pallas_call(
        functools.partial(second_kernel, counts),
        out_shape=jax.ShapeDtypeStruct((1, rows, walkers, occupied), wide),
        in_specs=[vmem_spec] * (2 + len(pieces)),
        out_specs=vmem_spec,
        scratch_shapes=[pltpu.VMEM((walkers, 2 * rows, occupied), narrow)],
        compiler_params=small,
        name="second_application",
    )(operator, base, *pieces)


def to_chip(value, step):
    return lax.ppermute(value, "chol", [(i, i ^ (2 * step)) for i in range(8)])


def to_core(value):
    return lax.ppermute(value, "chol", [(i, i ^ 1) for i in range(8)])


def across(value):
    return lax.ppermute(value, "walk", [(0, 1), (1, 0)])


def row_device(green_blocks, half_chol, full_chol, meanfield, noise_draws, orbitals):
    walkers, rows, _ = green_blocks.shape
    vectors = half_chol.shape[0]

    constants = jnp.concatenate([noise_draws.T.reshape(-1), jnp.repeat(meanfield, walkers)])
    constants = jnp.broadcast_to(constants[:, None], (2 * vectors * walkers, 128))
    constants_theirs = to_core(constants)

    near_messages = near_packed(full_chol, green_blocks)
    one, two = to_chip(near_messages[0], 1), to_chip(near_messages[1], 2)
    far_messages = far_packed(after(full_chol, *near_messages), rows)
    own = far_messages[1]
    green_three = to_chip(after(two, one, *far_messages)[:rows], 1)
    one_theirs = to_core(after(one, two, *far_messages))
    start = walker_major(orbitals)
    two_theirs = to_core(after(two, one, *far_messages, start))
    half_theirs = to_core(half_chol)

    bias = chip_bias(
        (green_blocks, one, two, after(green_three, one_theirs, two_theirs, start)),
        half_chol,
        half_theirs,
    )

    one_x = across(after(one, two, *far_messages)[rows:])
    one_x_theirs = to_core(one_x)
    two_x = across(after(two, one, *far_messages)[rows:])
    two_x_theirs = to_core(two_x)
    own_theirs = to_core(far_messages[2])
    three = after(far_messages[0], half_theirs, own_theirs, constants_theirs, one, two)
    three = to_chip(three, 3)
    three_theirs = to_core(three)
    bias_theirs = to_core(bias)

    bias = after(bias, one_x_theirs, two_x_theirs, three_theirs)
    bias_shift, field = chip_field(bias, bias_theirs, constants, constants_theirs, vectors)
    field_one, field_two = to_chip(field, 1), to_chip(field, 2)
    summed = early_operator(
        walkers,
        (field, field_one, field_two),
        own,
        own_theirs,
        (one, one_x, one_theirs, one_x_theirs, two, two_x, two_theirs, two_x_theirs),
    )
    field_three = to_chip(field, 3)
    three_x = across(three)
    three_x_theirs = to_core(after(three_x, field_one, field_two))
    operator = split_operator(
        summed, field_three, (three, three_x, three_theirs, three_x_theirs)
    )

    start_one, start_two = to_chip(after(start, one_x), 1), to_chip(after(start, one_x), 2)
    theirs = [to_core(start), to_core(after(start_one, bias_shift, field)), to_core(start_two)]
    groups = [[each] for each in (start, start_one, start_two, *theirs)]
    partial = near_application(operator, groups)
    start_three = to_chip(start_two, 1)
    start_three_theirs = to_core(after(start_three, summed, partial))
    first_term, first = first_application(
        operator, partial, [start_three], [start_three_theirs]
    )

    half = walkers // 2
    first_one = to_chip(first, 1)
    first_two = [to_chip(first[:half], 2), to_chip(first[half:], 2)]
    theirs = [[to_core(first)], [to_core(after(first_one, first_two[0]))]]
    theirs.append([to_core(each) for each in first_two])
    groups = [[first], [first_one], first_two, *theirs]
    base = near_application(operator, groups, first_term, orbitals)
    first_three = [to_chip(each, 1) for each in first_two]
    theirs = [to_core(first_three[0]), to_core(after(first_three[1], base))]
    walkers_next = second_application(operator, base, first_three, theirs)
    return (walkers_next, bias_shift.T)


def solution(mesh):
    placed = (
        P(("grp", "walk"), "chol", "orb"),
        P(("grp", "chol"), None, "orb"),
        P(("grp", "chol"), "orb", None),
        P(("grp", "chol")),
        P(("grp", "walk"), "chol"),
        P("orb", "chol", ("grp", "walk"), None),
    )
    sizes = mesh.shape
    if sizes["orb"] == 1 and sizes["walk"] == 2 and sizes["chol"] == 8:
        per_device = row_device
    else:
        per_device = general_device
    return jax.shard_map(
        per_device,
        mesh=mesh,
        in_specs=placed,
        out_specs=(P("orb", "chol", ("grp", "walk"), None), P(("grp", "walk"), "chol")),
        check_vma=False,
    )
```

```python
import functools

import jax
import jax.numpy as jnp
from jax import lax
from jax.experimental import pallas as pl
from jax.experimental.pallas import tpu as pltpu
from jax.sharding import PartitionSpec as P

time_root = 0.1


def general_device(green_blocks, half_chol, full_chol, meanfield, noise_draws, orbitals):
    walkers_here = green_blocks.shape[0]
    chol_here = half_chol.shape[0]
    half_rows = full_chol.shape[1]
    orbital_count = full_chol.shape[2]
    occupied = orbitals.shape[3]
    rows_here = orbitals.shape[1]
    partial_bias = jnp.einsum(
        "wki,cki->wc",
        lax.all_gather(green_blocks, "chol", axis=1, tiled=True),
        half_chol,
        preferred_element_type=jnp.float32,
    )
    force_bias = lax.psum(partial_bias, "orb")
    bias_shift = jnp.clip(time_root * (force_bias - meanfield[None, :]), -1.0, 1.0)
    shifted_field = noise_draws - bias_shift
    combined = jnp.zeros((walkers_here, half_rows, orbital_count), jnp.float32)
    for chol_index in range(chol_here):
        combined = combined + shifted_field[:, chol_index, None, None] * full_chol[chol_index][
            None
        ].astype(jnp.float32)
    operator_rows = (time_root * combined).astype(jnp.bfloat16)

    def apply_operator(vector):
        both_halves = lax.all_gather(vector, "orb", axis=0, tiled=True)
        running = jnp.zeros((walkers_here, half_rows, occupied), jnp.float32)
        shard_piece = lax.all_gather(both_halves, "chol", axis=1, tiled=True)
        row_count = shard_piece.shape[1]
        for half_index in range(shard_piece.shape[0]):
            col_block = lax.dynamic_slice_in_dim(
                operator_rows, half_index * half_rows, row_count, 2
            )
            running = running + lax.dot_general(
                col_block,
                shard_piece[half_index],
                (((2,), (0,)), ((0,), (1,))),
                preferred_element_type=jnp.float32,
            )
        summed = lax.psum(running, "chol")
        chol_slot = lax.axis_index("chol")
        owned_rows = lax.dynamic_slice_in_dim(summed, chol_slot * rows_here, rows_here, 1)
        return jnp.transpose(owned_rows, (1, 0, 2))[None]

    first_term = apply_operator(orbitals.astype(jnp.bfloat16))
    second_term = apply_operator(first_term.astype(jnp.bfloat16))
    walkers_next = orbitals + first_term + 0.5 * second_term
    return (walkers_next, bias_shift)


vmem_spec = pl.BlockSpec(memory_space=pltpu.VMEM)
hbm_spec = pl.BlockSpec(memory_space=pltpu.HBM)
wide = jnp.float32
narrow = jnp.bfloat16
small = pltpu.CompilerParams(vmem_limit_bytes=8 << 20)
large = pltpu.CompilerParams(vmem_limit_bytes=16 << 20)
long = pl.CostEstimate(flops=10**11, bytes_accessed=0, transcendentals=0)


def after(value, *others):
    return lax.optimization_barrier((value, *others))[0]


def place():
    slot = lax.axis_index("chol")
    return slot // 2, slot % 2, lax.axis_index("walk")


def flipped(z, step):
    return lax.bitwise_xor(z, jnp.int32(step))


def chip_rows(step, core, rows):
    z, _, _ = place()
    return pl.ds(pl.multiple_of((2 * flipped(z, step) + core) * rows, rows), rows)


def started(copies, source, target, sem):
    copies.append(pltpu.make_async_copy(source, target, sem.at[len(copies)]))
    copies[-1].start()


def near_pack_kernel(full_ref, green_ref, one_ref, two_ref, sem):
    _, k, x = place()
    walkers, rows, occupied = green_ref.shape
    copies = []
    for step, message in ((2, two_ref), (1, one_ref)):
        for index, core in enumerate((1 - k, k)):
            target = message.at[pl.ds((1 + index) * rows, rows), :]
            started(copies, full_ref.at[x, chip_rows(step, core, rows), :], target, sem)
    for each in copies:
        each.wait()
    for message in (two_ref, one_ref):
        for w in range(walkers):
            message[:rows, w * occupied : (w + 1) * occupied] = green_ref[w]


def near_packed(full_chol, green_blocks):
    order = full_chol.shape[2]
    rows = green_blocks.shape[1]
    return pl.pallas_call(
        near_pack_kernel,
        out_shape=[jax.ShapeDtypeStruct((3 * rows, order), narrow)] * 2,
        in_specs=[hbm_spec, vmem_spec],
        out_specs=[vmem_spec] * 2,
        scratch_shapes=[pltpu.SemaphoreType.DMA((4,))],
        name="near_packed",
    )(full_chol, green_blocks)


def far_pack_kernel(full_ref, crossed_ref, straight_ref, own_ref, cross_ref, sem):
    _, k, x = place()
    rows = own_ref.shape[1]
    copies = []
    for target, core in ((crossed_ref, 1 - k), (straight_ref, k)):
        started(copies, full_ref.at[x, chip_rows(3, core, rows), :], target, sem)
    started(copies, full_ref.at[:, chip_rows(0, k, rows), :], own_ref, sem)
    started(copies, full_ref.at[:, chip_rows(0, 1 - k, rows), :], cross_ref, sem)
    for each in copies:
        each.wait()


def far_packed(full_chol, rows):
    order = full_chol.shape[2]
    shapes = [(rows, order)] * 2 + [(2, rows, order)] * 2
    return pl.pallas_call(
        far_pack_kernel,
        out_shape=[jax.ShapeDtypeStruct(shape, narrow) for shape in shapes],
        in_specs=[hbm_spec],
        out_specs=[vmem_spec] * 4,
        scratch_shapes=[pltpu.SemaphoreType.DMA((4,))],
        cost_estimate=long,
        name="far_packed",
    )(full_chol)


def start_kernel(orbitals_ref, out_ref):
    for walker in range(out_ref.shape[0]):
        out_ref[walker] = orbitals_ref[0, :, walker, :].astype(narrow)


def walker_major(orbitals):
    _, rows, walkers, occupied = orbitals.shape
    return pl.pallas_call(
        start_kernel,
        out_shape=jax.ShapeDtypeStruct((walkers, rows, occupied), narrow),
        in_specs=[vmem_spec],
        out_specs=vmem_spec,
        compiler_params=small,
        name="walker_major",
    )(orbitals)


def bias_kernel(here_ref, one_ref, two_ref, three_ref, mine_ref, theirs_ref, out_ref):
    z, k, _ = place()
    walkers, rows, occupied = here_ref.shape
    vectors = mine_ref.shape[0]
    step_rows = 16
    totals = [jnp.zeros((8, 128), wide) for _ in range(2 * vectors * walkers)]
    for step, green in enumerate((here_ref, one_ref, two_ref, three_ref)):
        base = (2 * flipped(z, step) + k) * rows

        def add(index, totals, step=step, base=base, green=green):
            here = pl.multiple_of(index * step_rows, step_rows)
            there = pl.multiple_of(base + index * step_rows, step_rows)
            picked = pl.ds(here, step_rows)
            if step == 0:
                greens = [green[w, picked, :] for w in range(walkers)]
            else:
                greens = [green[picked, w * occupied : (w + 1) * occupied] for w in range(walkers)]
            greens = [g.astype(wide) for g in greens]
            totals = list(totals)
            for c in range(2 * vectors):
                chol_ref = mine_ref if c < vectors else theirs_ref
                chol = chol_ref[c % vectors, pl.ds(there, step_rows), :].astype(wide)
                for w in range(walkers):
                    product = greens[w] * chol
                    tiles = [
                        product[r : r + 8, n : n + 128]
                        for r in range(0, step_rows, 8)
                        for n in range(0, occupied, 128)
                    ]
                    totals[c * walkers + w] = totals[c * walkers + w] + sum(tiles[1:], tiles[0])
            return tuple(totals)

        totals = lax.fori_loop(0, rows // step_rows, add, tuple(totals))
    for index, total in enumerate(totals):
        value = jnp.sum(jnp.sum(total, axis=0, keepdims=True), axis=1, keepdims=True)
        out_ref[pl.ds(index, 1), :] = jnp.broadcast_to(value, (1, 128))


def chip_bias(green, mine, theirs):
    entries = 2 * mine.shape[0] * green[0].shape[0]
    return pl.pallas_call(
        bias_kernel,
        out_shape=jax.ShapeDtypeStruct((entries, 128), wide),
        in_specs=[vmem_spec] * 6,
        out_specs=vmem_spec,
        compiler_params=small,
        cost_estimate=long,
        name="chip_bias",
    )(*green, mine, theirs)


def field_kernel(mine_ref, theirs_ref, noise_ref, noise_there_ref, shift_ref, field_ref):
    half = mine_ref.shape[0] // 2
    low, high = pl.ds(0, half), pl.ds(half, half)
    for rows, other, consts in ((low, high, noise_ref), (high, low, noise_there_ref)):
        force = mine_ref[rows, :] + theirs_ref[other, :]
        shift = jnp.clip(time_root * (force - consts[high, :]), -1.0, 1.0)
        field_ref[rows, :] = consts[low, :] - shift
        if rows is low:
            vectors, walkers = shift_ref.shape
            row = lax.broadcasted_iota(jnp.int32, (walkers, 128), 0)
            lane = lax.broadcasted_iota(jnp.int32, (walkers, 128), 1)
            for vector in range(vectors):
                part = shift[vector * walkers : (vector + 1) * walkers, :]
                picked = jnp.sum(jnp.where(row == lane, part, 0.0), axis=0, keepdims=True)
                shift_ref[vector : vector + 1, :] = picked[:, :walkers]


def chip_field(mine, theirs, noise, noise_there, vectors):
    entries = mine.shape[0]
    return pl.pallas_call(
        field_kernel,
        out_shape=[
            jax.ShapeDtypeStruct((vectors, entries // 2 // vectors), wide),
            jax.ShapeDtypeStruct((entries, 128), wide),
        ],
        in_specs=[vmem_spec] * 4,
        out_specs=[vmem_spec] * 2,
        compiler_params=small,
        cost_estimate=long,
        name="chip_field",
    )(mine, theirs, noise, noise_there)


def block_operators(x, walkers, sources, picked):
    tiles = []
    for field_ref, crossed, near, other in sources:
        first = 2 * walkers * crossed
        one, two = near(picked).astype(wide), other(picked).astype(wide)
        copies = one.shape[1] // 128
        tiles.append([])
        for w in range(walkers):
            scale_one = field_ref[pl.ds(first + x * walkers + w, 1), :]
            scale_two = field_ref[pl.ds(first + (1 - x) * walkers + w, 1), :]
            scale_one = jnp.concatenate([scale_one] * copies, 1)
            scale_two = jnp.concatenate([scale_two] * copies, 1)
            block = time_root * (scale_one * one + scale_two * two)
            tiles[-1].append(block.astype(narrow))
    return tiles


def over_tiles(rows, order, body):
    high, across = 16, 256
    columns = order // across

    def tile(index, carry):
        row = pl.multiple_of((index // columns) * high, high)
        column = pl.multiple_of((index % columns) * across, across)
        body((pl.ds(row, high), pl.ds(column, across)))
        return carry

    lax.fori_loop(0, (rows // high) * columns, tile, 0)


def of_pair(ref, index):
    return lambda picked: ref[(index, *picked)]


def below(ref, top):
    return lambda picked: ref[pl.ds(top + picked[0].start, picked[0].size), picked[1]]


def both_cores(field_ref, rows, mine, mine_x, theirs, theirs_x):
    top = mine.shape[0] - 2 * rows
    return [
        (field_ref, 0, below(mine, top + rows), below(mine_x, rows)),
        (field_ref, 1, below(theirs, top), below(theirs_x, 0)),
    ]


def of_one(ref):
    return lambda picked: ref[picked]


def early_kernel(walkers, field_here, field_one, field_two, field_three, own, own_theirs, *refs):
    theirs, theirs_x, near, near_x, near_theirs, near_theirs_x, summed_ref = refs
    _, _, x = place()
    rows = own.shape[1]
    sources = [
        (field_here, 0, of_pair(own, x), of_pair(own, 1 - x)),
        (field_here, 1, of_pair(own_theirs, x), of_pair(own_theirs, 1 - x)),
        (field_three, 1, of_one(theirs), of_one(theirs_x)),
    ]
    for index, field_ref in enumerate((field_one, field_two)):
        top = 2 * rows * index
        sources += [
            (field_ref, 0, below(near, top + rows), below(near_x, top + rows)),
            (field_ref, 1, below(near_theirs, top), below(near_theirs_x, top)),
        ]

    def body(picked):
        tiles = block_operators(x, walkers, sources, picked)
        for w in range(walkers):
            parts = [block[w].astype(wide) for block in tiles]
            summed_ref[(w, *picked)] = sum(parts[1:], parts[0])

    over_tiles(*summed_ref.shape[1:], body)


def early_operator(walkers, fields, own, own_theirs, blocks):
    _, rows, order = own.shape
    return pl.pallas_call(
        functools.partial(early_kernel, walkers),
        out_shape=jax.ShapeDtypeStruct((walkers, rows, order), wide),
        in_specs=[vmem_spec] * (6 + len(blocks)),
        out_specs=vmem_spec,
        compiler_params=large,
        name="early_operator",
    )(*fields, own, own_theirs, *blocks)


def late_kernel(summed_ref, field_ref, mine, mine_x, operator_ref):
    walkers, rows, order = summed_ref.shape
    _, _, x = place()
    sources = [(field_ref, 0, of_one(mine), of_one(mine_x))]

    def body(picked):
        tiles = block_operators(x, walkers, sources, picked)
        row, column = picked
        for w in range(walkers):
            value = summed_ref[(w, *picked)] + tiles[0][w].astype(wide)
            top = value.astype(narrow)
            operator_ref[w, row, column] = top
            rest = (value - top.astype(wide)).astype(narrow)
            operator_ref[w, pl.ds(rows + row.start, row.size), column] = rest

    over_tiles(rows, order, body)


def split_operator(summed, field, mine, mine_x):
    walkers, rows, order = summed.shape
    return pl.pallas_call(
        late_kernel,
        out_shape=jax.ShapeDtypeStruct((walkers, 2 * rows, order), narrow),
        in_specs=[vmem_spec] * 4,
        out_specs=vmem_spec,
        compiler_params=large,
        name="split_operator",
    )(summed, field, mine, mine_x)


def applied(operator_ref, vector_ref, step, mine, theirs):
    z, k, _ = place()
    for core, refs in ((k, mine), (1 - k, theirs)):
        first = 0
        for ref in refs:
            count, rows, _ = ref.shape
            here = pl.ds(pl.multiple_of(core * rows, rows), rows)
            vector_ref[first : first + count, here, :] = ref[...]
            first += count
    start = pl.multiple_of(flipped(z, step) * 2 * rows, 2 * rows)

    def of_walker(w):
        both = jnp.dot(
            operator_ref[w, :, pl.ds(start, 2 * rows)],
            vector_ref[w],
            preferred_element_type=wide,
        )
        return both[:rows] + both[rows:]

    return of_walker


def flat(groups):
    return [each for group in groups for each in group]


def grouped(counts, refs):
    groups, refs = [], list(refs)
    for count in counts:
        groups.append(refs[:count])
        refs = refs[count:]
    return groups, refs


def near_parts(counts, operator_ref, refs):
    groups, (out_ref, vector_ref) = grouped(counts, refs)
    parts = [
        applied(operator_ref, vector_ref.at[step], step, groups[step], groups[3 + step])
        for step in range(3)
    ]
    return (lambda w: parts[0](w) + parts[1](w) + parts[2](w)), out_ref


def near_kernel(counts, operator_ref, *refs):
    part, out_ref = near_parts(counts, operator_ref, refs)
    for w in range(out_ref.shape[0]):
        out_ref[w] = part(w)


def base_kernel(counts, operator_ref, first_ref, orbitals_ref, *refs):
    part, out_ref = near_parts(counts, operator_ref, refs)
    for w in range(first_ref.shape[0]):
        out_ref[w] = orbitals_ref[0, :, w, :] + first_ref[w] + 0.5 * part(w)


def near_application(operator, groups, first_term=None, orbitals=None):
    walkers, rows = operator.shape[0], operator.shape[1] // 2
    occupied = groups[0][0].shape[2]
    counts = [len(group) for group in groups]
    kernel, name, more = near_kernel, "near_application", ()
    if first_term is not None:
        kernel, name, more = base_kernel, "base_application", (first_term, orbitals)
    pieces = flat(groups)
    return pl.pallas_call(
        functools.partial(kernel, counts),
        out_shape=jax.ShapeDtypeStruct((walkers, rows, occupied), wide),
        in_specs=[vmem_spec] * (1 + len(more) + len(pieces)),
        out_specs=vmem_spec,
        scratch_shapes=[pltpu.VMEM((3, walkers, 2 * rows, occupied), narrow)],
        compiler_params=small,
        name=name,
    )(operator, *more, *pieces)


def first_kernel(counts, operator_ref, *refs):
    groups, (first_ref, narrow_ref, vector_ref) = grouped(counts, refs)
    parts = [
        applied(operator_ref, vector_ref.at[step], step, groups[step], groups[4 + step])
        for step in range(4)
    ]
    for w in range(first_ref.shape[0]):
        term = (parts[0](w) + parts[1](w)) + (parts[2](w) + parts[3](w))
        first_ref[w] = term
        narrow_ref[w] = term.astype(narrow)


def first_application(operator, groups):
    walkers, rows = operator.shape[0], operator.shape[1] // 2
    occupied = groups[0][0].shape[2]
    counts = [len(group) for group in groups]
    pieces = flat(groups)
    return pl.pallas_call(
        functools.partial(first_kernel, counts),
        out_shape=[
            jax.ShapeDtypeStruct((walkers, rows, occupied), wide),
            jax.ShapeDtypeStruct((walkers, rows, occupied), narrow),
        ],
        in_specs=[vmem_spec] * (1 + len(pieces)),
        out_specs=[vmem_spec] * 2,
        scratch_shapes=[pltpu.VMEM((4, walkers, 2 * rows, occupied), narrow)],
        compiler_params=small,
        name="first_application",
    )(operator, *pieces)


def second_kernel(counts, operator_ref, base_ref, *refs):
    (mine, theirs), (out_ref, vector_ref) = grouped(counts, refs)
    part = applied(operator_ref, vector_ref, 3, mine, theirs)
    for w in range(base_ref.shape[0]):
        out_ref[0, :, w, :] = base_ref[w] + 0.5 * part(w)


def second_application(operator, base, mine, theirs):
    walkers, rows, occupied = base.shape
    counts, pieces = [len(mine), len(theirs)], [*mine, *theirs]
    return pl.pallas_call(
        functools.partial(second_kernel, counts),
        out_shape=jax.ShapeDtypeStruct((1, rows, walkers, occupied), wide),
        in_specs=[vmem_spec] * (2 + len(pieces)),
        out_specs=vmem_spec,
        scratch_shapes=[pltpu.VMEM((walkers, 2 * rows, occupied), narrow)],
        compiler_params=small,
        name="second_application",
    )(operator, base, *pieces)


def to_chip(value, step):
    return lax.ppermute(value, "chol", [(i, i ^ (2 * step)) for i in range(8)])


def to_core(value):
    return lax.ppermute(value, "chol", [(i, i ^ 1) for i in range(8)])


def across(value):
    return lax.ppermute(value, "walk", [(0, 1), (1, 0)])


def row_device(green_blocks, half_chol, full_chol, meanfield, noise_draws, orbitals):
    walkers, rows, _ = green_blocks.shape
    vectors = half_chol.shape[0]

    half = walkers // 2

    constants = jnp.concatenate([noise_draws.T.reshape(-1), jnp.repeat(meanfield, walkers)])
    constants = jnp.broadcast_to(constants[:, None], (2 * vectors * walkers, 128))
    constants_theirs = to_core(constants)

    near_messages = near_packed(full_chol, green_blocks)
    one = to_chip(near_messages[0], 1)
    two = to_chip(near_messages[1], 2)
    far_messages = far_packed(after(full_chol, *near_messages), rows)
    half_theirs = to_core(half_chol)
    own_theirs = to_core(far_messages[3])
    green_three = to_chip(after(two, *far_messages, half_theirs, own_theirs, constants_theirs, one)[:rows], 1)
    greens = (green_blocks, one, two, green_three)
    bias = chip_bias(greens, half_chol, half_theirs)
    start = walker_major(orbitals)
    start_two = to_chip(after(start, one, two), 2)
    start_three = to_chip(after(start_two, bias), 1)
    crossed = to_chip(after(far_messages[0], two), 3)
    straight = to_chip(after(far_messages[1], crossed), 3)
    start_one = to_chip(after(start, one, two), 1)
    bias_theirs = to_core(bias)

    bias_ready = after(bias, start_three, straight, start_one)
    bias_shift, field = chip_field(bias_ready, bias_theirs, constants, constants_theirs, vectors)
    near_rows = jnp.concatenate([after(one, *far_messages)[rows:], two[rows:]])
    near_rows_theirs = to_core(after(near_rows, bias))
    crossed_theirs = to_core(after(crossed, bias))
    field_one = to_chip(after(field, near_rows_theirs, crossed_theirs), 1)
    field_two = to_chip(after(field, near_rows_theirs, crossed_theirs), 2)
    field_three = to_chip(after(field, near_rows_theirs, crossed_theirs), 3)
    crossed_x = across(after(crossed, bias, one))
    crossed_x_theirs = to_core(crossed_x)
    near_rows_x = across(near_rows)
    near_rows_x_theirs = to_core(after(near_rows_x, bias))
    fields = (field, field_one, field_two, field_three)
    blocks = (crossed_theirs, crossed_x_theirs, near_rows, near_rows_x)
    blocks += (near_rows_theirs, near_rows_x_theirs)
    summed = early_operator(walkers, fields, far_messages[2], own_theirs, blocks)
    straight_x = across(after(straight, bias))
    operator = split_operator(summed, field_three, straight, straight_x)
    start_theirs = to_core(start)
    start_one_theirs = to_core(after(start_one, bias))
    start_two_theirs = to_core(start_two)
    start_three_theirs = to_core(after(start_three, summed))

    groups = (start, start_one, start_two, start_three)
    groups += (start_theirs, start_one_theirs, start_two_theirs, start_three_theirs)
    first_term, first = first_application(operator, [[each] for each in groups])

    first_one = to_chip(first, 1)
    first_two_low = to_chip(first[:half], 2)
    first_two_high = to_chip(first[half:], 2)
    first_theirs = to_core(first)
    first_one_theirs = to_core(after(first_one, first_two_low))
    two_low_theirs = to_core(first_two_low)
    two_high_theirs = to_core(first_two_high)
    groups = [[first], [first_one], [first_two_low, first_two_high]]
    groups += [[first_theirs], [first_one_theirs], [two_low_theirs, two_high_theirs]]
    base = near_application(operator, groups, first_term, orbitals)
    first_three_low = to_chip(first_two_low, 1)
    first_three_high = to_chip(first_two_high, 1)
    three_low_theirs = to_core(first_three_low)
    three_high_theirs = to_core(after(first_three_high, base))
    mine, theirs = [first_three_low, first_three_high], [three_low_theirs, three_high_theirs]
    walkers_next = second_application(operator, base, mine, theirs)
    return (walkers_next, bias_shift.T)


def solution(mesh):
    placed = (
        P(("grp", "walk"), "chol", "orb"),
        P(("grp", "chol"), None, "orb"),
        P(("grp", "chol"), "orb", None),
        P(("grp", "chol")),
        P(("grp", "walk"), "chol"),
        P("orb", "chol", ("grp", "walk"), None),
    )
    sizes = mesh.shape
    if sizes["orb"] == 1 and sizes["walk"] == 2 and sizes["chol"] == 8:
        per_device = row_device
    else:
        per_device = general_device
    return jax.shard_map(
        per_device,
        mesh=mesh,
        in_specs=placed,
        out_specs=(P("orb", "chol", ("grp", "walk"), None), P(("grp", "walk"), "chol")),
        check_vma=False,
    )
```

```python
import functools

import jax
import jax.numpy as jnp
from jax import lax
from jax.experimental import pallas as pl
from jax.experimental.pallas import tpu as pltpu
from jax.sharding import PartitionSpec as P

time_root = 0.1


def general_device(green_blocks, half_chol, full_chol, meanfield, noise_draws, orbitals):
    walkers_here = green_blocks.shape[0]
    chol_here = half_chol.shape[0]
    half_rows = full_chol.shape[1]
    orbital_count = full_chol.shape[2]
    occupied = orbitals.shape[3]
    rows_here = orbitals.shape[1]
    partial_bias = jnp.einsum(
        "wki,cki->wc",
        lax.all_gather(green_blocks, "chol", axis=1, tiled=True),
        half_chol,
        preferred_element_type=jnp.float32,
    )
    force_bias = lax.psum(partial_bias, "orb")
    bias_shift = jnp.clip(time_root * (force_bias - meanfield[None, :]), -1.0, 1.0)
    shifted_field = noise_draws - bias_shift
    combined = jnp.zeros((walkers_here, half_rows, orbital_count), jnp.float32)
    for chol_index in range(chol_here):
        combined = combined + shifted_field[:, chol_index, None, None] * full_chol[chol_index][
            None
        ].astype(jnp.float32)
    operator_rows = (time_root * combined).astype(jnp.bfloat16)

    def apply_operator(vector):
        both_halves = lax.all_gather(vector, "orb", axis=0, tiled=True)
        running = jnp.zeros((walkers_here, half_rows, occupied), jnp.float32)
        shard_piece = lax.all_gather(both_halves, "chol", axis=1, tiled=True)
        row_count = shard_piece.shape[1]
        for half_index in range(shard_piece.shape[0]):
            col_block = lax.dynamic_slice_in_dim(
                operator_rows, half_index * half_rows, row_count, 2
            )
            running = running + lax.dot_general(
                col_block,
                shard_piece[half_index],
                (((2,), (0,)), ((0,), (1,))),
                preferred_element_type=jnp.float32,
            )
        summed = lax.psum(running, "chol")
        chol_slot = lax.axis_index("chol")
        owned_rows = lax.dynamic_slice_in_dim(summed, chol_slot * rows_here, rows_here, 1)
        return jnp.transpose(owned_rows, (1, 0, 2))[None]

    first_term = apply_operator(orbitals.astype(jnp.bfloat16))
    second_term = apply_operator(first_term.astype(jnp.bfloat16))
    walkers_next = orbitals + first_term + 0.5 * second_term
    return (walkers_next, bias_shift)


vmem_spec = pl.BlockSpec(memory_space=pltpu.VMEM)
hbm_spec = pl.BlockSpec(memory_space=pltpu.HBM)
wide = jnp.float32
narrow = jnp.bfloat16
small = pltpu.CompilerParams(vmem_limit_bytes=8 << 20)
large = pltpu.CompilerParams(vmem_limit_bytes=16 << 20)
long = pl.CostEstimate(flops=10**11, bytes_accessed=0, transcendentals=0)


def after(value, *others):
    return lax.optimization_barrier((value, *others))[0]


def place():
    slot = lax.axis_index("chol")
    return slot // 2, slot % 2, lax.axis_index("walk")


def flipped(z, step):
    return lax.bitwise_xor(z, jnp.int32(step))


def chip_rows(step, core, rows):
    z, _, _ = place()
    return pl.ds(pl.multiple_of((2 * flipped(z, step) + core) * rows, rows), rows)


def started(copies, source, target, sem):
    copies.append(pltpu.make_async_copy(source, target, sem.at[len(copies)]))
    copies[-1].start()


def near_pack_kernel(full_ref, green_ref, one_ref, two_ref, sem):
    _, k, x = place()
    walkers, rows, occupied = green_ref.shape
    copies = []
    for step, message in ((2, two_ref), (1, one_ref)):
        for index, core in enumerate((1 - k, k)):
            target = message.at[pl.ds((1 + index) * rows, rows), :]
            started(copies, full_ref.at[x, chip_rows(step, core, rows), :], target, sem)
    for each in copies:
        each.wait()
    for message in (two_ref, one_ref):
        for w in range(walkers):
            message[:rows, w * occupied : (w + 1) * occupied] = green_ref[w]


def near_packed(full_chol, green_blocks):
    order = full_chol.shape[2]
    rows = green_blocks.shape[1]
    return pl.pallas_call(
        near_pack_kernel,
        out_shape=[jax.ShapeDtypeStruct((3 * rows, order), narrow)] * 2,
        in_specs=[hbm_spec, vmem_spec],
        out_specs=[vmem_spec] * 2,
        scratch_shapes=[pltpu.SemaphoreType.DMA((4,))],
        name="near_packed",
    )(full_chol, green_blocks)


def far_pack_kernel(full_ref, crossed_ref, straight_ref, own_ref, cross_ref, sem):
    _, k, x = place()
    rows = own_ref.shape[1]
    copies = []
    for target, core in ((crossed_ref, 1 - k), (straight_ref, k)):
        started(copies, full_ref.at[x, chip_rows(3, core, rows), :], target, sem)
    started(copies, full_ref.at[:, chip_rows(0, k, rows), :], own_ref, sem)
    started(copies, full_ref.at[:, chip_rows(0, 1 - k, rows), :], cross_ref, sem)
    for each in copies:
        each.wait()


def far_packed(full_chol, rows):
    order = full_chol.shape[2]
    shapes = [(rows, order)] * 2 + [(2, rows, order)] * 2
    return pl.pallas_call(
        far_pack_kernel,
        out_shape=[jax.ShapeDtypeStruct(shape, narrow) for shape in shapes],
        in_specs=[hbm_spec],
        out_specs=[vmem_spec] * 4,
        scratch_shapes=[pltpu.SemaphoreType.DMA((4,))],
        cost_estimate=long,
        name="far_packed",
    )(full_chol)


def start_kernel(orbitals_ref, out_ref):
    for walker in range(out_ref.shape[0]):
        out_ref[walker] = orbitals_ref[0, :, walker, :].astype(narrow)


def walker_major(orbitals):
    _, rows, walkers, occupied = orbitals.shape
    return pl.pallas_call(
        start_kernel,
        out_shape=jax.ShapeDtypeStruct((walkers, rows, occupied), narrow),
        in_specs=[vmem_spec],
        out_specs=vmem_spec,
        compiler_params=small,
        cost_estimate=long,
        name="walker_major",
    )(orbitals)


def bias_kernel(here_ref, one_ref, two_ref, three_ref, mine_ref, theirs_ref, out_ref):
    z, k, _ = place()
    walkers, rows, occupied = here_ref.shape
    vectors = mine_ref.shape[0]
    step_rows = 16
    totals = [jnp.zeros((8, 128), wide) for _ in range(2 * vectors * walkers)]
    for step, green in enumerate((here_ref, one_ref, two_ref, three_ref)):
        base = (2 * flipped(z, step) + k) * rows

        def add(index, totals, step=step, base=base, green=green):
            here = pl.multiple_of(index * step_rows, step_rows)
            there = pl.multiple_of(base + index * step_rows, step_rows)
            picked = pl.ds(here, step_rows)
            if step == 0:
                greens = [green[w, picked, :] for w in range(walkers)]
            else:
                greens = [green[picked, w * occupied : (w + 1) * occupied] for w in range(walkers)]
            greens = [g.astype(wide) for g in greens]
            totals = list(totals)
            for c in range(2 * vectors):
                chol_ref = mine_ref if c < vectors else theirs_ref
                chol = chol_ref[c % vectors, pl.ds(there, step_rows), :].astype(wide)
                for w in range(walkers):
                    product = greens[w] * chol
                    tiles = [
                        product[r : r + 8, n : n + 128]
                        for r in range(0, step_rows, 8)
                        for n in range(0, occupied, 128)
                    ]
                    totals[c * walkers + w] = totals[c * walkers + w] + sum(tiles[1:], tiles[0])
            return tuple(totals)

        totals = lax.fori_loop(0, rows // step_rows, add, tuple(totals))
    for index, total in enumerate(totals):
        value = jnp.sum(jnp.sum(total, axis=0, keepdims=True), axis=1, keepdims=True)
        out_ref[pl.ds(index, 1), :] = jnp.broadcast_to(value, (1, 128))


def chip_bias(green, mine, theirs):
    entries = 2 * mine.shape[0] * green[0].shape[0]
    return pl.pallas_call(
        bias_kernel,
        out_shape=jax.ShapeDtypeStruct((entries, 128), wide),
        in_specs=[vmem_spec] * 6,
        out_specs=vmem_spec,
        compiler_params=small,
        cost_estimate=long,
        name="chip_bias",
    )(*green, mine, theirs)


def field_kernel(mine_ref, theirs_ref, noise_ref, noise_there_ref, shift_ref, field_ref):
    half = mine_ref.shape[0] // 2
    low, high = pl.ds(0, half), pl.ds(half, half)
    for rows, other, consts in ((low, high, noise_ref), (high, low, noise_there_ref)):
        force = mine_ref[rows, :] + theirs_ref[other, :]
        shift = jnp.clip(time_root * (force - consts[high, :]), -1.0, 1.0)
        field_ref[rows, :] = consts[low, :] - shift
        if rows is low:
            vectors, walkers = shift_ref.shape
            row = lax.broadcasted_iota(jnp.int32, (walkers, 128), 0)
            lane = lax.broadcasted_iota(jnp.int32, (walkers, 128), 1)
            for vector in range(vectors):
                part = shift[vector * walkers : (vector + 1) * walkers, :]
                picked = jnp.sum(jnp.where(row == lane, part, 0.0), axis=0, keepdims=True)
                shift_ref[vector : vector + 1, :] = picked[:, :walkers]


def chip_field(mine, theirs, noise, noise_there, vectors):
    entries = mine.shape[0]
    return pl.pallas_call(
        field_kernel,
        out_shape=[
            jax.ShapeDtypeStruct((vectors, entries // 2 // vectors), wide),
            jax.ShapeDtypeStruct((entries, 128), wide),
        ],
        in_specs=[vmem_spec] * 4,
        out_specs=[vmem_spec] * 2,
        compiler_params=small,
        cost_estimate=long,
        name="chip_field",
    )(mine, theirs, noise, noise_there)


def block_operators(x, walkers, sources, picked):
    tiles = []
    for field_ref, crossed, near, other in sources:
        first = 2 * walkers * crossed
        one, two = near(picked).astype(wide), other(picked).astype(wide)
        copies = one.shape[1] // 128
        tiles.append([])
        for w in range(walkers):
            scale_one = field_ref[pl.ds(first + x * walkers + w, 1), :]
            scale_two = field_ref[pl.ds(first + (1 - x) * walkers + w, 1), :]
            scale_one = jnp.concatenate([scale_one] * copies, 1)
            scale_two = jnp.concatenate([scale_two] * copies, 1)
            block = time_root * (scale_one * one + scale_two * two)
            tiles[-1].append(block.astype(narrow))
    return tiles


def over_tiles(rows, order, body):
    high, across = 16, 256
    columns = order // across

    def tile(index, carry):
        row = pl.multiple_of((index // columns) * high, high)
        column = pl.multiple_of((index % columns) * across, across)
        body((pl.ds(row, high), pl.ds(column, across)))
        return carry

    lax.fori_loop(0, (rows // high) * columns, tile, 0)


def of_pair(ref, index):
    return lambda picked: ref[(index, *picked)]


def below(ref, top):
    return lambda picked: ref[pl.ds(top + picked[0].start, picked[0].size), picked[1]]


def both_cores(field_ref, rows, mine, mine_x, theirs, theirs_x):
    top = mine.shape[0] - 2 * rows
    return [
        (field_ref, 0, below(mine, top + rows), below(mine_x, rows)),
        (field_ref, 1, below(theirs, top), below(theirs_x, 0)),
    ]


def of_one(ref):
    return lambda picked: ref[picked]


def own_kernel(walkers, field_ref, own, own_theirs, summed_ref):
    _, _, x = place()
    sources = [
        (field_ref, 0, of_pair(own, x), of_pair(own, 1 - x)),
        (field_ref, 1, of_pair(own_theirs, x), of_pair(own_theirs, 1 - x)),
    ]

    def body(picked):
        tiles = block_operators(x, walkers, sources, picked)
        for w in range(walkers):
            summed_ref[(w, *picked)] = tiles[0][w].astype(wide) + tiles[1][w].astype(wide)

    over_tiles(*summed_ref.shape[1:], body)


def own_operator(walkers, field, own, own_theirs):
    _, rows, order = own.shape
    return pl.pallas_call(
        functools.partial(own_kernel, walkers),
        out_shape=jax.ShapeDtypeStruct((walkers, rows, order), wide),
        in_specs=[vmem_spec] * 3,
        out_specs=vmem_spec,
        compiler_params=large,
        name="own_operator",
    )(field, own, own_theirs)


def early_kernel(summed_ref, field_one, field_two, field_three, *refs):
    theirs, theirs_x, near, near_x, near_theirs, near_theirs_x, out_ref = refs
    walkers, rows, order = summed_ref.shape
    _, _, x = place()
    sources = [(field_three, 1, of_one(theirs), of_one(theirs_x))]
    for index, field_ref in enumerate((field_one, field_two)):
        top = 2 * rows * index
        sources += [
            (field_ref, 0, below(near, top + rows), below(near_x, top + rows)),
            (field_ref, 1, below(near_theirs, top), below(near_theirs_x, top)),
        ]

    def body(picked):
        tiles = block_operators(x, walkers, sources, picked)
        for w in range(walkers):
            parts = [block[w].astype(wide) for block in tiles]
            out_ref[(w, *picked)] = summed_ref[(w, *picked)] + sum(parts[1:], parts[0])

    over_tiles(rows, order, body)


def early_operator(summed, fields, blocks):
    return pl.pallas_call(
        early_kernel,
        out_shape=jax.ShapeDtypeStruct(summed.shape, wide),
        in_specs=[vmem_spec] * (4 + len(blocks)),
        out_specs=vmem_spec,
        compiler_params=large,
        name="early_operator",
    )(summed, *fields, *blocks)


def late_kernel(summed_ref, field_ref, mine, mine_x, operator_ref):
    walkers, rows, order = summed_ref.shape
    _, _, x = place()
    sources = [(field_ref, 0, of_one(mine), of_one(mine_x))]

    def body(picked):
        tiles = block_operators(x, walkers, sources, picked)
        row, column = picked
        for w in range(walkers):
            value = summed_ref[(w, *picked)] + tiles[0][w].astype(wide)
            top = value.astype(narrow)
            operator_ref[w, row, column] = top
            rest = (value - top.astype(wide)).astype(narrow)
            operator_ref[w, pl.ds(rows + row.start, row.size), column] = rest

    over_tiles(rows, order, body)


def split_operator(summed, field, mine, mine_x):
    walkers, rows, order = summed.shape
    return pl.pallas_call(
        late_kernel,
        out_shape=jax.ShapeDtypeStruct((walkers, 2 * rows, order), narrow),
        in_specs=[vmem_spec] * 4,
        out_specs=vmem_spec,
        compiler_params=large,
        name="split_operator",
    )(summed, field, mine, mine_x)


def applied(operator_ref, vector_ref, step, mine, theirs):
    z, k, _ = place()
    for core, refs in ((k, mine), (1 - k, theirs)):
        first = 0
        for ref in refs:
            count, rows, _ = ref.shape
            here = pl.ds(pl.multiple_of(core * rows, rows), rows)
            vector_ref[first : first + count, here, :] = ref[...]
            first += count
    start = pl.multiple_of(flipped(z, step) * 2 * rows, 2 * rows)

    def of_walker(w):
        both = jnp.dot(
            operator_ref[w, :, pl.ds(start, 2 * rows)],
            vector_ref[w],
            preferred_element_type=wide,
        )
        return both[:rows] + both[rows:]

    return of_walker


def flat(groups):
    return [each for group in groups for each in group]


def grouped(counts, refs):
    groups, refs = [], list(refs)
    for count in counts:
        groups.append(refs[:count])
        refs = refs[count:]
    return groups, refs


def near_parts(counts, operator_ref, refs):
    groups, (out_ref, vector_ref) = grouped(counts, refs)
    parts = [
        applied(operator_ref, vector_ref.at[step], step, groups[step], groups[3 + step])
        for step in range(3)
    ]
    return (lambda w: parts[0](w) + parts[1](w) + parts[2](w)), out_ref


def near_kernel(counts, operator_ref, *refs):
    part, out_ref = near_parts(counts, operator_ref, refs)
    for w in range(out_ref.shape[0]):
        out_ref[w] = part(w)


def base_kernel(counts, operator_ref, first_ref, orbitals_ref, *refs):
    part, out_ref = near_parts(counts, operator_ref, refs)
    for w in range(first_ref.shape[0]):
        out_ref[w] = orbitals_ref[0, :, w, :] + first_ref[w] + 0.5 * part(w)


def near_application(operator, groups, first_term=None, orbitals=None):
    walkers, rows = operator.shape[0], operator.shape[1] // 2
    occupied = groups[0][0].shape[2]
    counts = [len(group) for group in groups]
    kernel, name, more = near_kernel, "near_application", ()
    if first_term is not None:
        kernel, name, more = base_kernel, "base_application", (first_term, orbitals)
    pieces = flat(groups)
    return pl.pallas_call(
        functools.partial(kernel, counts),
        out_shape=jax.ShapeDtypeStruct((walkers, rows, occupied), wide),
        in_specs=[vmem_spec] * (1 + len(more) + len(pieces)),
        out_specs=vmem_spec,
        scratch_shapes=[pltpu.VMEM((3, walkers, 2 * rows, occupied), narrow)],
        compiler_params=small,
        name=name,
    )(operator, *more, *pieces)


def first_kernel(counts, operator_ref, *refs):
    groups, (first_ref, narrow_ref, vector_ref) = grouped(counts, refs)
    parts = [
        applied(operator_ref, vector_ref.at[step], step, groups[step], groups[4 + step])
        for step in range(4)
    ]
    for w in range(first_ref.shape[0]):
        term = (parts[0](w) + parts[1](w)) + (parts[2](w) + parts[3](w))
        first_ref[w] = term
        narrow_ref[w] = term.astype(narrow)


def first_application(operator, groups):
    walkers, rows = operator.shape[0], operator.shape[1] // 2
    occupied = groups[0][0].shape[2]
    counts = [len(group) for group in groups]
    pieces = flat(groups)
    return pl.pallas_call(
        functools.partial(first_kernel, counts),
        out_shape=[
            jax.ShapeDtypeStruct((walkers, rows, occupied), wide),
            jax.ShapeDtypeStruct((walkers, rows, occupied), narrow),
        ],
        in_specs=[vmem_spec] * (1 + len(pieces)),
        out_specs=[vmem_spec] * 2,
        scratch_shapes=[pltpu.VMEM((4, walkers, 2 * rows, occupied), narrow)],
        compiler_params=small,
        name="first_application",
    )(operator, *pieces)


def second_kernel(counts, operator_ref, base_ref, *refs):
    (mine, theirs), (out_ref, vector_ref) = grouped(counts, refs)
    part = applied(operator_ref, vector_ref, 3, mine, theirs)
    for w in range(base_ref.shape[0]):
        out_ref[0, :, w, :] = base_ref[w] + 0.5 * part(w)


def second_application(operator, base, mine, theirs):
    walkers, rows, occupied = base.shape
    counts, pieces = [len(mine), len(theirs)], [*mine, *theirs]
    return pl.pallas_call(
        functools.partial(second_kernel, counts),
        out_shape=jax.ShapeDtypeStruct((1, rows, walkers, occupied), wide),
        in_specs=[vmem_spec] * (2 + len(pieces)),
        out_specs=vmem_spec,
        scratch_shapes=[pltpu.VMEM((walkers, 2 * rows, occupied), narrow)],
        compiler_params=small,
        name="second_application",
    )(operator, base, *pieces)


def to_chip(value, step):
    return lax.ppermute(value, "chol", [(i, i ^ (2 * step)) for i in range(8)])


def to_core(value):
    return lax.ppermute(value, "chol", [(i, i ^ 1) for i in range(8)])


def across(value):
    return lax.ppermute(value, "walk", [(0, 1), (1, 0)])


def row_device(green_blocks, half_chol, full_chol, meanfield, noise_draws, orbitals):
    walkers, rows, _ = green_blocks.shape
    vectors = half_chol.shape[0]

    half = walkers // 2

    constants = jnp.concatenate([noise_draws.T.reshape(-1), jnp.repeat(meanfield, walkers)])
    constants = jnp.broadcast_to(constants[:, None], (2 * vectors * walkers, 128))
    constants_theirs = to_core(constants)

    near_messages = near_packed(full_chol, green_blocks)
    one = to_chip(near_messages[0], 1)
    two = to_chip(near_messages[1], 2)
    far_messages = far_packed(after(full_chol, *near_messages), rows)
    half_theirs = to_core(half_chol)
    own_theirs = to_core(far_messages[3])
    green_three = to_chip(after(two, *far_messages, half_theirs, own_theirs, constants_theirs, one)[:rows], 1)
    greens = (green_blocks, one, two, green_three)
    bias = chip_bias(greens, half_chol, half_theirs)
    start = walker_major(orbitals)
    start_one = to_chip(after(start, one, two), 1)
    bias_theirs = to_core(bias)

    bias_ready = after(bias, start_one)
    bias_shift, field = chip_field(bias_ready, bias_theirs, constants, constants_theirs, vectors)
    own_summed = own_operator(walkers, field, far_messages[2], own_theirs)
    near_rows = jnp.concatenate([after(one, *far_messages)[rows:], two[rows:]])
    near_rows_theirs = to_core(after(near_rows, bias))
    crossed = to_chip(far_messages[0], 3)
    crossed_theirs = to_core(after(crossed, bias))
    field_one = to_chip(after(field, near_rows_theirs, crossed_theirs), 1)
    field_two = to_chip(after(field, near_rows_theirs, crossed_theirs), 2)
    field_three = to_chip(after(field, near_rows_theirs, crossed_theirs), 3)
    crossed_x = across(after(crossed, bias, one))
    crossed_x_theirs = to_core(crossed_x)
    near_rows_x = across(near_rows)
    near_rows_x_theirs = to_core(after(near_rows_x, bias))
    fields = (field_one, field_two, field_three)
    blocks = (crossed_theirs, crossed_x_theirs, near_rows, near_rows_x)
    blocks += (near_rows_theirs, near_rows_x_theirs)
    summed = early_operator(own_summed, fields, blocks)
    straight = to_chip(after(far_messages[1], crossed), 3)
    straight_x = across(after(straight, bias))
    operator = split_operator(summed, field_three, straight, straight_x)
    start_two = to_chip(after(start, one, two), 2)
    start_three = to_chip(after(start_two, bias), 1)
    start_theirs = to_core(start)
    start_one_theirs = to_core(after(start_one, bias))
    start_two_theirs = to_core(after(start_two, near_rows_x))
    start_three_theirs = to_core(after(start_three, summed))

    groups = (start, start_one, start_two, start_three)
    groups += (start_theirs, start_one_theirs, start_two_theirs, start_three_theirs)
    first_term, first = first_application(operator, [[each] for each in groups])

    first_one = to_chip(first, 1)
    first_two_low = to_chip(first[:half], 2)
    first_two_high = to_chip(first[half:], 2)
    first_theirs = to_core(first)
    first_one_theirs = to_core(after(first_one, first_two_low))
    two_low_theirs = to_core(first_two_low)
    two_high_theirs = to_core(first_two_high)
    groups = [[first], [first_one], [first_two_low, first_two_high]]
    groups += [[first_theirs], [first_one_theirs], [two_low_theirs, two_high_theirs]]
    base = near_application(operator, groups, first_term, orbitals)
    first_three_low = to_chip(first_two_low, 1)
    first_three_high = to_chip(first_two_high, 1)
    three_low_theirs = to_core(first_three_low)
    three_high_theirs = to_core(after(first_three_high, base))
    mine, theirs = [first_three_low, first_three_high], [three_low_theirs, three_high_theirs]
    walkers_next = second_application(operator, base, mine, theirs)
    return (walkers_next, bias_shift.T)


def solution(mesh):
    placed = (
        P(("grp", "walk"), "chol", "orb"),
        P(("grp", "chol"), None, "orb"),
        P(("grp", "chol"), "orb", None),
        P(("grp", "chol")),
        P(("grp", "walk"), "chol"),
        P("orb", "chol", ("grp", "walk"), None),
    )
    sizes = mesh.shape
    if sizes["orb"] == 1 and sizes["walk"] == 2 and sizes["chol"] == 8:
        per_device = row_device
    else:
        per_device = general_device
    return jax.shard_map(
        per_device,
        mesh=mesh,
        in_specs=placed,
        out_specs=(P("orb", "chol", ("grp", "walk"), None), P(("grp", "walk"), "chol")),
        check_vma=False,
    )
```
